32 devices in a mesh: section: 2 (over y), dp: 16 (over z, x, core).
Axes of the slice: x: 2, y: 2, z: 4, core: 2. Of those that a mesh axis runs over, the one named last changes fastest.
Arguments:
- inputs: bfloat16 [2, 2048, 768], P(None, 'dp'), may hold values from -6 to 6
- cotangent: bfloat16 [2, 2048, 768], P(None, 'dp'), may hold values from -6 to 6
- markers: int32 [2, 2048], P(None, 'dp'), may hold values 0 or 1
- norm_gain: float32 [2, 768], P('section', 'dp'), may hold values from 0.5 to 1.5
- in_proj: float32 [2, 768, 3072], P('section', None, 'dp'), may hold values from -0.21875 to 0.21875
- conv_weight: float32 [2, 4, 1536], P('section', None, 'dp'), may hold values from -3 to 3
- conv_bias: float32 [2, 1536], P('section', 'dp'), may hold values from -3 to 3
- x_proj: float32 [2, 1536, 80], P('section', 'dp'), may hold values from -0.15625 to 0.15625
- dt_proj: float32 [2, 48, 1536], P('section', None, 'dp'), may hold values from -0.875 to 0.875
- dt_bias: float32 [2, 1536], P('section', 'dp'), may hold values from -6 to -2
- a_log: float32 [2, 1536, 16], P('section', 'dp'), may hold values from 0 to 2.77
- d_skip: float32 [2, 1536], P('section', 'dp'), may hold values from 0.5 to 1.5
- out_proj: float32 [2, 1536, 768], P('section', 'dp'), may hold values from -0.4375 to 0.4375
Outputs:
- section_out: bfloat16 [2, 2, 2048, 768], P('section', None, 'dp')
- section_grad: float32 [2, 2, 2048, 768], P('section', None, 'dp')
- grad_norm_gain: float32 [2, 768], P('section', 'dp')
- grad_in_proj: float32 [2, 768, 3072], P('section', None, 'dp')
- grad_conv_weight: float32 [2, 4, 1536], P('section', None, 'dp')
- grad_conv_bias: float32 [2, 1536], P('section', 'dp')
- grad_x_proj: float32 [2, 1536, 80], P('section', 'dp')
- grad_dt_proj: float32 [2, 48, 1536], P('section', None, 'dp')
- grad_dt_bias: float32 [2, 1536], P('section', 'dp')
- grad_a_log: float32 [2, 1536, 16], P('section', 'dp')
- grad_d_skip: float32 [2, 1536], P('section', 'dp')
- grad_out_proj: float32 [2, 1536, 768], P('section', 'dp')
The draws below stay inside these ranges and needn't reach their ends.
All inputs are finite; a program needn't handle non-finite values. No bound on the sum of `markers` on one device may be relied on, other than what follows from the above.
Results may differ from the reference program's by a relative error of at most 0.017.
The reference program's roundings to bfloat16 on the way count: a program that leaves them out, or rounds other values in their place, can miss the bound.
Values may be sent and summed in bfloat16 or wider, within the bound.
A program may use at most 384 MiB of HBM per device.

```python
import math
import jax
import jax.numpy as jnp
from jax import lax

D = 768
DI = 1536
NS = 16
KC = 4
RK = 48
LEN = 128
MICRO = 2
BLK = 128
TOKENS = 2048
N_SECTION = 2
N_DP = 16


def with_ends(entries, key, least, high):
    place = [jax.random.randint(jax.random.fold_in(key, axis), (), 0, length) for axis, length in enumerate(entries.shape)]
    widest = entries.shape.index(max(entries.shape))
    beside = place[:widest] + [(place[widest] + 1) % entries.shape[widest]] + place[widest + 1:]
    return entries.at[tuple(place)].set(least).at[tuple(beside)].set(high)


def shard_levels(key, shape, shards, least, largest):
    loudness = 1.0
    for axis_at, shards_of in shards:
        heights = jax.random.uniform(jax.random.fold_in(jax.random.fold_in(key, 6), axis_at), (shards_of,), jnp.float32, least / len(shards), largest / len(shards))
        loudness = loudness * jnp.repeat(jnp.exp(heights), shape[axis_at] // shards_of).reshape((-1,) + (1,) * (len(shape) - 1 - axis_at))
    return loudness


def centred(rng, dims, scale, most, cuts=(), held_as=jnp.bfloat16):
    gain = shard_levels(rng, dims, cuts, -0.22, 0.18) if cuts else 1.0
    values = jax.random.normal(rng, dims, jnp.float32) * scale * gain
    return jnp.minimum(jnp.maximum(values, -most), most).astype(held_as)


def setup_inputs(seed: int = 0) -> dict:
    splits = jax.random.split(jax.random.key(seed), 14)
    return {
        "inputs": centred(splits[0], (MICRO, TOKENS, D), 1.0, 6.0, ((1, 16),)),
        "cotangent": centred(splits[1], (MICRO, TOKENS, D), 1.0, 6.0, ((1, 16),)),
        "markers": with_ends((jax.random.randint(splits[2], (MICRO, TOKENS), 0, 64) < 1).astype(jnp.int32), jax.random.fold_in(splits[2], 1), 0, 1),
        "norm_gain": jnp.clip(1.0 + 0.1 * jax.random.normal(splits[3], (N_SECTION, D), jnp.float32), 0.5, 1.5),
        "in_proj": centred(splits[4], (N_SECTION, D, 2 * DI), D ** -0.5, 0.21875, ((0, 2), (2, 16)), jnp.float32),
        "conv_weight": centred(splits[5], (N_SECTION, KC, DI), KC ** -0.5, 3.0, ((0, 2), (2, 16)), jnp.float32),
        "conv_bias": centred(splits[6], (N_SECTION, DI), 0.5, 3.0, ((0, 2), (1, 16)), jnp.float32),
        "x_proj": centred(splits[7], (N_SECTION, DI, RK + 2 * NS), DI ** -0.5, 0.15625, ((0, 2), (1, 16)), jnp.float32),
        "dt_proj": centred(splits[8], (N_SECTION, RK, DI), RK ** -0.5, 0.875, ((0, 2), (2, 16)), jnp.float32),
        "dt_bias": jnp.clip(-6.0 + 4.0 * jax.random.uniform(splits[9], (N_SECTION, DI), jnp.float32) ** shard_levels(splits[9], (N_SECTION, DI), ((0, 2), (1, 16)), -0.2, 0.2), -6.0, -2.0),
        "a_log": jnp.clip(2.77 * jax.random.uniform(splits[10], (N_SECTION, DI, NS), jnp.float32) ** shard_levels(splits[10], (N_SECTION, DI, NS), ((0, 2), (1, 16)), -0.2, 0.2), 0.0, 2.77),
        "d_skip": jnp.clip(0.5 + 1.0 * jax.random.uniform(splits[11], (N_SECTION, DI), jnp.float32) ** shard_levels(splits[11], (N_SECTION, DI), ((0, 2), (1, 16)), -0.2, 0.2), 0.5, 1.5),
        "out_proj": centred(splits[12], (N_SECTION, DI, D), (DI // 8) ** -0.5, 0.4375, ((0, 2), (1, 16)), jnp.float32),
    }


EPSILON = 1e-05
HIGHEST = lax.Precision.HIGHEST

@jax.custom_vjp
def low(v):
    return lax.optimization_barrier(v.astype(jnp.bfloat16)).astype(jnp.float32)

@jax.custom_vjp
def low_back(v):
    return v

def low_keep(v):
    return (low(v), None)

def low_pass(kept, grad):
    return (grad,)

def back_keep(v):
    return (v, None)

def back_low(kept, grad):
    return (low(grad),)
low.defvjp(low_keep, low_pass)
low_back.defvjp(back_keep, back_low)

def combine(earlier, following):
    return (earlier[0] * following[0], following[0] * earlier[1] + following[1])

def delayed(values, delay_steps, fill_value):
    front_fill = jnp.full(values.shape[:1] + (delay_steps,) + values.shape[2:], fill_value, values.dtype)
    return jnp.concatenate([front_fill, values[:, :values.shape[1] - delay_steps]], axis=1)

def matmul(left_side, right_side):
    return jnp.einsum('rtk,kn->rtn', left_side, right_side, precision=HIGHEST)

def scan_block(a_negative, carry_state, pieces):
    rate_blk, act_blk, reset_blk, b_blk, c_blk = pieces
    decay_factor = jnp.exp(rate_blk[..., None] * a_negative) * (1.0 - reset_blk)[..., None, None]
    drive_term = (rate_blk * act_blk)[..., None] * b_blk[..., None, :]
    prefix_a, prefix_b = lax.associative_scan(combine, (decay_factor, drive_term), axis=1)
    states = prefix_a * carry_state[:, None] + prefix_b
    return (states[:, -1], lax.optimization_barrier(jnp.sum(states * c_blk[..., None, :], axis=-1)))

def to_blocks(values):
    shaped = values.reshape((values.shape[0], LEN // BLK, BLK) + values.shape[2:])
    return jnp.moveaxis(shaped, 1, 0)

def from_blocks(values):
    merged = jnp.moveaxis(values, 0, 1)
    return merged.reshape((merged.shape[0], LEN) + merged.shape[3:])

def mamba_layer(resid_in, resets_row, weights):
    norm_gain, in_proj, conv_weight, conv_bias, x_proj, dt_proj, dt_bias, a_log, d_skip, out_proj = weights
    inv_rms = lax.rsqrt(lax.optimization_barrier(jnp.mean(resid_in * resid_in, axis=-1, keepdims=True)) + EPSILON)
    normed = low(resid_in * inv_rms * norm_gain)
    mixed_out = low_back(matmul(normed, in_proj))
    x_part = mixed_out[..., :DI]
    z_part = mixed_out[..., DI:]
    conv_out = conv_bias + conv_weight[0] * x_part
    keep_mask = jnp.ones_like(resets_row)
    for offset in range(1, KC):
        keep_mask = keep_mask * (1.0 - delayed(resets_row, offset - 1, 1.0))
        conv_out = conv_out + conv_weight[offset] * delayed(x_part, offset, 0.0) * keep_mask[..., None]
    activated = low(jax.nn.silu(conv_out))
    projected = low_back(matmul(activated, x_proj))
    rate_in = low(projected[..., :RK])
    b_input = projected[..., RK:RK + NS]
    c_input = projected[..., RK + NS:]
    step_rate = jax.nn.softplus(low_back(matmul(rate_in, dt_proj) + dt_bias))
    a_negative = -jnp.exp(a_log)
    start_state = jnp.zeros((resid_in.shape[0], DI, NS), jnp.float32)
    pieces = tuple((to_blocks(values) for values in (step_rate, activated, resets_row, b_input, c_input)))

    def block_step(carry_state, block_pieces):
        return jax.checkpoint(scan_block)(a_negative, carry_state, block_pieces)
    final_state, scanned = lax.scan(block_step, start_state, pieces)
    ssm_out = from_blocks(scanned) + d_skip * activated
    gated_out = low(ssm_out * jax.nn.silu(z_part))
    return resid_in + low_back(matmul(gated_out, out_proj))

def two_layers(layer_weights, rows_in, resets_row, probe_zero):
    first_out = mamba_layer(rows_in, resets_row, layer_weights[0])
    second_out = mamba_layer(low(low_back(first_out)) + probe_zero, resets_row, layer_weights[1])
    return (first_out, second_out)

def reference(inputs, cotangent, markers, norm_gain, in_proj, conv_weight, conv_bias, x_proj, dt_proj, dt_bias, a_log, d_skip, out_proj):
    params = (norm_gain, in_proj, conv_weight, conv_bias, x_proj, dt_proj, dt_bias, a_log, d_skip, out_proj)
    row_count = MICRO * N_DP
    group_rows = math.gcd(row_count, max(1, 4096 // LEN))
    grid_shape = (row_count // group_rows, group_rows, LEN)
    first_pos = (jnp.arange(LEN) == 0)[None, :]
    starts = (markers.reshape(row_count, LEN) > 0) | first_pos
    resets = jnp.where(starts, 1.0, 0.0).astype(jnp.float32).reshape(grid_shape)
    rows_in = inputs.astype(jnp.float32).reshape(grid_shape + (D,))
    seed_grad = cotangent.astype(jnp.float32).reshape(grid_shape + (D,))
    probe_zero = jnp.zeros(grid_shape + (D,), jnp.float32)

    def forward(weights, rows_in, probe_zero):
        rounded = tuple((low(param) for param in weights))
        per_layer = tuple((tuple((param[layer_index] for param in rounded)) for layer_index in range(N_SECTION)))

        def group_step(carry_in, pieces):
            return (carry_in, jax.checkpoint(two_layers)(per_layer, pieces[0], pieces[1], pieces[2]))
        carry_in, outputs = lax.scan(group_step, jnp.zeros((), jnp.float32), (rows_in, resets, probe_zero))
        return outputs
    outputs, pullback = jax.vjp(forward, params, rows_in, probe_zero)
    weight_grads, grad_in, grad_probe = pullback((jnp.zeros_like(outputs[0]), seed_grad))
    section_out = jnp.stack([outputs[0], outputs[1]]).reshape(N_SECTION, MICRO, TOKENS, D).astype(jnp.bfloat16)
    section_grad = jnp.stack([grad_in, grad_probe]).reshape(N_SECTION, MICRO, TOKENS, D)
    return (section_out, section_grad, weight_grads[0], weight_grads[1], weight_grads[2], weight_grads[3], weight_grads[4], weight_grads[5], weight_grads[6], weight_grads[7], weight_grads[8], weight_grads[9])
```

```python
import functools
import types

import jax
import jax.numpy as jnp
from jax import lax
from jax.experimental import pallas as pl
from jax.experimental.pallas import tpu as pltpu
from jax.sharding import PartitionSpec as P

T = 128
D = 768
DI = 1536
NS = 16
KC = 4
RK = 48
MICRO = 2
C = 512
CS = 768
TB = 16
NB = T // TB
EPS = 1e-5
LOG2E = 1.4426950408889634
LN2 = 0.6931471805599453
BIG = 1e30
GAIN_LANE = 24
DP, SECTION = "dp", "section"
UP, DOWN, ACROSS, CORE = range(4)
BELOW, ABOVE = range(2)
START, FORWARD, FINISH = range(3)
RIGHT, LEFT = range(2)
f32 = jnp.float32
bf16 = jnp.bfloat16


def nn(a, b):
    return lax.dot_general(a, b, (((1,), (0,)), ((), ())), preferred_element_type=f32)


def nt(a, b):
    return lax.dot_general(a, b, (((1,), (1,)), ((), ())), preferred_element_type=f32)


def tn(a, b):
    return lax.dot_general(a, b, (((0,), (0,)), ((), ())), preferred_element_type=f32)


def iota(shape, axis):
    return lax.broadcasted_iota(jnp.int32, shape, axis)


def sigmoid(v):
    return 1.0 / (1.0 + jnp.exp(-v))


def softplus(v):
    return jnp.maximum(v, 0.0) + jnp.log1p(jnp.exp(-jnp.abs(v)))


def wide(v):
    return jnp.concatenate([v] * (CS // 128), axis=1)


def keeps(reset):
    keep = [None]
    cur = jnp.ones_like(reset)
    for k in range(1, KC):
        cur = cur * (1.0 - (reset if k == 1 else pltpu.roll(reset, k - 1, 0)))
        keep.append(cur)
    return keep


def block_diagonal(cols):
    tile = (iota((NS, NS * TB), 1) % NS == iota((NS, NS * TB), 0)).astype(bf16)
    rep = nn(cols.astype(bf16), tile)
    own = (iota((T, NS * TB), 1) // NS) == (iota((T, NS * TB), 0) % TB)
    return jnp.where(own, rep, 0.0).astype(bf16)


def lane_columns(dst, val):
    for t in range(T):
        dst[pl.ds(t * NS, NS), :] = jnp.broadcast_to(val[:, t : t + 1], (NS, 128))


def f_x(reset, normed, win, rows, x_ref, act):
    keep = keeps(reset)
    for c in range(DI // C):
        s = pl.ds(c * C, C)
        x = nt(normed[...], win[s, :])
        x_ref[:, s] = x
        v = rows[20:21, s] + rows[16:17, s] * x
        for k in range(1, KC):
            v = v + rows[16 + k : 17 + k, s] * (pltpu.roll(x, k, 0) * keep[k])
        act[:, s] = (v * sigmoid(v)).astype(bf16)


def f_rate(reset, act, small, rows, proj, rin, pre_ref, dec, drive, cols, diag):
    p = nn(act[...], small[:, 0:128])
    proj[...] = p
    lane_columns(cols, p.T[RK : RK + NS, :])
    diag[...] = block_diagonal(p[:, RK + NS : RK + 2 * NS])
    rin[...] = pltpu.roll(jnp.where(iota((T, 128), 1) < RK, p, 0.0), RK + 2 * NS, 1).astype(bf16)
    for c in range(DI // C):
        s = pl.ds(c * C, C)
        pre = nt(rin[...], small[s, 0:128]) + rows[21:22, s]
        pre_ref[:, s] = pre
        rate = softplus(pre)
        dec[:, s] = jnp.where(reset > 0.0, BIG, rate)
        drive[:, s] = rate * act[:, s].astype(f32)


def f_scan(act, rows, dec, drive, cols, diag, h_ref, ssm):
    h_ref[0:NS, :] = jnp.zeros((NS, DI), bf16)
    for c in range(DI // CS):
        s = pl.ds(c * CS, CS)

        def block(i, h):
            t0 = pl.multiple_of(i * TB, TB)
            a2 = rows[0:NS, s]
            d = dec[pl.ds(t0, TB), s]
            v = drive[pl.ds(t0, TB), s]
            for j in range(TB):
                b = wide(cols[pl.ds(t0 * NS + j * NS, NS), :])
                h = jnp.exp2(d[j : j + 1, :] * a2) * h + v[j : j + 1, :] * b
                h_ref[pl.ds(t0 * NS + (j + 1) * NS, NS), s] = h.astype(bf16)
            return h

        lax.fori_loop(0, NB, block, jnp.zeros((NS, CS), f32))

    def sums(i, carry):
        for q in range(4):
            t0 = pl.multiple_of(i * (4 * TB) + q * TB, TB)
            tt = pl.ds(t0, TB)
            y = nn(diag[tt, :], h_ref[pl.ds(t0 * NS + NS, TB * NS), :])
            ssm[tt, :] = y + rows[22:23, :] * act[tt, :].astype(f32)
        return carry

    lax.fori_loop(0, NB // 4, sums, 0)


def f_out(u, normed, win, wout, ssm, z_ref, gated, out):
    acc = u[...].astype(f32)
    for c in range(DI // C):
        s = pl.ds(c * C, C)
        z = nt(normed[...], win[pl.ds(DI + c * C, C), :])
        z_ref[:, s] = z
        g = (ssm[:, s] * (z * sigmoid(z))).astype(bf16)
        gated[:, s] = g
        acc = acc + nn(g, wout[s, :])
    out[...] = acc.astype(bf16)


def total(old, first, value):
    return jnp.where(first, value, old + value)


def b_gate(first, go_ref, wout, z_ref, ssm, act, gs_ref, gm, sm):
    go = go_ref[...]
    for c in range(DI // C):
        s = pl.ds(c * C, C)
        gg = nt(go, wout[s, :])
        z = z_ref[:, s]
        sg = sigmoid(z)
        gs = gg * z * sg
        gs_ref[:, s] = gs
        gm[:, pl.ds(DI + c * C, C)] = (gg * ssm[:, s] * sg * (1.0 + z * (1.0 - sg))).astype(bf16)
        part = jnp.sum(gs * act[:, s].astype(f32), axis=0, keepdims=True)
        sm[22:23, s] = total(sm[22:23, s], first, part)


def b_prep(reset, pre, act, proj, dec, drive, cols, diag):
    p = proj[...]
    lane_columns(cols, p.T[RK + NS : RK + 2 * NS, :])
    diag[...] = block_diagonal(p[:, RK : RK + NS])
    for c in range(DI // C):
        s = pl.ds(c * C, C)
        rate = softplus(pre[:, s])
        dec[:, s] = jnp.where(reset > 0.0, BIG, rate)
        drive[:, s] = (rate * act[:, s].astype(f32)).astype(bf16)


def b_scan(first, gs, rows, dec, cols, diag, drive, h_ref, adj_ref, gd, gr, gb, gc, sm):
    ones = (iota((TB, TB * NS), 1) // NS) == iota((TB, TB * NS), 0)
    od = ones.astype(bf16)

    def state_sums(i, carry):
        for q in range(4):
            t0 = pl.multiple_of(i * (4 * TB) + q * TB, TB)
            tt = pl.ds(t0, TB)
            full = nt(gs[tt, :].astype(bf16), h_ref[pl.ds(t0 * NS + NS, TB * NS), :])
            gc[tt, :] = jnp.where(ones, full, 0.0).astype(bf16)
        return carry

    lax.fori_loop(0, NB // 4, state_sums, 0)
    for c in range(DI // CS):
        s = pl.ds(c * CS, CS)

        def block(i, state):
            carry, acc = state
            t0 = pl.multiple_of((NB - 1 - i) * TB, TB)
            a2 = rows[0:NS, s]
            d = dec[pl.ds(t0, TB), s]
            g = gs[pl.ds(t0, TB), s]
            for j in reversed(range(TB)):
                row = pl.ds(t0 * NS + j * NS, NS)
                adj = g[j : j + 1, :] * wide(cols[row, :]) + carry
                adj_ref[row, :] = adj.astype(bf16)
                dj = d[j : j + 1, :]
                carry = jnp.exp2(dj * a2) * adj
                expo = carry * h_ref[row, s].astype(f32)
                h_ref[row, s] = (expo * a2).astype(bf16)
                acc = acc + expo * dj
            return carry, acc

        zero = jnp.zeros((NS, CS), f32)
        _, acc = lax.fori_loop(0, NB, block, (zero, zero))
        sm[0:NS, s] = total(sm[0:NS, s], first, acc * rows[0:NS, s] * LN2)

        def adjoint_sums(i, carry):
            for q in range(4):
                t0 = pl.multiple_of(i * (4 * TB) + q * TB, TB)
                tt = pl.ds(t0, TB)
                row = pl.ds(t0 * NS, TB * NS)
                gd[tt, s] = nn(diag[tt, :], adj_ref[row, :])
                gr[tt, s] = nn(od, h_ref[row, s]) * LN2
                full = nt(drive[tt, s], adj_ref[row, :])
                gb[tt, :] = full if c == 0 else gb[tt, :] + full
            return carry

        lax.fori_loop(0, NB // 4, adjoint_sums, 0)


def b_pre(first, act, pre, small, gd, gr, gb, gc, gpre, gp, sm):
    acc = jnp.zeros((T, 128), f32)
    for c in range(DI // C):
        s = pl.ds(c * C, C)
        g = ((gr[:, s] + gd[:, s] * act[:, s].astype(f32)) * sigmoid(pre[:, s])).astype(bf16)
        gpre[:, s] = g
        part = jnp.sum(g.astype(f32), axis=0, keepdims=True)
        sm[21:22, s] = total(sm[21:22, s], first, part)
        acc = acc + nn(g, small[s, 0:128])
    k = iota((TB * NS, 128), 0) % NS
    lane = iota((TB * NS, 128), 1)
    own = (iota((T, NS * TB), 1) // NS) == (iota((T, NS * TB), 0) % TB)
    gb_own = jnp.where(own, gb[...], 0.0).astype(bf16)
    bc = nn(gb_own, (lane == RK + k).astype(bf16)) + nn(gc[...], (lane == RK + NS + k).astype(bf16))
    gp[...] = jnp.where(iota((T, 128), 1) < RK, pltpu.roll(acc, RK, 1), bc).astype(bf16)


def b_conv(first, reset, rows, small, x_ref, gs, gd, pre, gp, gm, sm):
    keep = keeps(reset)
    for c in range(DI // C):
        s = pl.ds(c * C, C)
        x = x_ref[:, s]
        xs = [x] + [pltpu.roll(x, k, 0) * keep[k] for k in range(1, KC)]
        v = rows[20:21, s]
        for k in range(KC):
            v = v + rows[16 + k : 17 + k, s] * xs[k]
        ga = gs[:, s] * rows[22:23, s] + gd[:, s] * softplus(pre[:, s]) + nt(gp[...], small[s, 0:128])
        sg = sigmoid(v)
        gc = ga * sg * (1.0 + v * (1.0 - sg))
        part = jnp.sum(gc, axis=0, keepdims=True)
        sm[20:21, s] = total(sm[20:21, s], first, part)
        gx = gc * rows[16:17, s]
        for k in range(KC):
            part = jnp.sum(gc * xs[k], axis=0, keepdims=True)
            sm[16 + k : 17 + k, s] = total(sm[16 + k : 17 + k, s], first, part)
            if k:
                gx = gx + pltpu.roll(gc * keep[k], T - k, 0) * rows[16 + k : 17 + k, s]
        gm[:, s] = gx.astype(bf16)


def b_in(first, u_ref, go_ref, gain, win, gm, sg, gg):
    gn = jnp.zeros((T, D), f32)
    for c in range(2 * DI // C):
        s = pl.ds(c * C, C)
        gn = gn + nn(gm[:, s], win[s, :])
    u = u_ref[...].astype(f32)
    inv = lax.rsqrt(jnp.mean(u * u, axis=-1, keepdims=True) + EPS)
    g = gn * gain[...]
    gg[...] = total(gg[...], first, jnp.sum(gn * u * inv, axis=0, keepdims=True))
    mean = jnp.mean(g * u, axis=-1, keepdims=True)
    sg[...] = go_ref[...].astype(f32) + inv * g - u * (inv * inv * inv) * mean


class Links:
    def __init__(self, n):
        self.zs = n // 4
        i = lax.axis_index(DP)
        self.i = i
        self.c = i % 2
        self.x = (i // 2) % 2
        self.z = i // 4

    def owner(self, z, x, c):
        return 4 * z + 2 * x + c

    def dev(self, route):
        step = (4, -4, 2 - 4 * self.x, 1 - 2 * self.c)[route]
        return dict(dp=self.i + step)

    def barrier(self):
        sem = pltpu.get_barrier_semaphore()

        def tell(device):
            pl.semaphore_signal(sem, inc=1, device_id=device, device_id_type=pl.DeviceIdType.MESH)

        tell(self.dev(ACROSS))
        tell(self.dev(CORE))
        tell(dict(section=1 - lax.axis_index(SECTION)))

        @pl.when(self.z < self.zs - 1)
        def _():
            tell(self.dev(UP))

        @pl.when(self.z > 0)
        def _():
            tell(self.dev(DOWN))

        ends = jnp.where(self.z < self.zs - 1, 1, 0) + jnp.where(self.z > 0, 1, 0)
        pl.semaphore_wait(sem, 3 + ends)


def part(ref, index, count):
    return ref.at[pl.ds(pl.multiple_of(index * count, 16), count), :]


def remote(src, dst, send, recv, device):
    return pltpu.make_async_remote_copy(
        src_ref=src,
        dst_ref=dst,
        send_sem=send,
        recv_sem=recv,
        device_id=device,
        device_id_type=pl.DeviceIdType.MESH,
    )


class Gather:
    def __init__(self, links, pieces, line_send, core_send, recv):
        self.k, self.pieces = links, pieces
        self.line_send, self.core_send, self.recv = line_send, core_send, recv

    def copy(self, p, z, x, c, route):
        whole, count = self.pieces[p][:2]
        ref = part(whole, self.k.owner(z, x, c), count)
        if route == CORE:
            send = self.core_send.at[p, 2 * z + x]
        else:
            send = self.line_send.at[p, route, z]
        return remote(ref, ref, send, self.recv.at[p, self.k.owner(z, x, c)], self.k.dev(route))

    def each(self, p, side, r, act):
        k = self.k
        lo, hi = self.pieces[p][2:]
        z = k.z - r if side == BELOW else k.z + r

        @pl.when((z >= lo) & (z < hi))
        def _():
            act(z)

    def pump(self, ps, do):
        k = self.k
        for r in range(k.zs):
            for p in ps:

                def out(z, p=p, r=r, side=None):
                    def go(route):
                        copy = self.copy(p, z, k.x, k.c, route)
                        copy.wait_send() if do == FINISH else copy.start()

                    if r and do == FORWARD:
                        self.copy(p, z, k.x, k.c, ACROSS).wait_recv()
                    if side != ABOVE:

                        @pl.when(k.z < k.zs - 1)
                        def _():
                            go(UP)

                    if side != BELOW:

                        @pl.when(k.z > 0)
                        def _():
                            go(DOWN)

                    go(ACROSS)
                    go(CORE)

                if r == 0:
                    if do != FORWARD:
                        self.each(p, BELOW, 0, out)
                elif do != START:
                    self.each(p, BELOW, r, functools.partial(out, side=BELOW))
                    self.each(p, ABOVE, r, functools.partial(out, side=ABOVE))
            if do == START:
                continue
            for p in ps:

                def across(z, p=p):
                    copy = self.copy(p, z, 1 - k.x, k.c, CORE)
                    if do == FINISH:
                        copy.wait_send()
                    else:
                        copy.wait_recv()
                        copy.start()

                self.each(p, BELOW, r, across)
                if r:
                    self.each(p, ABOVE, r, across)
        if do == FORWARD:
            for p in ps:
                for z in range(*self.pieces[p][2:]):
                    for x in range(2):
                        self.copy(p, z, x, 1 - k.c, CORE).wait_recv()


def add_rows(dst, src, count):
    step = 48 if count % 48 == 0 else 16

    def add(i, carry):
        s = pl.ds(pl.multiple_of(i * step, 16), step)
        dst[s, :] = (dst[s, :].astype(f32) + src[s, :].astype(f32)).astype(dst.dtype)
        return carry

    lax.fori_loop(0, count // step, add, 0)


class Scatter:
    def __init__(self, links, pieces, core_sems, line_sems):
        self.k, self.pieces = links, pieces
        self.core_sems, self.line_sems = core_sems, line_sems

    def copy(self, p, route, z, x=None):
        k = self.k
        g, core, across, below, above, _, count = self.pieces[p]
        if route == CORE:
            slot = 2 * z + x
            send, recv = self.core_sems.at[p, 0, slot], self.core_sems.at[p, 1, slot]
            src, dst = part(g, k.owner(z, x, 1 - k.c), count), part(core, slot, count)
        else:
            at = route
            send, recv = self.line_sems.at[p, 2 * at, z], self.line_sems.at[p, 2 * at + 1, z]
            src = part(g, k.owner(z, 1 - k.x if route == ACROSS else k.x, k.c), count)
            dst = part((below, above, across)[at], z, count)
        return remote(src, dst, send, recv, k.dev(route))

    def far_first(self, i):
        k = self.k
        table = [sorted(range(k.zs), key=lambda o: (-abs(o - z), o))[i] for z in range(k.zs)]
        z = table[0]
        for at in range(1, k.zs):
            z = jnp.where(k.z == at, table[at], z)
        return z

    def start(self, p):
        for i in range(self.k.zs):
            z = self.far_first(i)
            for x in (1 - self.k.x, self.k.x):
                self.copy(p, CORE, z, x).start()

    def across(self, p):
        k = self.k
        g, core, count = self.pieces[p][0], self.pieces[p][1], self.pieces[p][6]
        for i in range(k.zs):
            z = self.far_first(i)
            for x in (1 - k.x, k.x):
                self.copy(p, CORE, z, x).wait_recv()
                add_rows(part(g, k.owner(z, x, k.c), count), part(core, 2 * z + x, count), count)
                if x is not k.x:
                    self.copy(p, ACROSS, z).start()

    def line(self, p):
        k = self.k
        g, _, across, below, above, result, count = self.pieces[p]
        for i in range(k.zs):
            z = self.far_first(i)
            mine = part(g, k.owner(z, k.x, k.c), count)
            self.copy(p, ACROSS, z).wait_recv()
            add_rows(mine, part(across, z, count), count)

            def hop(route, inner, source):
                @pl.when(inner)
                def _():
                    self.copy(p, route, z).wait_recv()
                    add_rows(mine, part(source, z, count), count)

                self.copy(p, route, z).start()

            @pl.when(z > k.z)
            def _():
                hop(UP, k.z > 0, below)

            @pl.when(z < k.z)
            def _():
                hop(DOWN, k.z < k.zs - 1, above)

            @pl.when(z == k.z)
            def _():
                result[...] = mine[...].astype(f32)

                @pl.when(k.z > 0)
                def _():
                    self.copy(p, UP, z).wait_recv()
                    add_rows(result, part(below, z, count), count)

                @pl.when(k.z < k.zs - 1)
                def _():
                    self.copy(p, DOWN, z).wait_recv()
                    add_rows(result, part(above, z, count), count)

    def finish(self, p):
        k = self.k
        for z in range(k.zs):
            for x in range(2):
                self.copy(p, CORE, z, x).wait_send()
            self.copy(p, ACROSS, z).wait_send()

            @pl.when(z > k.z)
            def _():
                self.copy(p, UP, z).wait_send()

            @pl.when(z < k.z)
            def _():
                self.copy(p, DOWN, z).wait_send()


def block(names, inside, n, *refs):
    r = types.SimpleNamespace(**dict(zip(names, refs)))
    sec = lax.axis_index(SECTION)
    links = Links(n)
    r1, r2 = 2 * DI // n, DI // n
    U, GO = r.u, r.go

    @pl.when(sec == 0)
    def _():
        for m in range(MICRO):
            U[pl.ds(m * T, T), :] = r.inputs[m]

    @pl.when(sec == 1)
    def _():
        for m in range(MICRO):
            GO[pl.ds(m * T, T), :] = r.cotangent[m]

    if inside:
        for whole, shard, count in (
            (r.win, r.win_shard, r1),
            (r.wout, r.wout_shard, r2),
            (r.small, r.small_shard, r2),
        ):
            part(whole, links.i, count)[...] = shard[...]
        links.barrier()
        half = links.zs // 2
        gather = Gather(
            links,
            [
                (r.small, r2, 0, links.zs),
                (r.win, r1, 0, half),
                (r.win, r1, half, links.zs),
                (r.wout, r2, 0, links.zs),
            ],
            r.ag_line,
            r.ag_core,
            r.ag_recv,
        )
        gather.pump((0, 1, 2, 3), START)
        gather.pump((0, 1), FORWARD)

        @pl.when(sec == 1)
        def _():
            gather.pump((2, 3), FORWARD)
    else:
        sem = pltpu.get_barrier_semaphore()
        pl.semaphore_signal(
            sem, inc=1, device_id=dict(section=1 - sec), device_id_type=pl.DeviceIdType.MESH
        )
        pl.semaphore_wait(sem, 1)

    rows, small, gain, win, wout = r.rows, r.small, r.gain, r.win, r.wout
    for c in range(DI // C):
        s = pl.ds(c * C, C)
        tr = small[s, 128:256].astype(f32).T
        rows[0:NS, s] = -jnp.exp(tr[0:NS]) * LOG2E
        rows[NS : NS + 8, s] = tr[NS : NS + 8]
    if inside:
        gw = D // n
        lane = iota((1, D), 1)
        acc = jnp.zeros((1, D), f32)
        for i in range(n):
            piece = small[i * r2 : i * r2 + 16, 128:256].astype(f32)[0:1]
            spread = jnp.concatenate([piece, jnp.zeros((1, D - 128), f32)], axis=1)
            moved = pltpu.roll(spread, (i * gw - GAIN_LANE) % D, 1)
            acc = jnp.where((lane >= i * gw) & (lane < (i + 1) * gw), moved, acc)
        gain[...] = acc

    def of(ref, m):
        return ref.at[pl.ds(pl.multiple_of(m * T, T), T), :]

    def boundary(route, m):
        if route == RIGHT:
            src, dst, at = r.section_out.at[m], of(r.u, m), 0
        else:
            src, dst, at = of(r.back, m), of(r.go, m), 1
        return remote(src, dst, r.edge.at[at, 0, m], r.edge.at[at, 1, m], dict(section=1 - sec))

    def forward(k, carry):
        m = k - sec

        @pl.when((m >= 0) & (m < MICRO))
        def _():
            @pl.when(sec == 1)
            def _():
                boundary(RIGHT, m).wait_recv()

            u = of(r.u, m)
            reset = r.reset[m]
            v = u[...].astype(f32)
            inv = lax.rsqrt(jnp.mean(v * v, axis=-1, keepdims=True) + EPS)
            of(r.normed, m)[...] = (v * inv * gain[...]).astype(bf16)
            f_x(reset, of(r.normed, m), win, rows, of(r.x, m), of(r.act, m))
            f_rate(
                reset,
                of(r.act, m),
                small,
                rows,
                of(r.proj, m),
                of(r.rin, m),
                of(r.pre, m),
                r.dec,
                r.gs,
                r.cols,
                r.diag,
            )
            f_scan(
                of(r.act, m), rows, r.dec, r.gs, r.cols, r.diag, r.h.at[m], of(r.ssm, m)
            )
            if inside:

                @pl.when((sec == 0) & (m == 0))
                def _():
                    gather.pump((2, 3), FORWARD)

            f_out(
                u, of(r.normed, m), win, wout, of(r.ssm, m), of(r.z, m), of(r.gated, m), r.section_out.at[m]
            )

            @pl.when(sec == 0)
            def _():
                boundary(RIGHT, m).start()

        return carry

    lax.fori_loop(0, MICRO + 1, forward, 0)
    if inside:
        gather.pump((0, 1, 2, 3), FINISH)

    def backward(k, carry):
        m = k - (1 - sec)

        @pl.when((m >= 0) & (m < MICRO))
        def _():
            @pl.when(sec == 0)
            def _():
                boundary(LEFT, m).wait_recv()

            first = m == 0
            reset = r.reset[m]
            go, gm, sm = of(r.go, m), of(r.gm, m), r.sm
            act, pre = of(r.act, m), of(r.pre, m)
            gs, gd, gr, gb, gc = r.gs, r.dec, r.gr, r.gb, r.gc
            b_gate(first, go, wout, of(r.z, m), of(r.ssm, m), act, gs, gm, sm)
            b_prep(reset, pre, act, of(r.proj, m), r.dec, r.drive, r.cols, r.diag)
            b_scan(
                first,
                gs,
                rows,
                r.dec,
                r.cols,
                r.diag,
                r.drive,
                r.h.at[m],
                r.adj,
                gd,
                gr,
                gb,
                gc,
                sm,
            )
            b_pre(first, act, pre, small, gd, gr, gb, gc, of(r.gpre, m), of(r.gp, m), sm)
            b_conv(first, reset, rows, small, of(r.x, m), gs, gd, pre, of(r.gp, m), gm, sm)
            sg = r.section_grad.at[m]
            b_in(first, of(r.u, m), go, gain, win, gm, sg, r.gg)

            @pl.when(sec == 1)
            def _():
                of(r.back, m)[...] = sg[...].astype(bf16)
                boundary(LEFT, m).start()

        return carry

    lax.fori_loop(0, MICRO + 1, backward, 0)

    gwi, gwo, gws = r.gwi, r.gwo, r.gws
    for c in range(DI // C):
        s = pl.ds(c * C, C)
        gwo[s, :] = tn(r.gated[:, s], GO[...]).astype(gwo.dtype)
    for c in range(2 * DI // C):
        s = pl.ds(c * C, C)
        gwi[s, :] = tn(r.gm[:, s], r.normed[...]).astype(gwi.dtype)
    for c in range(DI // C):
        s = pl.ds(c * C, C)
        head = tn(r.act[:, s], r.gp[...]) + tn(r.gpre[:, s], r.rin[...])
        gws[s, 0:128] = head.astype(gws.dtype)
        tail = jnp.concatenate([r.sm[0:24, s], jnp.zeros((104, C), f32)], axis=0).T
        gws[s, 128:256] = tail.astype(gws.dtype)
    if inside:
        lane = iota((16, 128), 1)
        own = (iota((16, 128), 0) == 0) & (lane >= GAIN_LANE) & (lane < GAIN_LANE + gw)
        for i in range(n):
            moved = pltpu.roll(r.gg[...], (GAIN_LANE - i * gw) % D, 1)[:, 0:128]
            at = pl.ds(i * r2, 16)
            old = gws[at, 128:256].astype(f32)
            gws[at, 128:256] = jnp.where(own, jnp.broadcast_to(moved, (16, 128)), old).astype(gws.dtype)
        scatter = Scatter(
            links,
            [
                (gwo, r.co, r.xo, r.uo, r.do, r.gout_shard, r2),
                (gwi, r.ci, r.xi, r.ui, r.di, r.gin_shard, r1),
                (gws, r.cs, r.xs, r.us, r.ds, r.gsmall_shard, r2),
            ],
            r.rs_core,
            r.rs_line,
        )
        for stage in (scatter.start, scatter.across, scatter.line, scatter.finish):
            for p in range(3):
                stage(p)

    for m in range(MICRO):

        @pl.when(sec == 0)
        def _():
            boundary(RIGHT, m).wait_send()

        @pl.when(sec == 1)
        def _():
            boundary(LEFT, m).wait_send()


def call(n, inside, arrays):
    r1, r2, zs = 2 * DI // n, DI // n, n // 4
    rows2 = MICRO * T
    outs = dict(
        section_out=((MICRO, T, D), bf16),
        section_grad=((MICRO, T, D), f32),
    )
    scratch = dict(
        u=((rows2, D), bf16),
        go=((rows2, D), bf16),
        back=((rows2, D), bf16),
        normed=((rows2, D), bf16),
        x=((rows2, DI), f32),
        z=((rows2, DI), f32),
        pre=((rows2, DI), f32),
        ssm=((rows2, DI), f32),
        act=((rows2, DI), bf16),
        gated=((rows2, DI), bf16),
        gpre=((rows2, DI), bf16),
        gm=((rows2, 2 * DI), bf16),
        proj=((rows2, 128), f32),
        rin=((rows2, 128), bf16),
        gp=((rows2, 128), bf16),
        h=((MICRO, (T + 1) * NS, DI), bf16),
        adj=((T * NS, CS), bf16),
        dec=((T, DI), f32),
        gs=((T, DI), f32),
        gr=((T, DI), f32),
        gb=((T, NS * TB), f32),
        gc=((T, NS * TB), bf16),
        drive=((T, DI), bf16),
        cols=((T * NS, 128), f32),
        diag=((T, NS * TB), bf16),
        rows=((32, DI), f32),
        sm=((32, DI), f32),
    )
    sems = dict(edge=(2, 2, MICRO))
    if inside:
        outs |= dict(gin_shard=((r1, D), f32))
        outs |= dict(gout_shard=((r2, D), f32))
        outs |= dict(gsmall_shard=((r2, 256), f32))
        scratch |= dict(gain=((1, D), f32))
        scratch |= dict(gg=((1, D), f32))
        scratch |= dict(win=((2 * DI, D), bf16))
        scratch |= dict(wout=((DI, D), bf16))
        scratch |= dict(small=((DI, 256), bf16))
        scratch |= dict(gwi=((2 * DI, D), bf16))
        scratch |= dict(gwo=((DI, D), bf16))
        scratch |= dict(gws=((DI, 256), bf16))
        two, one = 2 * zs, zs
        scratch |= dict(ci=((two * r1, D), bf16), co=((two * r2, D), bf16), cs=((two * r2, 256), bf16))
        scratch |= dict(xi=((one * r1, D), bf16), xo=((one * r2, D), bf16), xs=((one * r2, 256), bf16))
        scratch |= dict(ui=((one * r1, D), bf16), uo=((one * r2, D), bf16), us=((one * r2, 256), bf16))
        scratch |= dict(di=((one * r1, D), bf16), do=((one * r2, D), bf16), ds=((one * r2, 256), bf16))
        sems |= dict(ag_line=(4, 3, zs))
        sems |= dict(ag_core=(4, 2 * zs))
        sems |= dict(ag_recv=(4, n))
        sems |= dict(rs_core=(3, 2, 2 * zs))
        sems |= dict(rs_line=(3, 6, zs))
    else:
        outs |= dict(gwi=((2 * DI, D), f32))
        outs |= dict(gwo=((DI, D), f32))
        outs |= dict(gws=((DI, 256), f32))
        outs |= dict(gg=((1, D), f32))
    names = list(arrays) + list(outs) + list(scratch) + list(sems)
    whole = pl.BlockSpec(memory_space=pltpu.VMEM)
    results = pl.pallas_call(
        functools.partial(block, names, inside, n),
        out_shape=[jax.ShapeDtypeStruct(*spec) for spec in outs.values()],
        in_specs=[whole] * len(arrays),
        out_specs=[whole] * len(outs),
        scratch_shapes=[pltpu.VMEM(*spec) for spec in scratch.values()]
        + [pltpu.SemaphoreType.DMA(shape) for shape in sems.values()],
        compiler_params=pltpu.CompilerParams(
            collective_id=0, has_side_effects=True, vmem_limit_bytes=63 * 2**20
        ),
        name="two_layer_block",
    )(*arrays.values())
    return types.SimpleNamespace(**dict(zip(outs, results)))


def on_device(
    inputs,
    cotangent,
    markers,
    norm_gain,
    in_proj,
    conv_weight,
    conv_bias,
    x_proj,
    dt_proj,
    dt_bias,
    a_log,
    d_skip,
    out_proj,
):
    n = lax.axis_size(DP)
    inside = n % 4 == 0 and (DI // n) % 16 == 0
    r2, gw = DI // n, D // n
    first = (jnp.arange(T) == 0)[None, :]
    reset = jnp.where((markers > 0) | first, 1.0, 0.0).astype(f32)[:, :, None]
    win = in_proj[0].T.astype(bf16)
    wout = out_proj[0].astype(bf16)
    gain = jnp.zeros((r2, 128 - GAIN_LANE), f32).at[0, 0:gw].set(norm_gain[0])
    small = jnp.concatenate(
        [
            x_proj[0],
            dt_proj[0].T,
            a_log[0],
            conv_weight[0].T,
            conv_bias[0][:, None],
            dt_bias[0][:, None],
            d_skip[0][:, None],
            jnp.zeros((r2, 1), f32),
            gain,
        ],
        axis=1,
    ).astype(bf16)
    arrays = dict(inputs=inputs, cotangent=cotangent, reset=reset)
    if inside:
        arrays |= dict(win_shard=win, wout_shard=wout, small_shard=small)
        res = call(n, inside, arrays)
        gin, gout, gsmall = res.gin_shard, res.gout_shard, res.gsmall_shard
        ggain = gsmall[0, 128 + GAIN_LANE : 128 + GAIN_LANE + gw]
    else:
        gains = lax.all_gather(norm_gain.astype(bf16), DP, axis=1, tiled=True).astype(f32)
        arrays |= dict(
            win=lax.all_gather(win, DP, axis=0, tiled=True),
            wout=lax.all_gather(wout, DP, axis=0, tiled=True),
            small=lax.all_gather(small, DP, axis=0, tiled=True),
            gain=gains,
        )
        res = call(n, inside, arrays)
        gin = lax.psum_scatter(res.gwi, DP, scatter_dimension=0, tiled=True)
        gout = lax.psum_scatter(res.gwo, DP, scatter_dimension=0, tiled=True)
        gsmall = lax.psum_scatter(res.gws, DP, scatter_dimension=0, tiled=True)
        ggain = lax.psum_scatter(res.gg, DP, scatter_dimension=1, tiled=True)[0]
    tail = gsmall[:, 128:]
    return (
        res.section_out[None],
        res.section_grad[None],
        ggain[None],
        gin.T[None],
        tail[:, NS : NS + KC].T[None],
        tail[:, 20][None],
        gsmall[:, 0 : RK + 2 * NS][None],
        gsmall[:, RK + 2 * NS : 128].T[None],
        tail[:, 21][None],
        tail[:, 0:NS][None],
        tail[:, 22][None],
        gout[None],
    )


def solution(mesh):
    tokens = P(None, DP, None)
    columns = P(SECTION, None, DP)
    channels = P(SECTION, DP)
    rows = P(SECTION, DP, None)
    kept = P(SECTION, None, DP, None)
    weights = (
        channels,
        columns,
        columns,
        channels,
        rows,
        columns,
        channels,
        rows,
        channels,
        rows,
    )
    return jax.shard_map(
        on_device,
        mesh=mesh,
        in_specs=(tokens, tokens, P(None, DP)) + weights,
        out_specs=(kept, kept) + weights,
        check_vma=False,
    )
```

```python
import functools
import types

import jax
import jax.numpy as jnp
from jax import lax
from jax.experimental import pallas as pl
from jax.experimental.pallas import tpu as pltpu
from jax.sharding import PartitionSpec as P

T = 128
D = 768
DI = 1536
NS = 16
KC = 4
RK = 48
MICRO = 2
C = 512
CS = 768
TB = 16
NB = T // TB
EPS = 1e-5
LOG2E = 1.4426950408889634
LN2 = 0.6931471805599453
BIG = 1e30
DP, SECTION = "dp", "section"
UP, DOWN, ACROSS, CORE = range(4)
BELOW, ABOVE = range(2)
START, FINISH = range(2)
RIGHT, LEFT = range(2)
f32 = jnp.float32
bf16 = jnp.bfloat16


def nn(a, b):
    return lax.dot_general(a, b, (((1,), (0,)), ((), ())), preferred_element_type=f32)


def nt(a, b):
    return lax.dot_general(a, b, (((1,), (1,)), ((), ())), preferred_element_type=f32)


def tn(a, b):
    return lax.dot_general(a, b, (((0,), (0,)), ((), ())), preferred_element_type=f32)


def iota(shape, axis):
    return lax.broadcasted_iota(jnp.int32, shape, axis)


def sigmoid(v):
    return 1.0 / (1.0 + jnp.exp(-v))


def softplus(v):
    return jnp.maximum(v, 0.0) + jnp.log1p(jnp.exp(-jnp.abs(v)))


def wide(v):
    return jnp.concatenate([v] * (CS // 128), axis=1)


def keeps(reset):
    keep = [None]
    cur = jnp.ones_like(reset)
    for k in range(1, KC):
        cur = cur * (1.0 - (reset if k == 1 else pltpu.roll(reset, k - 1, 0)))
        keep.append(cur)
    return keep


def block_diagonal(cols):
    tile = (iota((NS, NS * TB), 1) % NS == iota((NS, NS * TB), 0)).astype(bf16)
    rep = nn(cols.astype(bf16), tile)
    own = (iota((T, NS * TB), 1) // NS) == (iota((T, NS * TB), 0) % TB)
    return jnp.where(own, rep, 0.0).astype(bf16)


def lane_columns(dst, val):
    for t in range(T):
        dst[pl.ds(t * NS, NS), :] = jnp.broadcast_to(val[:, t : t + 1], (NS, 128))


def f_x(reset, normed, win, rows, x_ref, act):
    keep = keeps(reset)
    for c in range(DI // C):
        s = pl.ds(c * C, C)
        x = nt(normed[...], win[s, :])
        x_ref[:, s] = x
        v = rows[20:21, s] + rows[16:17, s] * x
        for k in range(1, KC):
            v = v + rows[16 + k : 17 + k, s] * (pltpu.roll(x, k, 0) * keep[k])
        act[:, s] = (v * sigmoid(v)).astype(bf16)


def f_rate(reset, act, small, rows, proj, rin, pre_ref, dec, drive, cols, diag):
    p = nn(act[...], small[:, 0:128])
    proj[...] = p
    lane_columns(cols, p.T[RK : RK + NS, :])
    diag[...] = block_diagonal(p[:, RK + NS : RK + 2 * NS])
    rin[...] = pltpu.roll(jnp.where(iota((T, 128), 1) < RK, p, 0.0), RK + 2 * NS, 1).astype(bf16)
    for c in range(DI // C):
        s = pl.ds(c * C, C)
        pre = nt(rin[...], small[s, 0:128]) + rows[21:22, s]
        pre_ref[:, s] = pre
        rate = softplus(pre)
        dec[:, s] = jnp.where(reset > 0.0, BIG, rate)
        drive[:, s] = rate * act[:, s].astype(f32)


def f_scan(act, rows, dec, drive, cols, diag, h_ref, ssm):
    h_ref[0:NS, :] = jnp.zeros((NS, DI), bf16)
    for c in range(DI // CS):
        s = pl.ds(c * CS, CS)

        def block(i, h):
            t0 = pl.multiple_of(i * TB, TB)
            a2 = rows[0:NS, s]
            d = dec[pl.ds(t0, TB), s]
            v = drive[pl.ds(t0, TB), s]
            for j in range(TB):
                b = wide(cols[pl.ds(t0 * NS + j * NS, NS), :])
                h = jnp.exp2(d[j : j + 1, :] * a2) * h + v[j : j + 1, :] * b
                h_ref[pl.ds(t0 * NS + (j + 1) * NS, NS), s] = h.astype(bf16)
            return h

        lax.fori_loop(0, NB, block, jnp.zeros((NS, CS), f32))

    def sums(i, carry):
        for q in range(4):
            t0 = pl.multiple_of(i * (4 * TB) + q * TB, TB)
            tt = pl.ds(t0, TB)
            y = nn(diag[tt, :], h_ref[pl.ds(t0 * NS + NS, TB * NS), :])
            ssm[tt, :] = y + rows[22:23, :] * act[tt, :].astype(f32)
        return carry

    lax.fori_loop(0, NB // 4, sums, 0)


def f_out(u, normed, win, wout, ssm, z_ref, gated, out):
    acc = u[...].astype(f32)
    for c in range(DI // C):
        s = pl.ds(c * C, C)
        z = nt(normed[...], win[pl.ds(DI + c * C, C), :])
        z_ref[:, s] = z
        g = (ssm[:, s] * (z * sigmoid(z))).astype(bf16)
        gated[:, s] = g
        acc = acc + nn(g, wout[s, :])
    out[...] = acc.astype(bf16)


def total(old, first, value):
    return jnp.where(first, value, old + value)


def b_gate(first, go_ref, wout, z_ref, ssm, act, gs_ref, gm, sm):
    go = go_ref[...]
    for c in range(DI // C):
        s = pl.ds(c * C, C)
        gg = nt(go, wout[s, :])
        z = z_ref[:, s]
        sg = sigmoid(z)
        gs = gg * z * sg
        gs_ref[:, s] = gs
        gm[:, pl.ds(DI + c * C, C)] = (gg * ssm[:, s] * sg * (1.0 + z * (1.0 - sg))).astype(bf16)
        part = jnp.sum(gs * act[:, s].astype(f32), axis=0, keepdims=True)
        sm[22:23, s] = total(sm[22:23, s], first, part)


def b_prep(reset, pre, act, proj, dec, drive, cols, diag):
    p = proj[...]
    lane_columns(cols, p.T[RK + NS : RK + 2 * NS, :])
    diag[...] = block_diagonal(p[:, RK : RK + NS])
    for c in range(DI // C):
        s = pl.ds(c * C, C)
        rate = softplus(pre[:, s])
        dec[:, s] = jnp.where(reset > 0.0, BIG, rate)
        drive[:, s] = (rate * act[:, s].astype(f32)).astype(bf16)


def b_scan(first, gs, rows, dec, cols, diag, drive, h_ref, adj_ref, gd, gr, gb, gc, sm):
    ones = (iota((TB, TB * NS), 1) // NS) == iota((TB, TB * NS), 0)
    od = ones.astype(bf16)

    def state_sums(i, carry):
        for q in range(4):
            t0 = pl.multiple_of(i * (4 * TB) + q * TB, TB)
            tt = pl.ds(t0, TB)
            full = nt(gs[tt, :].astype(bf16), h_ref[pl.ds(t0 * NS + NS, TB * NS), :])
            gc[tt, :] = jnp.where(ones, full, 0.0).astype(bf16)
        return carry

    lax.fori_loop(0, NB // 4, state_sums, 0)
    for c in range(DI // CS):
        s = pl.ds(c * CS, CS)

        def block(i, state):
            carry, acc = state
            t0 = pl.multiple_of((NB - 1 - i) * TB, TB)
            a2 = rows[0:NS, s]
            d = dec[pl.ds(t0, TB), s]
            g = gs[pl.ds(t0, TB), s]
            for j in reversed(range(TB)):
                row = pl.ds(t0 * NS + j * NS, NS)
                adj = g[j : j + 1, :] * wide(cols[row, :]) + carry
                adj_ref[row, :] = adj.astype(bf16)
                dj = d[j : j + 1, :]
                carry = jnp.exp2(dj * a2) * adj
                expo = carry * h_ref[row, s].astype(f32)
                h_ref[row, s] = (expo * a2).astype(bf16)
                acc = acc + expo * dj
            return carry, acc

        zero = jnp.zeros((NS, CS), f32)
        _, acc = lax.fori_loop(0, NB, block, (zero, zero))
        sm[0:NS, s] = total(sm[0:NS, s], first, acc * rows[0:NS, s] * LN2)

        def adjoint_sums(i, carry):
            for q in range(4):
                t0 = pl.multiple_of(i * (4 * TB) + q * TB, TB)
                tt = pl.ds(t0, TB)
                row = pl.ds(t0 * NS, TB * NS)
                gd[tt, s] = nn(diag[tt, :], adj_ref[row, :])
                gr[tt, s] = nn(od, h_ref[row, s]) * LN2
                full = nt(drive[tt, s], adj_ref[row, :])
                gb[tt, :] = full if c == 0 else gb[tt, :] + full
            return carry

        lax.fori_loop(0, NB // 4, adjoint_sums, 0)


def b_pre(first, act, pre, small, gd, gr, gb, gc, gpre, gp, sm):
    acc = jnp.zeros((T, 128), f32)
    for c in range(DI // C):
        s = pl.ds(c * C, C)
        g = ((gr[:, s] + gd[:, s] * act[:, s].astype(f32)) * sigmoid(pre[:, s])).astype(bf16)
        gpre[:, s] = g
        part = jnp.sum(g.astype(f32), axis=0, keepdims=True)
        sm[21:22, s] = total(sm[21:22, s], first, part)
        acc = acc + nn(g, small[s, 0:128])
    k = iota((TB * NS, 128), 0) % NS
    lane = iota((TB * NS, 128), 1)
    own = (iota((T, NS * TB), 1) // NS) == (iota((T, NS * TB), 0) % TB)
    gb_own = jnp.where(own, gb[...], 0.0).astype(bf16)
    bc = nn(gb_own, (lane == RK + k).astype(bf16)) + nn(gc[...], (lane == RK + NS + k).astype(bf16))
    gp[...] = jnp.where(iota((T, 128), 1) < RK, pltpu.roll(acc, RK, 1), bc).astype(bf16)


def b_conv(first, reset, rows, small, x_ref, gs, gd, pre, gp, gm, sm):
    keep = keeps(reset)
    for c in range(DI // C):
        s = pl.ds(c * C, C)
        x = x_ref[:, s]
        xs = [x] + [pltpu.roll(x, k, 0) * keep[k] for k in range(1, KC)]
        v = rows[20:21, s]
        for k in range(KC):
            v = v + rows[16 + k : 17 + k, s] * xs[k]
        ga = gs[:, s] * rows[22:23, s] + gd[:, s] * softplus(pre[:, s]) + nt(gp[...], small[s, 0:128])
        sg = sigmoid(v)
        gc = ga * sg * (1.0 + v * (1.0 - sg))
        part = jnp.sum(gc, axis=0, keepdims=True)
        sm[20:21, s] = total(sm[20:21, s], first, part)
        gx = gc * rows[16:17, s]
        for k in range(KC):
            part = jnp.sum(gc * xs[k], axis=0, keepdims=True)
            sm[16 + k : 17 + k, s] = total(sm[16 + k : 17 + k, s], first, part)
            if k:
                gx = gx + pltpu.roll(gc * keep[k], T - k, 0) * rows[16 + k : 17 + k, s]
        gm[:, s] = gx.astype(bf16)


def b_in(first, u_ref, go_ref, gain, win, gm, sg, gg):
    gn = jnp.zeros((T, D), f32)
    for c in range(2 * DI // C):
        s = pl.ds(c * C, C)
        gn = gn + nn(gm[:, s], win[s, :])
    u = u_ref[...].astype(f32)
    inv = lax.rsqrt(jnp.mean(u * u, axis=-1, keepdims=True) + EPS)
    g = gn * gain[...]
    gg[...] = total(gg[...], first, jnp.sum(gn * u * inv, axis=0, keepdims=True))
    mean = jnp.mean(g * u, axis=-1, keepdims=True)
    sg[...] = go_ref[...].astype(f32) + inv * g - u * (inv * inv * inv) * mean


class Links:
    def __init__(self, n):
        self.zs = n // 4
        i = lax.axis_index(DP)
        self.i = i
        self.c = i % 2
        self.x = (i // 2) % 2
        self.z = i // 4

    def owner(self, z, x, c):
        return 4 * z + 2 * x + c

    def dev(self, route):
        step = (4, -4, 2 - 4 * self.x, 1 - 2 * self.c)[route]
        return dict(dp=self.i + step)

    def greet(self):
        sem = pltpu.get_barrier_semaphore()

        def tell(device):
            pl.semaphore_signal(sem, inc=1, device_id=device, device_id_type=pl.DeviceIdType.MESH)

        tell(self.dev(ACROSS))
        tell(self.dev(CORE))
        tell(dict(section=1 - lax.axis_index(SECTION)))

        @pl.when(self.z < self.zs - 1)
        def _():
            tell(self.dev(UP))

        @pl.when(self.z > 0)
        def _():
            tell(self.dev(DOWN))

    def meet(self):
        ends = jnp.where(self.z < self.zs - 1, 1, 0) + jnp.where(self.z > 0, 1, 0)
        pl.semaphore_wait(pltpu.get_barrier_semaphore(), 3 + ends)


def part(ref, index, count):
    return ref.at[pl.ds(pl.multiple_of(index * count, 16), count), :]


def remote(src, dst, send, recv, device):
    return pltpu.make_async_remote_copy(
        src_ref=src,
        dst_ref=dst,
        send_sem=send,
        recv_sem=recv,
        device_id=device,
        device_id_type=pl.DeviceIdType.MESH,
    )


class Gather:
    def __init__(self, links, pieces, line_send, core_send, recv):
        self.k, self.pieces = links, pieces
        self.line_send, self.core_send, self.recv = line_send, core_send, recv

    def copy(self, p, z, x, c, route):
        whole, count = self.pieces[p][:2]
        ref = part(whole, self.k.owner(z, x, c), count)
        if route == CORE:
            send = self.core_send.at[p, 2 * z + x]
        else:
            send = self.line_send.at[p, route, z]
        return remote(ref, ref, send, self.recv.at[p, self.k.owner(z, x, c)], self.k.dev(route))

    def each(self, p, side, r, act):
        k = self.k
        lo, hi = self.pieces[p][2:]
        z = k.z - r if side == BELOW else k.z + r

        @pl.when((z >= lo) & (z < hi))
        def _():
            act(z)

    def line(self, p, r):
        def pass_on(z, side):
            k = self.k
            self.copy(p, z, k.x, k.c, ACROSS).wait_recv()
            self.go(p, z, side, START)

        for side in (BELOW, ABOVE):
            self.each(p, side, r, functools.partial(pass_on, side=side))

    def go(self, p, z, side, do):
        k = self.k

        def one(route):
            copy = self.copy(p, z, k.x, k.c, route)
            copy.wait_send() if do == FINISH else copy.start()

        one(ACROSS)
        if side != ABOVE:

            @pl.when(k.z < k.zs - 1)
            def _():
                one(UP)

        if side != BELOW:

            @pl.when(k.z > 0)
            def _():
                one(DOWN)

        one(CORE)

    def start(self, p):
        self.each(p, BELOW, 0, lambda z: self.go(p, z, None, START))

    def across(self, p, r):
        def pass_on(z):
            copy = self.copy(p, z, 1 - self.k.x, self.k.c, CORE)
            copy.wait_recv()
            copy.start()

        self.each(p, BELOW, r, pass_on)
        if r:
            self.each(p, ABOVE, r, pass_on)

    def arrived(self, p):
        for z in range(*self.pieces[p][2:]):
            for x in range(2):
                self.copy(p, z, x, 1 - self.k.c, CORE).wait_recv()

    def finish(self, p):
        k = self.k

        def crossed(z):
            self.copy(p, z, 1 - k.x, k.c, CORE).wait_send()

        for r in range(k.zs):
            for side in (BELOW, ABOVE) if r else (BELOW,):
                self.each(p, side, r, lambda z, side=side: self.go(p, z, side if r else None, FINISH))
                self.each(p, side, r, crossed)


def add_rows(dst, src, count):
    step = 48 if count % 48 == 0 else 16

    def add(i, carry):
        s = pl.ds(pl.multiple_of(i * step, 16), step)
        dst[s, :] = (dst[s, :].astype(f32) + src[s, :].astype(f32)).astype(dst.dtype)
        return carry

    lax.fori_loop(0, count // step, add, 0)


class Scatter:
    def __init__(self, links, pieces, core_sems, line_sems):
        self.k, self.pieces = links, pieces
        self.core_sems, self.line_sems = core_sems, line_sems

    def copy(self, p, route, z, x=None):
        k = self.k
        g, core, across, below, above, _, count, _, _ = self.pieces[p]
        if route == CORE:
            slot = 2 * z + x
            send, recv = self.core_sems.at[p, 0, slot], self.core_sems.at[p, 1, slot]
            src, dst = part(g, k.owner(z, x, 1 - k.c), count), part(core, slot, count)
        else:
            send, recv = self.line_sems.at[p, 2 * route, z], self.line_sems.at[p, 2 * route + 1, z]
            src = part(g, k.owner(z, 1 - k.x if route == ACROSS else k.x, k.c), count)
            dst = part((below, above, across)[route], z, count)
        return remote(src, dst, send, recv, k.dev(route))

    def far_first(self, p):
        k = self.k
        lo, hi = self.pieces[p][7:]
        for i in range(hi - lo):
            table = [sorted(range(lo, hi), key=lambda o: (-abs(o - z), o))[i] for z in range(k.zs)]
            z = table[0]
            for at in range(1, k.zs):
                z = jnp.where(k.z == at, table[at], z)
            yield z

    def start(self, p):
        for z in self.far_first(p):
            for x in (1 - self.k.x, self.k.x):
                self.copy(p, CORE, z, x).start()

    def across(self, p):
        k = self.k
        g, core, count = self.pieces[p][0], self.pieces[p][1], self.pieces[p][6]
        for z in self.far_first(p):
            for x in (1 - k.x, k.x):
                self.copy(p, CORE, z, x).wait_recv()
                add_rows(part(g, k.owner(z, x, k.c), count), part(core, 2 * z + x, count), count)
                if x is not k.x:
                    self.copy(p, ACROSS, z).start()

    def line(self, p):
        k = self.k
        g, _, across, below, above, _, count, _, _ = self.pieces[p]
        for z in self.far_first(p):
            mine = part(g, k.owner(z, k.x, k.c), count)
            self.copy(p, ACROSS, z).wait_recv()
            add_rows(mine, part(across, z, count), count)

            def hop(route, inner, source):
                @pl.when(inner)
                def _():
                    self.copy(p, route, z).wait_recv()
                    add_rows(mine, part(source, z, count), count)

                self.copy(p, route, z).start()

            @pl.when(z > k.z)
            def _():
                hop(UP, k.z > 0, below)

            @pl.when(z < k.z)
            def _():
                hop(DOWN, k.z < k.zs - 1, above)

    def own(self, p):
        k = self.k
        g, _, _, below, above, result, count, lo, hi = self.pieces[p]

        @pl.when((k.z >= lo) & (k.z < hi))
        def _():
            result[...] = part(g, k.i, count)[...].astype(f32)

            @pl.when(k.z > 0)
            def _():
                self.copy(p, UP, k.z).wait_recv()
                add_rows(result, part(below, k.z, count), count)

            @pl.when(k.z < k.zs - 1)
            def _():
                self.copy(p, DOWN, k.z).wait_recv()
                add_rows(result, part(above, k.z, count), count)

    def finish(self, p):
        k = self.k
        for z in range(*self.pieces[p][7:]):
            for x in range(2):
                self.copy(p, CORE, z, x).wait_send()
            self.copy(p, ACROSS, z).wait_send()

            @pl.when(z > k.z)
            def _():
                self.copy(p, UP, z).wait_send()

            @pl.when(z < k.z)
            def _():
                self.copy(p, DOWN, z).wait_send()


def weight_rows(tails, rows, gain, n):
    r2, gw = DI // n, D // n
    parts = [tails[i * 32 : i * 32 + 32, :].astype(f32) for i in range(n)]
    rows[...] = jnp.concatenate([p[:, 0:r2] for p in parts], axis=1)
    gain[...] = jnp.concatenate([p[23:24, 0:gw] for p in parts], axis=1)


def block(names, inside, n, *refs):
    r = types.SimpleNamespace(**dict(zip(names, refs)))
    sec = lax.axis_index(SECTION)
    links = Links(n)
    r1, r2, gw = 2 * DI // n, DI // n, D // n
    rows, small, gain, win, wout = r.rows, r.small, r.gain, r.win, r.wout

    def of(ref, m):
        return ref.at[pl.ds(pl.multiple_of(m * T, T), T), :]

    def load(m, at):
        src, dst = ((r.inputs, r.u), (r.cotangent, r.go))[at]
        return pltpu.make_async_copy(src.at[m], of(dst, m), r.loads.at[m])

    r.sm[...] = jnp.zeros_like(r.sm)
    starts = jnp.where((r.markers[...] > 0) | (iota((MICRO, T), 1) == 0), 1.0, 0.0)
    starts = jnp.concatenate([starts, jnp.zeros((8 - MICRO, T), f32)], axis=0).T
    for m in range(MICRO):
        r.reset[m] = jnp.broadcast_to(starts[:, m : m + 1], (T, 128))
    for at in range(2):

        @pl.when(sec == at)
        def _():
            for m in range(MICRO):
                load(m, at).start()

    def boundary(route, m):
        if route == RIGHT:
            src, dst, at = r.section_out.at[m], of(r.u, m), 0
        else:
            src, dst, at = of(r.back, m), of(r.go, m), 1
        return remote(src, dst, r.edge.at[at, 0, m], r.edge.at[at, 1, m], dict(section=1 - sec))

    if inside:
        tails = r.tails
        links.greet()
        part(win, links.i, r1)[...] = r.in_proj[...].astype(bf16)
        part(wout, links.i, r2)[...] = r.out_proj[0].astype(bf16)
        head = jnp.concatenate([r.x_proj[...], r.dt_proj[0]], axis=0).T
        part(small, links.i, r2)[...] = head.astype(bf16)
        top = [r.a_log[...], r.conv_weight[0], r.conv_bias[...], r.dt_bias[...], r.d_skip[...]]
        top.append(jnp.concatenate([r.norm_gain[...], jnp.zeros((1, r2 - gw), f32)], axis=1))
        top = jnp.concatenate(top + [jnp.zeros((8, r2), f32)], axis=0)
        top = jnp.concatenate([top, jnp.zeros((32, 128 - r2), f32)], axis=1)
        part(tails, links.i, 32)[...] = top.astype(bf16)
        links.meet()
        half = links.zs // 2
        pieces = [
            (tails, 32, 0, links.zs),
            (small, r2, 0, links.zs),
            (win, r1, 0, half),
            (win, r1, half, links.zs),
            (wout, r2, 0, links.zs),
        ]
        gather = Gather(links, pieces, r.ag_line, r.ag_core, r.ag_recv)
        early, late = (0, 1, 2), (3, 4)

        def pass_on(ps, hops):
            for hop in hops:
                for p in ps:
                    if hop < links.zs:
                        gather.line(p, hop)
                for p in ps:
                    gather.across(p, hop - 1)

        for p in early + late:
            gather.start(p)
        pass_on(early + late, range(1, links.zs - 1))
        pass_on(early, range(links.zs - 1, links.zs + 1))
        for p in early:
            gather.arrived(p)

        def rest(hops):
            pass_on(late, hops)
            if links.zs in hops:
                for p in late:
                    gather.arrived(p)

        @pl.when(sec == 1)
        def _():
            rest((links.zs - 1, links.zs))

        weight_rows(tails, rows, gain, n)
        scatter = Scatter(
            links,
            [
                (r.gwo, r.co, r.xo, r.uo, r.do, r.gout_shard, r2, 0, links.zs),
                (r.gwi, r.ci, r.xi, r.ui, r.di, r.gin_shard, r1, half, links.zs),
                (r.gwi, r.ci, r.xi, r.ui, r.di, r.gin_shard, r1, 0, half),
                (r.gws, r.cs, r.xs, r.us, r.ds, r.gsmall_shard, r2, 0, links.zs),
                (r.gwt, r.ct, r.xt, r.ut, r.dt, r.gtail_shard, 32, 0, links.zs),
            ],
            r.rs_core,
            r.rs_line,
        )
    else:
        sem = pltpu.get_barrier_semaphore()
        pl.semaphore_signal(
            sem, inc=1, device_id=dict(section=1 - sec), device_id_type=pl.DeviceIdType.MESH
        )
        pl.semaphore_wait(sem, 1)
        rows[...] = r.raw_rows[...]
    for c in range(DI // C):
        s = pl.ds(c * C, C)
        rows[0:NS, s] = -jnp.exp(rows[0:NS, s]) * LOG2E

    def forward(k, carry):
        m = k - sec

        @pl.when((m >= 0) & (m < MICRO))
        def _():
            @pl.when(sec == 1)
            def _():
                boundary(RIGHT, m).wait_recv()

            @pl.when(sec == 0)
            def _():
                load(m, 0).wait()

            def gathering(hops):
                if inside:

                    @pl.when((sec == 0) & (m == 0))
                    def _():
                        rest(hops)

            u = of(r.u, m)
            reset = r.reset[m][:, 0:1]
            v = u[...].astype(f32)
            inv = lax.rsqrt(jnp.mean(v * v, axis=-1, keepdims=True) + EPS)
            normed, act, ssm = of(r.normed, m), of(r.act, m), of(r.ssm, m)
            normed[...] = (v * inv * gain[...]).astype(bf16)
            f_x(reset, normed, win, rows, of(r.x, m), act)
            gathering((links.zs - 1,))
            f_rate(
                reset, act, small, rows, of(r.proj, m), of(r.rin, m), of(r.pre, m), r.dec, r.gs, r.cols, r.diag
            )
            f_scan(act, rows, r.dec, r.gs, r.cols, r.diag, r.h.at[m], ssm)
            gathering((links.zs,))
            f_out(u, normed, win, wout, ssm, of(r.z, m), of(r.gated, m), r.section_out.at[m])

            @pl.when(sec == 0)
            def _():
                boundary(RIGHT, m).start()

        return carry

    lax.fori_loop(0, MICRO + 1, forward, 0)

    @pl.when(sec == 1)
    def _():
        for m in range(MICRO):
            load(m, 1).wait()

    def products_out():
        for c in range(DI // C):
            s = pl.ds(c * C, C)
            r.gwo[s, :] = tn(r.gated[:, s], r.go[...]).astype(r.gwo.dtype)

    def products_in(lo):
        for c in range(DI // C):
            s = pl.ds(lo + c * C, C)
            r.gwi[s, :] = tn(r.gm[:, s], r.normed[...]).astype(r.gwi.dtype)

    def products_small():
        for c in range(DI // C):
            s = pl.ds(c * C, C)
            r.gws[s, :] = (tn(r.act[:, s], r.gp[...]) + tn(r.gpre[:, s], r.rin[...])).astype(r.gws.dtype)
        if inside:
            sm, gg = r.sm[0:32, :], r.gg[...]
            for i in range(n):
                top = pltpu.roll(sm, -i * r2 % DI, 1)[:, 0:128]
                g = pltpu.roll(gg, -i * gw % D, 1)[:, 0:128]
                top = jnp.where(iota((32, 128), 0) == 23, jnp.broadcast_to(g, (32, 128)), top)
                r.gwt[pl.ds(32 * i, 32), :] = top.astype(bf16)

    def backward(k, carry):
        m = k - (1 - sec)

        @pl.when((m >= 0) & (m < MICRO))
        def _():
            @pl.when(sec == 0)
            def _():
                boundary(LEFT, m).wait_recv()

            first = m == 0
            reset = r.reset[m][:, 0:1]
            go, gm, sm = of(r.go, m), of(r.gm, m), r.sm
            act, pre = of(r.act, m), of(r.pre, m)
            gs, gd, gr, gb, gc = r.gs, r.dec, r.gr, r.gb, r.gc

            def last(*steps):
                @pl.when(m == MICRO - 1)
                def _():
                    for step in steps:
                        step()

            def scattering(*steps):
                if inside:
                    last(*(functools.partial(stage, p) for stage, p in steps))

            b_gate(first, go, wout, of(r.z, m), of(r.ssm, m), act, gs, gm, sm)
            last(products_out, lambda: products_in(DI))
            if inside:
                scattering((scatter.start, 0), (scatter.start, 1))
            b_prep(reset, pre, act, of(r.proj, m), r.dec, r.drive, r.cols, r.diag)
            if inside:
                scattering((scatter.across, 0))
            b_scan(
                first, gs, rows, r.dec, r.cols, r.diag, r.drive, r.h.at[m], r.adj, gd, gr, gb, gc, sm
            )
            if inside:
                scattering((scatter.across, 1))
            b_pre(first, act, pre, small, gd, gr, gb, gc, of(r.gpre, m), of(r.gp, m), sm)
            b_conv(first, reset, rows, small, of(r.x, m), gs, gd, pre, of(r.gp, m), gm, sm)
            last(lambda: products_in(0))
            if inside:
                scattering((scatter.start, 2))
            sg = r.section_grad.at[m]
            b_in(first, of(r.u, m), go, gain, win, gm, sg, r.gg)

            @pl.when(sec == 1)
            def _():
                of(r.back, m)[...] = sg[...].astype(bf16)
                boundary(LEFT, m).start()

        return carry

    lax.fori_loop(0, MICRO + 1, backward, 0)
    products_small()
    if inside:
        for p in (3, 4):
            scatter.start(p)
        for p in (2, 3, 4):
            scatter.across(p)
        for p in range(5):
            scatter.line(p)
        for p in range(5):
            scatter.own(p)
        for p in range(5):
            gather.finish(p)
            scatter.finish(p)

    for m in range(MICRO):

        @pl.when(sec == 0)
        def _():
            boundary(RIGHT, m).wait_send()

        @pl.when(sec == 1)
        def _():
            boundary(LEFT, m).wait_send()


def call(n, inside, arrays):
    r1, r2, zs = 2 * DI // n, DI // n, n // 4
    rows2 = MICRO * T
    outs = dict(
        section_out=((MICRO, T, D), bf16),
        section_grad=((MICRO, T, D), f32),
    )
    scratch = dict(
        reset=((MICRO, T, 128), f32),
        u=((rows2, D), bf16),
        go=((rows2, D), bf16),
        back=((rows2, D), bf16),
        normed=((rows2, D), bf16),
        x=((rows2, DI), f32),
        z=((rows2, DI), f32),
        pre=((rows2, DI), f32),
        ssm=((rows2, DI), f32),
        act=((rows2, DI), bf16),
        gated=((rows2, DI), bf16),
        gpre=((rows2, DI), bf16),
        gm=((rows2, 2 * DI), bf16),
        proj=((rows2, 128), f32),
        rin=((rows2, 128), bf16),
        gp=((rows2, 128), bf16),
        h=((MICRO, (T + 1) * NS, DI), bf16),
        adj=((T * NS, CS), bf16),
        dec=((T, DI), f32),
        gs=((T, DI), f32),
        gr=((T, DI), f32),
        gb=((T, NS * TB), f32),
        gc=((T, NS * TB), bf16),
        drive=((T, DI), bf16),
        cols=((T * NS, 128), f32),
        diag=((T, NS * TB), bf16),
        rows=((32, DI), f32),
    )
    sems = dict(edge=(2, 2, MICRO), loads=(MICRO,))
    if inside:
        outs |= dict(
            gin_shard=((r1, D), f32),
            gout_shard=((r2, D), f32),
            gsmall_shard=((r2, 128), f32),
            gtail_shard=((32, 128), f32),
        )
        scratch |= dict(
            sm=((32, DI), f32),
            gain=((1, D), f32),
            gg=((1, D), f32),
            win=((2 * DI, D), bf16),
            wout=((DI, D), bf16),
            small=((DI, 128), bf16),
            tails=((32 * n, 128), bf16),
            gwi=((2 * DI, D), bf16),
            gwo=((DI, D), bf16),
            gws=((DI, 128), bf16),
            gwt=((32 * n, 128), bf16),
            ci=((2 * zs * r1, D), bf16),
            co=((2 * zs * r2, D), bf16),
            cs=((2 * zs * r2, 128), bf16),
            ct=((2 * zs * 32, 128), bf16),
            xi=((zs * r1, D), bf16),
            xo=((zs * r2, D), bf16),
            xs=((zs * r2, 128), bf16),
            xt=((zs * 32, 128), bf16),
            ui=((zs * r1, D), bf16),
            uo=((zs * r2, D), bf16),
            us=((zs * r2, 128), bf16),
            ut=((zs * 32, 128), bf16),
            di=((zs * r1, D), bf16),
            do=((zs * r2, D), bf16),
            ds=((zs * r2, 128), bf16),
            dt=((zs * 32, 128), bf16),
        )
        sems |= dict(
            ag_line=(5, 3, zs),
            ag_core=(5, 2 * zs),
            ag_recv=(5, n),
            rs_core=(5, 2, 2 * zs),
            rs_line=(5, 6, zs),
        )
    else:
        outs |= dict(
            gwi=((2 * DI, D), f32),
            gwo=((DI, D), f32),
            gws=((DI, 128), f32),
            gg=((1, D), f32),
            sm=((32, DI), f32),
        )
    names = list(arrays) + list(outs) + list(scratch) + list(sems)
    whole = pl.BlockSpec(memory_space=pltpu.VMEM)
    far = pl.BlockSpec(memory_space=pl.ANY)
    results = pl.pallas_call(
        functools.partial(block, names, inside, n),
        out_shape=[jax.ShapeDtypeStruct(*spec) for spec in outs.values()],
        in_specs=[far] * 2 + [whole] * (len(arrays) - 2),
        out_specs=[whole] * len(outs),
        scratch_shapes=[pltpu.VMEM(*spec) for spec in scratch.values()]
        + [pltpu.SemaphoreType.DMA(shape) for shape in sems.values()],
        compiler_params=pltpu.CompilerParams(
            collective_id=0, has_side_effects=True, vmem_limit_bytes=63 * 2**20
        ),
        name="two_layer_block",
    )(*arrays.values())
    return types.SimpleNamespace(**dict(zip(outs, results)))


def unpack(
    out, grad, gin, gout, gsmall, gtail, out_o, grad_o, gain_o, in_o, cw_o, cb_o, x_o, dt_o, db_o, a_o, ds_o, po_o
):
    r2, gw = cb_o.shape[1], gain_o.shape[1]
    out_o[0] = out[...]
    grad_o[0] = grad[...]
    po_o[0] = gout[...]
    in_o[...] = gin[...]
    gain_o[...] = gtail[23:24, 0:gw]
    cw_o[0] = gtail[NS : NS + KC, 0:r2]
    cb_o[...] = gtail[20:21, 0:r2]
    db_o[...] = gtail[21:22, 0:r2]
    ds_o[...] = gtail[22:23, 0:r2]
    a_o[...] = gtail[0:NS, 0:r2]
    small = gsmall[...].T
    x_o[...] = small[0 : RK + 2 * NS, :]
    dt_o[0] = small[RK + 2 * NS : 128, :]


def on_device(inputs, cotangent, markers, *weights):
    (
        norm_gain,
        in_proj,
        conv_weight,
        conv_bias,
        x_proj,
        dt_proj,
        dt_bias,
        a_log,
        d_skip,
        out_proj,
    ) = weights
    n = lax.axis_size(DP)
    inside = n == 16
    arrays = dict(inputs=inputs, cotangent=cotangent, markers=markers)
    if inside:
        arrays |= dict(
            norm_gain=norm_gain,
            in_proj=in_proj[0].T,
            conv_weight=conv_weight,
            conv_bias=conv_bias,
            x_proj=x_proj[0].T,
            dt_proj=dt_proj,
            dt_bias=dt_bias,
            a_log=a_log[0].T,
            d_skip=d_skip,
            out_proj=out_proj,
        )
        res = call(n, inside, arrays)
        whole = pl.BlockSpec(memory_space=pltpu.VMEM)
        turned = (in_proj, x_proj, a_log)
        shapes = [((1,) + res.section_out.shape, bf16), ((1,) + res.section_grad.shape, f32)]
        shapes += [(w.shape[:0:-1] if any(w is t for t in turned) else w.shape, f32) for w in weights]
        done = pl.pallas_call(
            unpack,
            out_shape=[jax.ShapeDtypeStruct(*spec) for spec in shapes],
            in_specs=[whole] * 6,
            out_specs=[whole] * 12,
            name="unpack",
        )(
            res.section_out,
            res.section_grad,
            res.gin_shard,
            res.gout_shard,
            res.gsmall_shard,
            res.gtail_shard,
        )
        grads = (g.T[None] if any(w is t for t in turned) else g for w, g in zip(weights, done[2:]))
        return (*done[:2], *grads)

    def gathered(value, axis):
        return lax.all_gather(value.astype(bf16), DP, axis=axis, tiled=True)

    r2 = DI // n
    raw = jnp.concatenate(
        [a_log[0].T, conv_weight[0], conv_bias, dt_bias, d_skip, jnp.zeros((9, r2), f32)], axis=0
    )
    arrays |= dict(
        win=gathered(in_proj[0].T, 0),
        wout=gathered(out_proj[0], 0),
        small=gathered(jnp.concatenate([x_proj[0], dt_proj[0].T], axis=1), 0),
        raw_rows=gathered(raw, 1).astype(f32),
        gain=gathered(norm_gain, 1).astype(f32),
    )
    res = call(n, inside, arrays)

    def scattered(value, axis):
        return lax.psum_scatter(value, DP, scatter_dimension=axis, tiled=True)

    gin, gout, gsmall = scattered(res.gwi, 0), scattered(res.gwo, 0), scattered(res.gws, 0)
    rows = scattered(res.sm, 1)
    return (
        res.section_out[None],
        res.section_grad[None],
        scattered(res.gg, 1),
        gin.T[None],
        rows[NS : NS + KC][None],
        rows[20:21],
        gsmall[:, 0 : RK + 2 * NS][None],
        gsmall[:, RK + 2 * NS : 128].T[None],
        rows[21:22],
        rows[0:NS].T[None],
        rows[22:23],
        gout[None],
    )


def solution(mesh):
    tokens = P(None, DP, None)
    columns = P(SECTION, None, DP)
    channels = P(SECTION, DP)
    rows = P(SECTION, DP, None)
    kept = P(SECTION, None, DP, None)
    weights = (
        channels,
        columns,
        columns,
        channels,
        rows,
        columns,
        channels,
        rows,
        channels,
        rows,
    )
    return jax.shard_map(
        on_device,
        mesh=mesh,
        in_specs=(tokens, tokens, P(None, DP)) + weights,
        out_specs=(kept, kept) + weights,
        check_vma=False,
    )
```

```python
import functools
import types

import jax
import jax.numpy as jnp
from jax import lax
from jax.experimental import pallas as pl
from jax.experimental.pallas import tpu as pltpu
from jax.sharding import PartitionSpec as P

T = 128
D = 768
DI = 1536
NS = 16
KC = 4
RK = 48
MICRO = 2
C = 512
CS = 768
TB = 16
NB = T // TB
EPS = 1e-5
LOG2E = 1.4426950408889634
LN2 = 0.6931471805599453
BIG = 1e30
DP, SECTION = "dp", "section"
UP, DOWN, ACROSS, CORE = range(4)
BELOW, ABOVE = range(2)
START, FINISH = range(2)
RIGHT, LEFT = range(2)
f32 = jnp.float32
bf16 = jnp.bfloat16


def nn(a, b):
    return lax.dot_general(a, b, (((1,), (0,)), ((), ())), preferred_element_type=f32)


def nt(a, b):
    return lax.dot_general(a, b, (((1,), (1,)), ((), ())), preferred_element_type=f32)


def tn(a, b):
    return lax.dot_general(a, b, (((0,), (0,)), ((), ())), preferred_element_type=f32)


def iota(shape, axis):
    return lax.broadcasted_iota(jnp.int32, shape, axis)


def sigmoid(v):
    return 1.0 / (1.0 + jnp.exp(-v))


def wide(v):
    return jnp.concatenate([v] * (CS // 128), axis=1)


def keeps(reset):
    keep = [None]
    cur = jnp.ones_like(reset)
    for k in range(1, KC):
        cur = cur * (1.0 - (reset if k == 1 else pltpu.roll(reset, k - 1, 0)))
        keep.append(cur)
    return keep


def block_diagonal(cols):
    tile = (iota((NS, NS * TB), 1) % NS == iota((NS, NS * TB), 0)).astype(bf16)
    rep = nn(cols.astype(bf16), tile)
    own = (iota((T, NS * TB), 1) // NS) == (iota((T, NS * TB), 0) % TB)
    return jnp.where(own, rep, 0.0).astype(bf16)


def lane_columns(dst, val):
    for t in range(T):
        dst[pl.ds(t * NS, NS), :] = jnp.broadcast_to(val[:, t : t + 1], (NS, 128))


def f_x(reset, normed, win, rows, x_ref, act, dact):
    keep = keeps(reset)
    for c in range(DI // C):
        s = pl.ds(c * C, C)
        x = nt(normed[...], win[s, :])
        x_ref[:, s] = x
        v = rows[20:21, s] + rows[16:17, s] * x
        for k in range(1, KC):
            v = v + rows[16 + k : 17 + k, s] * (pltpu.roll(x, k, 0) * keep[k])
        sg = sigmoid(v)
        act[:, s] = (v * sg).astype(bf16)
        dact[:, s] = sg * (1.0 + v * (1.0 - sg))


def f_rate(reset, act, small, rows, proj, rin, rate_ref, drate, dec, drive, drive_low, cols, diag):
    p = nn(act[...], small[:, 0:128])
    proj[...] = p
    lane_columns(cols, p.T[RK : RK + NS, :])
    diag[...] = block_diagonal(p[:, RK + NS : RK + 2 * NS])
    rin[...] = pltpu.roll(jnp.where(iota((T, 128), 1) < RK, p, 0.0), RK + 2 * NS, 1).astype(bf16)
    for c in range(DI // C):
        s = pl.ds(c * C, C)
        pre = nt(rin[...], small[s, 0:128]) + rows[21:22, s]
        e = jnp.exp(-jnp.abs(pre))
        rate = jnp.maximum(pre, 0.0) + jnp.log1p(e)
        rate_ref[:, s] = rate
        drate[:, s] = jnp.where(pre >= 0.0, 1.0, e) / (1.0 + e)
        dec[:, s] = jnp.where(reset > 0.0, BIG, rate)
        both = rate * act[:, s].astype(f32)
        drive[:, s] = both
        drive_low[:, s] = both.astype(bf16)


def f_scan(act, rows, dec, drive, cols, diag, h_ref, ssm):
    h_ref[0:NS, :] = jnp.zeros((NS, DI), bf16)
    for c in range(DI // CS):
        s = pl.ds(c * CS, CS)

        def block(i, h):
            t0 = pl.multiple_of(i * TB, TB)
            a2 = rows[0:NS, s]
            d = dec[pl.ds(t0, TB), s]
            v = drive[pl.ds(t0, TB), s]
            for j in range(TB):
                b = wide(cols[pl.ds(t0 * NS + j * NS, NS), :])
                h = jnp.exp2(d[j : j + 1, :] * a2) * h + v[j : j + 1, :] * b
                h_ref[pl.ds(t0 * NS + (j + 1) * NS, NS), s] = h.astype(bf16)
            return h

        lax.fori_loop(0, NB, block, jnp.zeros((NS, CS), f32))

    def sums(i, carry):
        for q in range(4):
            t0 = pl.multiple_of(i * (4 * TB) + q * TB, TB)
            tt = pl.ds(t0, TB)
            y = nn(diag[tt, :], h_ref[pl.ds(t0 * NS + NS, TB * NS), :])
            ssm[tt, :] = y + rows[22:23, :] * act[tt, :].astype(f32)
        return carry

    lax.fori_loop(0, NB // 4, sums, 0)


def f_out(u, normed, win, wout, ssm, sz_ref, dz_ref, gated, out):
    acc = u[...].astype(f32)
    for c in range(DI // C):
        s = pl.ds(c * C, C)
        z = nt(normed[...], win[pl.ds(DI + c * C, C), :])
        sg = sigmoid(z)
        sz = z * sg
        sz_ref[:, s] = sz
        dz_ref[:, s] = ssm[:, s] * (sg * (1.0 + z * (1.0 - sg)))
        g = (ssm[:, s] * sz).astype(bf16)
        gated[:, s] = g
        acc = acc + nn(g, wout[s, :])
    out[...] = acc.astype(bf16)


def total(old, first, value):
    return jnp.where(first, value, old + value)


def b_gate(first, go_ref, wout, sz, dz, act, gs_ref, gm, sm):
    go = go_ref[...]
    for c in range(DI // C):
        s = pl.ds(c * C, C)
        gg = nt(go, wout[s, :])
        gs = gg * sz[:, s]
        gs_ref[:, s] = gs
        gm[:, pl.ds(DI + c * C, C)] = (gg * dz[:, s]).astype(bf16)
        part = jnp.sum(gs * act[:, s].astype(f32), axis=0, keepdims=True)
        sm[22:23, s] = total(sm[22:23, s], first, part)


def b_prep(proj, cols, diag):
    p = proj[...]
    lane_columns(cols, p.T[RK + NS : RK + 2 * NS, :])
    diag[...] = block_diagonal(p[:, RK : RK + NS])


def b_scan(between, first, gs, rows, dec, cols, diag, drive, h_ref, adj_ref, gd, gr, gb, gc, sm):
    ones = (iota((TB, TB * NS), 1) // NS) == iota((TB, TB * NS), 0)
    od = ones.astype(bf16)

    def state_sums(i, carry):
        for q in range(4):
            t0 = pl.multiple_of(i * (4 * TB) + q * TB, TB)
            tt = pl.ds(t0, TB)
            full = nt(gs[tt, :].astype(bf16), h_ref[pl.ds(t0 * NS + NS, TB * NS), :])
            gc[tt, :] = jnp.where(ones, full, 0.0).astype(bf16)
        return carry

    lax.fori_loop(0, NB // 4, state_sums, 0)
    for c in range(DI // CS):
        s = pl.ds(c * CS, CS)

        def block(i, state):
            carry, acc = state
            t0 = pl.multiple_of((NB - 1 - i) * TB, TB)
            a2 = rows[0:NS, s]
            d = dec[pl.ds(t0, TB), s]
            g = gs[pl.ds(t0, TB), s]
            for j in reversed(range(TB)):
                row = pl.ds(t0 * NS + j * NS, NS)
                adj = g[j : j + 1, :] * wide(cols[row, :]) + carry
                adj_ref[row, :] = adj.astype(bf16)
                dj = d[j : j + 1, :]
                carry = jnp.exp2(dj * a2) * adj
                expo = carry * h_ref[row, s].astype(f32)
                h_ref[row, s] = (expo * a2).astype(bf16)
                acc = acc + expo * dj
            return carry, acc

        zero = jnp.zeros((NS, CS), f32)
        _, acc = lax.fori_loop(0, NB, block, (zero, zero))
        sm[0:NS, s] = total(sm[0:NS, s], first, acc * rows[0:NS, s] * LN2)

        def adjoint_sums(i, carry):
            for q in range(4):
                t0 = pl.multiple_of(i * (4 * TB) + q * TB, TB)
                tt = pl.ds(t0, TB)
                row = pl.ds(t0 * NS, TB * NS)
                gd[tt, s] = nn(diag[tt, :], adj_ref[row, :])
                gr[tt, s] = nn(od, h_ref[row, s]) * LN2
                full = nt(drive[tt, s], adj_ref[row, :])
                gb[tt, :] = full if c == 0 else gb[tt, :] + full
            return carry

        lax.fori_loop(0, NB // 4, adjoint_sums, 0)
        if c == 0 and between is not None:
            between()


def b_pre(first, act, drate, small, gd, gr, gb, gc, gpre, gp, sm):
    acc = jnp.zeros((T, 128), f32)
    for c in range(DI // C):
        s = pl.ds(c * C, C)
        g = ((gr[:, s] + gd[:, s] * act[:, s].astype(f32)) * drate[:, s]).astype(bf16)
        gpre[:, s] = g
        part = jnp.sum(g.astype(f32), axis=0, keepdims=True)
        sm[21:22, s] = total(sm[21:22, s], first, part)
        acc = acc + nn(g, small[s, 0:128])
    k = iota((TB * NS, 128), 0) % NS
    lane = iota((TB * NS, 128), 1)
    own = (iota((T, NS * TB), 1) // NS) == (iota((T, NS * TB), 0) % TB)
    gb_own = jnp.where(own, gb[...], 0.0).astype(bf16)
    bc = nn(gb_own, (lane == RK + k).astype(bf16)) + nn(gc[...], (lane == RK + NS + k).astype(bf16))
    gp[...] = jnp.where(iota((T, 128), 1) < RK, pltpu.roll(acc, RK, 1), bc).astype(bf16)


def b_conv(first, reset, rows, small, x_ref, dact, gs, gd, rate, gp, gm, sm):
    keep = keeps(reset)
    for c in range(DI // C):
        s = pl.ds(c * C, C)
        ga = gs[:, s] * rows[22:23, s] + gd[:, s] * rate[:, s] + nt(gp[...], small[s, 0:128])
        gc = ga * dact[:, s]
        x = x_ref[:, s]
        part = jnp.sum(gc, axis=0, keepdims=True)
        sm[20:21, s] = total(sm[20:21, s], first, part)
        gx = jnp.zeros((T, C), f32)
        for k in range(KC):
            ahead = pltpu.roll(gc * keep[k], T - k, 0) if k else gc
            part = jnp.sum(ahead * x, axis=0, keepdims=True)
            sm[16 + k : 17 + k, s] = total(sm[16 + k : 17 + k, s], first, part)
            gx = gx + ahead * rows[16 + k : 17 + k, s]
        gm[:, s] = gx.astype(bf16)


def b_in(first, u_ref, go_ref, gain, win, gm, sg, gg):
    gn = jnp.zeros((T, D), f32)
    for c in range(2 * DI // C):
        s = pl.ds(c * C, C)
        gn = gn + nn(gm[:, s], win[s, :])
    u = u_ref[...].astype(f32)
    inv = lax.rsqrt(jnp.mean(u * u, axis=-1, keepdims=True) + EPS)
    g = gn * gain[...]
    gg[...] = total(gg[...], first, jnp.sum(gn * u * inv, axis=0, keepdims=True))
    mean = jnp.mean(g * u, axis=-1, keepdims=True)
    sg[...] = go_ref[...].astype(f32) + inv * g - u * (inv * inv * inv) * mean


class Links:
    def __init__(self, n):
        self.zs = n // 4
        i = lax.axis_index(DP)
        self.i = i
        self.c = i % 2
        self.x = (i // 2) % 2
        self.z = i // 4

    def owner(self, z, x, c):
        return 4 * z + 2 * x + c

    def dev(self, route):
        step = (4, -4, 2 - 4 * self.x, 1 - 2 * self.c)[route]
        return dict(dp=self.i + step)

    def greet(self):
        sem = pltpu.get_barrier_semaphore()

        def tell(device):
            pl.semaphore_signal(sem, inc=1, device_id=device, device_id_type=pl.DeviceIdType.MESH)

        tell(self.dev(ACROSS))
        tell(self.dev(CORE))
        tell(dict(section=1 - lax.axis_index(SECTION)))

        @pl.when(self.z < self.zs - 1)
        def _():
            tell(self.dev(UP))

        @pl.when(self.z > 0)
        def _():
            tell(self.dev(DOWN))

    def meet(self):
        ends = jnp.where(self.z < self.zs - 1, 1, 0) + jnp.where(self.z > 0, 1, 0)
        pl.semaphore_wait(pltpu.get_barrier_semaphore(), 3 + ends)


def part(ref, index, count, first=0, rows=None):
    return ref.at[pl.ds(pl.multiple_of(index * count + first, 16), rows or count), :]


def remote(src, dst, send, recv, device):
    return pltpu.make_async_remote_copy(
        src_ref=src,
        dst_ref=dst,
        send_sem=send,
        recv_sem=recv,
        device_id=device,
        device_id_type=pl.DeviceIdType.MESH,
    )


class Gather:
    def __init__(self, links, pieces, line_send, core_send, recv):
        self.k, self.pieces = links, pieces
        self.line_send, self.core_send, self.recv = line_send, core_send, recv

    def copy(self, p, z, x, c, route):
        whole, count = self.pieces[p][:2]
        ref = part(whole, self.k.owner(z, x, c), count)
        if route == CORE:
            send = self.core_send.at[p, 2 * z + x]
        else:
            send = self.line_send.at[p, route, z]
        return remote(ref, ref, send, self.recv.at[p, self.k.owner(z, x, c)], self.k.dev(route))

    def each(self, p, side, r, act):
        k = self.k
        lo, hi = self.pieces[p][2:]
        z = k.z - r if side == BELOW else k.z + r

        @pl.when((z >= lo) & (z < hi))
        def _():
            act(z)

    def line(self, p, r):
        def pass_on(z, side):
            k = self.k
            self.copy(p, z, k.x, k.c, ACROSS).wait_recv()
            self.go(p, z, side, START)

        for side in (BELOW, ABOVE):
            self.each(p, side, r, functools.partial(pass_on, side=side))

    def go(self, p, z, side, do):
        k = self.k

        def one(route):
            copy = self.copy(p, z, k.x, k.c, route)
            copy.wait_send() if do == FINISH else copy.start()

        one(ACROSS)
        if side != ABOVE:

            @pl.when(k.z < k.zs - 1)
            def _():
                one(UP)

        if side != BELOW:

            @pl.when(k.z > 0)
            def _():
                one(DOWN)

        one(CORE)

    def start(self, p):
        self.each(p, BELOW, 0, lambda z: self.go(p, z, None, START))

    def across(self, p, r):
        def pass_on(z):
            copy = self.copy(p, z, 1 - self.k.x, self.k.c, CORE)
            copy.wait_recv()
            copy.start()

        self.each(p, BELOW, r, pass_on)
        if r:
            self.each(p, ABOVE, r, pass_on)

    def arrived(self, p):
        for z in range(*self.pieces[p][2:]):
            for x in range(2):
                self.copy(p, z, x, 1 - self.k.c, CORE).wait_recv()

    def finish(self, p):
        k = self.k

        def crossed(z):
            self.copy(p, z, 1 - k.x, k.c, CORE).wait_send()

        for r in range(k.zs):
            for side in (BELOW, ABOVE) if r else (BELOW,):
                self.each(p, side, r, lambda z, side=side: self.go(p, z, side if r else None, FINISH))
                self.each(p, side, r, crossed)


def add_rows(dst, src):
    count = dst.shape[0]
    step = 48 if count % 48 == 0 else 16

    def add(i, carry):
        s = pl.ds(pl.multiple_of(i * step, 16), step)
        dst[s, :] = (dst[s, :].astype(f32) + src[s, :].astype(f32)).astype(dst.dtype)
        return carry

    lax.fori_loop(0, count // step, add, 0)


class Scatter:
    def __init__(self, links, pieces, core_sems, line_sems):
        self.k, self.pieces = links, pieces
        self.core_sems, self.line_sems = core_sems, line_sems

    def rows(self, p, c, z, count=1):
        g, first, _, _, _, _, size, _, _ = self.pieces[p]
        return part(g, 1, first + (c * self.k.zs + z) * size, 0, count * size)

    def mine(self, p, z):
        return self.rows(p, self.k.c, z)

    def copy(self, p, route, z=None):
        k = self.k
        _, _, core, below, above, _, size, lo, hi = self.pieces[p]
        if route == CORE:
            send, recv = self.core_sems.at[p, 0], self.core_sems.at[p, 1]
            src, dst = self.rows(p, 1 - k.c, lo, hi - lo), part(core, 1, lo * size, 0, (hi - lo) * size)
        else:
            send, recv = self.line_sems.at[p, 2 * route, z], self.line_sems.at[p, 2 * route + 1, z]
            src, dst = self.mine(p, z), part((below, above)[route], z, size)
        return remote(src, dst, send, recv, k.dev(route))

    def far_first(self, p):
        k = self.k
        lo, hi = self.pieces[p][7:]
        for i in range(hi - lo):
            table = [sorted(range(lo, hi), key=lambda o: (-abs(o - z), o))[i] for z in range(k.zs)]
            z = table[0]
            for at in range(1, k.zs):
                z = jnp.where(k.z == at, table[at], z)
            yield z

    def start(self, p):
        self.copy(p, CORE).start()

    def core(self, p):
        _, _, core, _, _, _, size, lo, hi = self.pieces[p]
        self.copy(p, CORE).wait_recv()
        add_rows(self.rows(p, self.k.c, lo, hi - lo), part(core, 1, lo * size, 0, (hi - lo) * size))

    def line(self, p):
        k = self.k
        _, _, _, below, above, _, size, _, _ = self.pieces[p]
        for z in self.far_first(p):

            def hop(route, inner, source):
                @pl.when(inner)
                def _():
                    self.copy(p, route, z).wait_recv()
                    add_rows(self.mine(p, z), part(source, z, size))

                self.copy(p, route, z).start()

            @pl.when(z > k.z)
            def _():
                hop(UP, k.z > 0, below)

            @pl.when(z < k.z)
            def _():
                hop(DOWN, k.z < k.zs - 1, above)

    def own(self, p):
        k = self.k
        _, _, _, below, above, result, size, lo, hi = self.pieces[p]

        @pl.when((k.z >= lo) & (k.z < hi))
        def _():
            result[...] = self.mine(p, k.z)[...].astype(f32)

            @pl.when(k.z > 0)
            def _():
                self.copy(p, UP, k.z).wait_recv()
                add_rows(result, part(below, k.z, size))

            @pl.when(k.z < k.zs - 1)
            def _():
                self.copy(p, DOWN, k.z).wait_recv()
                add_rows(result, part(above, k.z, size))

    def finish(self, p):
        k = self.k
        self.copy(p, CORE).wait_send()
        for z in range(*self.pieces[p][7:]):

            @pl.when(z > k.z)
            def _():
                self.copy(p, UP, z).wait_send()

            @pl.when(z < k.z)
            def _():
                self.copy(p, DOWN, z).wait_send()


def weight_rows(tails, rows, gain, n):
    r2, gw = DI // n, D // n
    parts = [tails[i * 32 : i * 32 + 32, :].astype(f32) for i in range(n)]
    rows[...] = jnp.concatenate([p[:, 0:r2] for p in parts], axis=1)
    gain[...] = jnp.concatenate([p[23:24, 0:gw] for p in parts], axis=1)


def block(names, inside, n, *refs):
    r = types.SimpleNamespace(**dict(zip(names, refs)))
    sec = lax.axis_index(SECTION)
    links = Links(n)
    r1, r2, gw = 2 * DI // n, DI // n, D // n
    r3 = r2 + 32
    rows, small, gain, win, wout = r.rows, r.small, r.gain, r.win, r.wout

    def of(ref, m):
        return ref.at[pl.ds(pl.multiple_of(m * T, T), T), :]

    def load(m, at):
        src, dst = ((r.inputs, r.u), (r.cotangent, r.go))[at]
        return pltpu.make_async_copy(src.at[m], of(dst, m), r.loads.at[m])

    r.sm[...] = jnp.zeros_like(r.sm)
    starts = jnp.where((r.markers[...] > 0) | (iota((MICRO, T), 1) == 0), 1.0, 0.0)
    starts = jnp.concatenate([starts, jnp.zeros((8 - MICRO, T), f32)], axis=0).T
    for m in range(MICRO):
        r.reset[m] = jnp.broadcast_to(starts[:, m : m + 1], (T, 128))
    for at in range(2):

        @pl.when(sec == at)
        def _():
            for m in range(MICRO):
                load(m, at).start()

    def boundary(route, m):
        if route == RIGHT:
            src, dst, at = r.section_out.at[m], of(r.u, m), 0
        else:
            src, dst, at = of(r.back, m), of(r.go, m), 1
        return remote(src, dst, r.edge.at[at, 0, m], r.edge.at[at, 1, m], dict(section=1 - sec))

    if inside:
        tails = r.tails
        links.greet()
        part(win, links.i, r1)[...] = r.in_proj[...].astype(bf16)
        part(wout, links.i, r2)[...] = r.out_proj[0].astype(bf16)
        head = jnp.concatenate([r.x_proj[...], r.dt_proj[0]], axis=0).T
        part(small, links.i, r2)[...] = head.astype(bf16)
        top = [r.a_log[...], r.conv_weight[0], r.conv_bias[...], r.dt_bias[...], r.d_skip[...]]
        top.append(jnp.concatenate([r.norm_gain[...], jnp.zeros((1, r2 - gw), f32)], axis=1))
        top = jnp.concatenate(top + [jnp.zeros((8, r2), f32)], axis=0)
        top = jnp.concatenate([top, jnp.zeros((32, 128 - r2), f32)], axis=1)
        part(tails, links.i, 32)[...] = top.astype(bf16)
        links.meet()
        half = links.zs // 2
        pieces = [
            (tails, 32, 0, links.zs),
            (small, r2, 0, links.zs),
            (win, r1, 0, half),
            (win, r1, half, links.zs),
            (wout, r2, 0, links.zs),
        ]
        gather = Gather(links, pieces, r.ag_line, r.ag_core, r.ag_recv)
        early, late = (0, 1, 2), (3, 4)

        def pass_on(ps, hops):
            for hop in hops:
                for p in ps:
                    if hop < links.zs:
                        gather.line(p, hop)
                for p in ps:
                    gather.across(p, hop - 1)

        for p in early + late:
            gather.start(p)
        pass_on(early + late, range(1, links.zs - 1))
        pass_on(early, range(links.zs - 1, links.zs + 1))
        for p in early:
            gather.arrived(p)

        def rest(hops):
            pass_on(late, hops)
            if links.zs in hops:
                for p in late:
                    gather.arrived(p)

        @pl.when(sec == 1)
        def _():
            rest((links.zs - 1, links.zs))

        weight_rows(tails, rows, gain, n)
        half_rows = 2 * links.zs
        pieces = [
            (r.gwo, 0, r.co, r.uo, r.do, r.gout_shard, r2, 0, links.zs),
            (r.gwi, 0, r.ci, r.ui, r.di, r.gin_shard, r1, half, links.zs),
            (r.gwi, 0, r.ci, r.ui, r.di, r.gin_shard, r1, 0, half),
            (r.gws, links.x * half_rows * r3, r.cs, None, None, None, r3, 0, links.zs),
        ]
        scatter = Scatter(links, pieces, r.rs_core, r.rs_line)
        strip = 2 * r1

        def operand(kind, m, zz=0):
            src = of((r.gated, r.normed, r.go, r.gm)[kind], m)
            dst = of((r.xg, r.xn, r.xo, r.xm)[kind], m)
            if kind == 3:
                at = pl.multiple_of((2 * zz + 1 - links.x) * strip, 128)
                src, dst = src.at[:, pl.ds(at, strip)], dst.at[:, pl.ds(zz * strip, strip)]
            sems = r.xs_sems.at[kind + zz, m]
            return remote(src, dst, sems.at[0], sems.at[1], links.dev(ACROSS))

        def small_across():
            sems = r.xs_sems.at[7, 0]
            src = part(r.gws, 1 - links.x, half_rows * r3)
            return remote(src, r.xs, sems.at[0], sems.at[1], links.dev(ACROSS))

        def small_direct(act):
            for step in range(1, links.zs):
                to = (links.z + step) % links.zs
                sems = r.xs_sems.at[7, step]
                dst = part(r.ss, step, r3)
                act(remote(scatter.mine(3, to), dst, sems.at[0], sems.at[1], dict(dp=links.owner(to, links.x, links.c))))

    else:
        sem = pltpu.get_barrier_semaphore()
        pl.semaphore_signal(
            sem, inc=1, device_id=dict(section=1 - sec), device_id_type=pl.DeviceIdType.MESH
        )
        pl.semaphore_wait(sem, 1)
        rows[...] = r.raw_rows[...]
    for c in range(DI // C):
        s = pl.ds(c * C, C)
        rows[0:NS, s] = -jnp.exp(rows[0:NS, s]) * LOG2E

    def forward(k, carry):
        m = k - sec

        @pl.when((m >= 0) & (m < MICRO))
        def _():
            @pl.when(sec == 1)
            def _():
                boundary(RIGHT, m).wait_recv()

            @pl.when(sec == 0)
            def _():
                load(m, 0).wait()

            def gathering(hops):
                if inside:

                    @pl.when((sec == 0) & (m == 0))
                    def _():
                        rest(hops)

            u = of(r.u, m)
            reset = r.reset[m][:, 0:1]
            v = u[...].astype(f32)
            inv = lax.rsqrt(jnp.mean(v * v, axis=-1, keepdims=True) + EPS)
            normed, act, ssm = of(r.normed, m), of(r.act, m), r.gr
            normed[...] = (v * inv * gain[...]).astype(bf16)
            f_x(reset, normed, win, rows, of(r.x, m), act, of(r.dact, m))
            gathering((links.zs - 1,))
            f_rate(
                reset,
                act,
                small,
                rows,
                of(r.proj, m),
                of(r.rin, m),
                of(r.rate, m),
                of(r.drate, m),
                of(r.dec, m),
                r.gs,
                of(r.drive, m),
                r.cols,
                r.diag,
            )
            f_scan(act, rows, of(r.dec, m), r.gs, r.cols, r.diag, r.h.at[m], ssm)
            gathering((links.zs,))
            f_out(u, normed, win, wout, ssm, of(r.sz, m), of(r.dz, m), of(r.gated, m), r.section_out.at[m])

            @pl.when(sec == 0)
            def _():
                boundary(RIGHT, m).start()

            if inside:
                operand(0, m).start()
                operand(1, m).start()

        return carry

    lax.fori_loop(0, MICRO + 1, forward, 0)

    @pl.when(sec == 1)
    def _():
        for m in range(MICRO):
            load(m, 1).wait()

    def owners_rows(g, first, size, zz, value):
        for c in range(2):
            at = pl.ds(pl.multiple_of(first + (c * links.zs + zz) * size, 16), size)
            g[at, :] = value[c * size : (c + 1) * size].astype(g.dtype)

    def products_out():
        if inside:
            for kind in (0, 2):
                for m in range(MICRO):
                    operand(kind, m).wait_recv()
            for zz in range(links.zs):
                s = pl.ds(zz * 4 * r2, 4 * r2)
                full = tn(r.gated[:, s], r.go[...]) + tn(r.xg[:, s], r.xo[...])
                owners_rows(r.gwo, 0, r2, zz, jnp.where(links.x == 0, full[: 2 * r2], full[2 * r2 :]))
        else:
            for c in range(DI // C):
                s = pl.ds(c * C, C)
                r.gwo[s, :] = tn(r.gated[:, s], r.go[...])

    def products_in(zzs):
        if inside:
            for m in range(MICRO):
                if half in zzs:
                    operand(1, m).wait_recv()
                for zz in zzs:
                    operand(3, m, zz).wait_recv()
            for zz in zzs:
                mine = pl.ds(pl.multiple_of((2 * zz + links.x) * strip, 128), strip)
                full = tn(r.gm[:, mine], r.normed[...]) + tn(r.xm[:, pl.ds(zz * strip, strip)], r.xn[...])
                owners_rows(r.gwi, 0, r1, zz, full)
        else:
            for c in range(2 * DI // C):
                s = pl.ds(c * C, C)
                r.gwi[s, :] = tn(r.gm[:, s], r.normed[...])

    def products_head():
        for c in range(DI // C):
            s = pl.ds(c * C, C)
            value = tn(r.act[:, s], r.gp[...]) + tn(r.gpre[:, s], r.rin[...])
            if inside:
                r.head[s, :] = value
            else:
                r.gws[s, :] = value

    def products_small():
        sm, gg = r.sm[0:32, :], r.gg[...]
        for i in range(n):
            z, x, c = i // 4, (i // 2) % 2, i % 2
            to = ((x * 2 + c) * links.zs + z) * r3
            r.gws[pl.ds(to, r2), :] = r.head[pl.ds(i * r2, r2), :].astype(bf16)
            top = pltpu.roll(sm, -i * r2 % DI, 1)[:, 0:128]
            g = pltpu.roll(gg, -i * gw % D, 1)[:, 0:128]
            top = jnp.where(iota((32, 128), 0) == 23, jnp.broadcast_to(g, (32, 128)), top)
            r.gws[pl.ds(to + r2, 32), :] = top.astype(bf16)

    if inside:
        low, high = range(half), range(half, links.zs)
        end = (links.z == 0) | (links.z == links.zs - 1)

        def first_products():
            products_out()
            scatter.start(0)

        def second_products():
            scatter.core(0)
            products_in(high)
            scatter.start(1)

            @pl.when(end)
            def _():
                scatter.line(0)

        def fourth_step():
            products_small()
            small_across().start()
            scatter.core(1)

            @pl.when(end)
            def _():
                scatter.line(1)

    def backward(k, carry):
        m = k - (1 - sec)

        @pl.when((m >= 0) & (m < MICRO))
        def _():
            @pl.when(sec == 0)
            def _():
                boundary(LEFT, m).wait_recv()

            first = m == 0
            reset = r.reset[m][:, 0:1]
            go, gm, sm = of(r.go, m), of(r.gm, m), r.sm
            act, dec = of(r.act, m), of(r.dec, m)
            gs, gd, gr, gb, gc = r.gs, dec, r.gr, r.gb, r.gc

            def early(step):
                @pl.when((m == MICRO - 1) & (sec == 0))
                def _():
                    step()

            if inside:
                operand(2, m).start()
            b_gate(first, go, wout, of(r.sz, m), of(r.dz, m), act, gs, gm, sm)
            if inside:
                for zz in high:
                    operand(3, m, zz).start()
            b_prep(of(r.proj, m), r.cols, r.diag)
            b_scan(
                (lambda: early(first_products)) if inside else None,
                first, gs, rows, dec, r.cols, r.diag, of(r.drive, m), r.h.at[m], r.adj, gd, gr, gb, gc, sm
            )
            if inside:
                early(second_products)
            b_pre(first, act, of(r.drate, m), small, gd, gr, gb, gc, of(r.gpre, m), of(r.gp, m), sm)
            b_conv(first, reset, rows, small, of(r.x, m), of(r.dact, m), gs, gd, of(r.rate, m), of(r.gp, m), gm, sm)
            if inside:
                for zz in low:
                    operand(3, m, zz).start()
                early(products_head)
            sg = r.section_grad.at[m]
            b_in(first, of(r.u, m), go, gain, win, gm, sg, r.gg)

            @pl.when(sec == 1)
            def _():
                of(r.back, m)[...] = sg[...].astype(bf16)
                boundary(LEFT, m).start()

            if inside:
                early(fourth_step)

        return carry

    lax.fori_loop(0, MICRO + 1, backward, 0)
    if inside:

        @pl.when(sec == 1)
        def _():
            first_products()
            second_products()
            products_head()
            fourth_step()

        @pl.when(jnp.logical_not(end))
        def _():
            scatter.line(0)

        products_in(low)
        scatter.start(2)
        small_across().wait_recv()
        add_rows(part(r.gws, links.x, half_rows * r3), r.xs)
        scatter.start(3)

        @pl.when(jnp.logical_not(end))
        def _():
            scatter.line(1)

        scatter.core(2)

        @pl.when(end)
        def _():
            scatter.line(2)

        scatter.core(3)
        small_direct(lambda copy: copy.start())

        @pl.when(jnp.logical_not(end))
        def _():
            scatter.line(2)

        small_direct(lambda copy: copy.wait_recv())
        total_small = scatter.mine(3, links.z)[...].astype(f32)
        for step in range(1, links.zs):
            total_small = total_small + part(r.ss, step, r3)[...].astype(f32)
        r.gsmall_shard[...] = total_small
        for p in range(3):
            scatter.own(p)
        for p in range(3):
            scatter.finish(p)
        scatter.copy(3, CORE).wait_send()
        small_direct(lambda copy: copy.wait_send())
        for p in range(len(gather.pieces)):
            gather.finish(p)
        for m in range(MICRO):
            for kind in range(3):
                operand(kind, m).wait_send()
            for zz in range(links.zs):
                operand(3, m, zz).wait_send()
        small_across().wait_send()
    else:
        products_out()
        products_in(None)
        products_head()

    for m in range(MICRO):

        @pl.when(sec == 0)
        def _():
            boundary(RIGHT, m).wait_send()

        @pl.when(sec == 1)
        def _():
            boundary(LEFT, m).wait_send()


def call(n, inside, arrays):
    r1, r2, zs = 2 * DI // n, DI // n, n // 4
    rows2 = MICRO * T
    outs = dict(
        section_out=((MICRO, T, D), bf16),
        section_grad=((MICRO, T, D), f32),
    )
    scratch = dict(
        reset=((MICRO, T, 128), f32),
        u=((rows2, D), bf16),
        go=((rows2, D), bf16),
        back=((rows2, D), bf16),
        normed=((rows2, D), bf16),
        x=((rows2, DI), f32),
        dact=((rows2, DI), f32),
        sz=((rows2, DI), f32),
        dz=((rows2, DI), f32),
        rate=((rows2, DI), f32),
        drate=((rows2, DI), f32),
        act=((rows2, DI), bf16),
        gated=((rows2, DI), bf16),
        gpre=((rows2, DI), bf16),
        gm=((rows2, 2 * DI), bf16),
        proj=((rows2, 128), f32),
        rin=((rows2, 128), bf16),
        gp=((rows2, 128), bf16),
        h=((MICRO, (T + 1) * NS, DI), bf16),
        adj=((T * NS, CS), bf16),
        dec=((rows2, DI), f32),
        gs=((T, DI), f32),
        gr=((T, DI), f32),
        gb=((T, NS * TB), f32),
        gc=((T, NS * TB), bf16),
        drive=((rows2, DI), bf16),
        cols=((T * NS, 128), f32),
        diag=((T, NS * TB), bf16),
        rows=((32, DI), f32),
    )
    sems = dict(edge=(2, 2, MICRO), loads=(MICRO,))
    if inside:
        outs |= dict(
            gin_shard=((r1, D), f32),
            gout_shard=((r2, D), f32),
            gsmall_shard=((r2 + 32, 128), f32),
        )
        scratch |= dict(
            sm=((32, DI), f32),
            gain=((1, D), f32),
            gg=((1, D), f32),
            win=((2 * DI, D), bf16),
            wout=((DI, D), bf16),
            small=((DI, 128), bf16),
            tails=((32 * n, 128), bf16),
            gwi=((DI, D), bf16),
            gwo=((DI // 2, D), bf16),
            gws=((n * (r2 + 32), 128), bf16),
            head=((DI, 128), f32),
            xg=((rows2, DI), bf16),
            xn=((rows2, D), bf16),
            xo=((rows2, D), bf16),
            xm=((rows2, DI), bf16),
            ci=((zs * r1, D), bf16),
            co=((zs * r2, D), bf16),
            cs=((zs * (r2 + 32), 128), bf16),
            xs=((2 * zs * (r2 + 32), 128), bf16),
            ss=((zs * (r2 + 32), 128), bf16),
            ui=((zs * r1, D), bf16),
            uo=((zs * r2, D), bf16),
            di=((zs * r1, D), bf16),
            do=((zs * r2, D), bf16),
        )
        sems |= dict(
            ag_line=(5, 3, zs),
            ag_core=(5, 2 * zs),
            ag_recv=(5, n),
            rs_core=(4, 2),
            rs_line=(3, 4, zs),
            xs_sems=(8, max(MICRO, zs), 2),
        )
    else:
        outs |= dict(
            gwi=((2 * DI, D), f32),
            gwo=((DI, D), f32),
            gws=((DI, 128), f32),
            gg=((1, D), f32),
            sm=((32, DI), f32),
        )
    names = list(arrays) + list(outs) + list(scratch) + list(sems)
    whole = pl.BlockSpec(memory_space=pltpu.VMEM)
    far = pl.BlockSpec(memory_space=pl.ANY)
    results = pl.pallas_call(
        functools.partial(block, names, inside, n),
        out_shape=[jax.ShapeDtypeStruct(*spec) for spec in outs.values()],
        in_specs=[far] * 2 + [whole] * (len(arrays) - 2),
        out_specs=[whole] * len(outs),
        scratch_shapes=[pltpu.VMEM(*spec) for spec in scratch.values()]
        + [pltpu.SemaphoreType.DMA(shape) for shape in sems.values()],
        compiler_params=pltpu.CompilerParams(
            collective_id=0, has_side_effects=True, vmem_limit_bytes=63 * 2**20
        ),
        name="two_layer_block",
    )(*arrays.values())
    return types.SimpleNamespace(**dict(zip(outs, results)))


def unpack(
    out, grad, gin, gout, gsmall, out_o, grad_o, gain_o, in_o, cw_o, cb_o, x_o, dt_o, db_o, a_o, ds_o, po_o
):
    r2, gw = cb_o.shape[1], gain_o.shape[1]
    out_o[0] = out[...]
    grad_o[0] = grad[...]
    po_o[0] = gout[...]
    in_o[...] = gin[...]
    tail = gsmall[pl.ds(r2, 32), :]
    gain_o[...] = tail[23:24, 0:gw]
    cw_o[0] = tail[NS : NS + KC, 0:r2]
    cb_o[...] = tail[20:21, 0:r2]
    db_o[...] = tail[21:22, 0:r2]
    ds_o[...] = tail[22:23, 0:r2]
    a_o[...] = tail[0:NS, 0:r2]
    small = gsmall[pl.ds(0, r2), :].T
    x_o[...] = small[0 : RK + 2 * NS, :]
    dt_o[0] = small[RK + 2 * NS : 128, :]


def on_device(inputs, cotangent, markers, *weights):
    (
        norm_gain,
        in_proj,
        conv_weight,
        conv_bias,
        x_proj,
        dt_proj,
        dt_bias,
        a_log,
        d_skip,
        out_proj,
    ) = weights
    n = lax.axis_size(DP)
    inside = n == 16
    arrays = dict(inputs=inputs, cotangent=cotangent, markers=markers)
    if inside:
        arrays |= dict(
            norm_gain=norm_gain,
            in_proj=in_proj[0].T,
            conv_weight=conv_weight,
            conv_bias=conv_bias,
            x_proj=x_proj[0].T,
            dt_proj=dt_proj,
            dt_bias=dt_bias,
            a_log=a_log[0].T,
            d_skip=d_skip,
            out_proj=out_proj,
        )
        res = call(n, inside, arrays)
        whole = pl.BlockSpec(memory_space=pltpu.VMEM)
        turned = (in_proj, x_proj, a_log)
        shapes = [((1,) + res.section_out.shape, bf16), ((1,) + res.section_grad.shape, f32)]
        shapes += [(w.shape[:0:-1] if any(w is t for t in turned) else w.shape, f32) for w in weights]
        done = pl.pallas_call(
            unpack,
            out_shape=[jax.ShapeDtypeStruct(*spec) for spec in shapes],
            in_specs=[whole] * 5,
            out_specs=[whole] * 12,
            name="unpack",
        )(
            res.section_out,
            res.section_grad,
            res.gin_shard,
            res.gout_shard,
            res.gsmall_shard,
        )
        grads = (g.T[None] if any(w is t for t in turned) else g for w, g in zip(weights, done[2:]))
        return (*done[:2], *grads)

    def gathered(value, axis):
        return lax.all_gather(value.astype(bf16), DP, axis=axis, tiled=True)

    r2 = DI // n
    raw = jnp.concatenate(
        [a_log[0].T, conv_weight[0], conv_bias, dt_bias, d_skip, jnp.zeros((9, r2), f32)], axis=0
    )
    arrays |= dict(
        win=gathered(in_proj[0].T, 0),
        wout=gathered(out_proj[0], 0),
        small=gathered(jnp.concatenate([x_proj[0], dt_proj[0].T], axis=1), 0),
        raw_rows=gathered(raw, 1).astype(f32),
        gain=gathered(norm_gain, 1).astype(f32),
    )
    res = call(n, inside, arrays)

    def scattered(value, axis):
        return lax.psum_scatter(value, DP, scatter_dimension=axis, tiled=True)

    gin, gout, gsmall = scattered(res.gwi, 0), scattered(res.gwo, 0), scattered(res.gws, 0)
    rows = scattered(res.sm, 1)
    return (
        res.section_out[None],
        res.section_grad[None],
        scattered(res.gg, 1),
        gin.T[None],
        rows[NS : NS + KC][None],
        rows[20:21],
        gsmall[:, 0 : RK + 2 * NS][None],
        gsmall[:, RK + 2 * NS : 128].T[None],
        rows[21:22],
        rows[0:NS].T[None],
        rows[22:23],
        gout[None],
    )


def solution(mesh):
    tokens = P(None, DP, None)
    columns = P(SECTION, None, DP)
    channels = P(SECTION, DP)
    rows = P(SECTION, DP, None)
    kept = P(SECTION, None, DP, None)
    weights = (
        channels,
        columns,
        columns,
        channels,
        rows,
        columns,
        channels,
        rows,
        channels,
        rows,
    )
    return jax.shard_map(
        on_device,
        mesh=mesh,
        in_specs=(tokens, tokens, P(None, DP)) + weights,
        out_specs=(kept, kept) + weights,
        check_vma=False,
    )
```

```python
import functools
import types

import jax
import jax.numpy as jnp
from jax import lax
from jax.experimental import pallas as pl
from jax.experimental.pallas import tpu as pltpu
from jax.sharding import PartitionSpec as P

T = 128
D = 768
DI = 1536
NS = 16
KC = 4
RK = 48
MICRO = 2
C = 512
CS = 768
TB = 16
NB = T // TB
EPS = 1e-5
LOG2E = 1.4426950408889634
LN2 = 0.6931471805599453
BIG = 1e30
DP, SECTION = "dp", "section"
UP, DOWN, ACROSS, CORE = range(4)
BELOW, ABOVE = range(2)
START, FINISH = range(2)
RIGHT, LEFT = range(2)
f32 = jnp.float32
bf16 = jnp.bfloat16


def nn(a, b):
    return lax.dot_general(a, b, (((1,), (0,)), ((), ())), preferred_element_type=f32)


def nt(a, b):
    return lax.dot_general(a, b, (((1,), (1,)), ((), ())), preferred_element_type=f32)


def tn(a, b):
    return lax.dot_general(a, b, (((0,), (0,)), ((), ())), preferred_element_type=f32)


def iota(shape, axis):
    return lax.broadcasted_iota(jnp.int32, shape, axis)


def sigmoid(v):
    return 1.0 / (1.0 + jnp.exp(-v))


def wide(v):
    return jnp.concatenate([v] * (CS // 128), axis=1)


def keeps(reset):
    keep = [None]
    cur = jnp.ones_like(reset)
    for k in range(1, KC):
        cur = cur * (1.0 - (reset if k == 1 else pltpu.roll(reset, k - 1, 0)))
        keep.append(cur)
    return keep


def block_diagonal(cols):
    tile = (iota((NS, NS * TB), 1) % NS == iota((NS, NS * TB), 0)).astype(bf16)
    rep = nn(cols.astype(bf16), tile)
    own = (iota((T, NS * TB), 1) // NS) == (iota((T, NS * TB), 0) % TB)
    return jnp.where(own, rep, 0.0).astype(bf16)


def lane_columns(dst, val):
    for t in range(T):
        dst[pl.ds(t * NS, NS), :] = jnp.broadcast_to(val[:, t : t + 1], (NS, 128))


def f_x(reset, normed, win, rows, x_ref, act, dact):
    keep = keeps(reset)
    for c in range(DI // C):
        s = pl.ds(c * C, C)
        x = nt(normed[...], win[s, :])
        x_ref[:, s] = x
        v = rows[20:21, s] + rows[16:17, s] * x
        for k in range(1, KC):
            v = v + rows[16 + k : 17 + k, s] * (pltpu.roll(x, k, 0) * keep[k])
        sg = sigmoid(v)
        act[:, s] = (v * sg).astype(bf16)
        dact[:, s] = sg * (1.0 + v * (1.0 - sg))


def f_rate(reset, act, small, rows, proj, rin, rate_ref, drate, dec, drive, drive_low, cols, diag):
    p = nn(act[...], small[:, 0:128])
    proj[...] = p
    lane_columns(cols, p.T[RK : RK + NS, :])
    diag[...] = block_diagonal(p[:, RK + NS : RK + 2 * NS])
    rin[...] = pltpu.roll(jnp.where(iota((T, 128), 1) < RK, p, 0.0), RK + 2 * NS, 1).astype(bf16)
    for c in range(DI // C):
        s = pl.ds(c * C, C)
        pre = nt(rin[...], small[s, 0:128]) + rows[21:22, s]
        e = jnp.exp(-jnp.abs(pre))
        rate = jnp.maximum(pre, 0.0) + jnp.log1p(e)
        rate_ref[:, s] = rate
        drate[:, s] = jnp.where(pre >= 0.0, 1.0, e) / (1.0 + e)
        dec[:, s] = jnp.where(reset > 0.0, BIG, rate)
        both = rate * act[:, s].astype(f32)
        drive[:, s] = both
        drive_low[:, s] = both.astype(bf16)


def f_scan(act, rows, dec, drive, cols, diag, h_ref, ssm):
    h_ref[0:NS, :] = jnp.zeros((NS, DI), bf16)
    for c in range(DI // CS):
        s = pl.ds(c * CS, CS)

        def block(i, h):
            t0 = pl.multiple_of(i * TB, TB)
            a2 = rows[0:NS, s]
            d = dec[pl.ds(t0, TB), s]
            v = drive[pl.ds(t0, TB), s]
            for j in range(TB):
                b = wide(cols[pl.ds(t0 * NS + j * NS, NS), :])
                h = jnp.exp2(d[j : j + 1, :] * a2) * h + v[j : j + 1, :] * b
                h_ref[pl.ds(t0 * NS + (j + 1) * NS, NS), s] = h.astype(bf16)
            return h

        lax.fori_loop(0, NB, block, jnp.zeros((NS, CS), f32))

    def sums(i, carry):
        for q in range(4):
            t0 = pl.multiple_of(i * (4 * TB) + q * TB, TB)
            tt = pl.ds(t0, TB)
            y = nn(diag[tt, :], h_ref[pl.ds(t0 * NS + NS, TB * NS), :])
            ssm[tt, :] = y + rows[22:23, :] * act[tt, :].astype(f32)
        return carry

    lax.fori_loop(0, NB // 4, sums, 0)


def f_out(u, normed, win, wout, ssm, sz_ref, dz_ref, gated, out):
    acc = u[...].astype(f32)
    for c in range(DI // C):
        s = pl.ds(c * C, C)
        z = nt(normed[...], win[pl.ds(DI + c * C, C), :])
        sg = sigmoid(z)
        sz = z * sg
        sz_ref[:, s] = sz
        dz_ref[:, s] = ssm[:, s] * (sg * (1.0 + z * (1.0 - sg)))
        g = (ssm[:, s] * sz).astype(bf16)
        gated[:, s] = g
        acc = acc + nn(g, wout[s, :])
    out[...] = acc.astype(bf16)


def total(old, first, value):
    return jnp.where(first, value, old + value)


def b_gate(first, go_ref, wout, sz, dz, act, gs_ref, gm, sm):
    go = go_ref[...]
    for c in range(DI // C):
        s = pl.ds(c * C, C)
        gg = nt(go, wout[s, :])
        gs = gg * sz[:, s]
        gs_ref[:, s] = gs
        gm[:, pl.ds(DI + c * C, C)] = (gg * dz[:, s]).astype(bf16)
        part = jnp.sum(gs * act[:, s].astype(f32), axis=0, keepdims=True)
        sm[22:23, s] = total(sm[22:23, s], first, part)


def b_prep(proj, cols, diag):
    p = proj[...]
    lane_columns(cols, p.T[RK + NS : RK + 2 * NS, :])
    diag[...] = block_diagonal(p[:, RK : RK + NS])


def b_scan(between, first, gs, rows, dec, cols, diag, drive, h_ref, adj_ref, gd, gr, gb, gc, sm):
    ones = (iota((TB, TB * NS), 1) // NS) == iota((TB, TB * NS), 0)
    od = ones.astype(bf16)

    def state_sums(i, carry):
        for q in range(4):
            t0 = pl.multiple_of(i * (4 * TB) + q * TB, TB)
            tt = pl.ds(t0, TB)
            full = nt(gs[tt, :].astype(bf16), h_ref[pl.ds(t0 * NS + NS, TB * NS), :])
            gc[tt, :] = jnp.where(ones, full, 0.0).astype(bf16)
        return carry

    lax.fori_loop(0, NB // 4, state_sums, 0)
    for c in range(DI // CS):
        s = pl.ds(c * CS, CS)

        def block(i, state):
            carry, acc = state
            t0 = pl.multiple_of((NB - 1 - i) * TB, TB)
            a2 = rows[0:NS, s]
            d = dec[pl.ds(t0, TB), s]
            g = gs[pl.ds(t0, TB), s]
            for j in reversed(range(TB)):
                row = pl.ds(t0 * NS + j * NS, NS)
                adj = g[j : j + 1, :] * wide(cols[row, :]) + carry
                adj_ref[row, :] = adj.astype(bf16)
                dj = d[j : j + 1, :]
                carry = jnp.exp2(dj * a2) * adj
                expo = carry * h_ref[row, s].astype(f32)
                h_ref[row, s] = (expo * a2).astype(bf16)
                acc = acc + expo * dj
            return carry, acc

        zero = jnp.zeros((NS, CS), f32)
        _, acc = lax.fori_loop(0, NB, block, (zero, zero))
        sm[0:NS, s] = total(sm[0:NS, s], first, acc * rows[0:NS, s] * LN2)

        def adjoint_sums(i, carry):
            for q in range(4):
                t0 = pl.multiple_of(i * (4 * TB) + q * TB, TB)
                tt = pl.ds(t0, TB)
                row = pl.ds(t0 * NS, TB * NS)
                gd[tt, s] = nn(diag[tt, :], adj_ref[row, :])
                gr[tt, s] = nn(od, h_ref[row, s]) * LN2
                full = nt(drive[tt, s], adj_ref[row, :])
                gb[tt, :] = full if c == 0 else gb[tt, :] + full
            return carry

        lax.fori_loop(0, NB // 4, adjoint_sums, 0)
        if c == 0 and between is not None:
            between()


def b_pre(first, act, drate, small, gd, gr, gb, gc, gpre, gp, sm):
    acc = jnp.zeros((T, 128), f32)
    for c in range(DI // C):
        s = pl.ds(c * C, C)
        g = ((gr[:, s] + gd[:, s] * act[:, s].astype(f32)) * drate[:, s]).astype(bf16)
        gpre[:, s] = g
        part = jnp.sum(g.astype(f32), axis=0, keepdims=True)
        sm[21:22, s] = total(sm[21:22, s], first, part)
        acc = acc + nn(g, small[s, 0:128])
    k = iota((TB * NS, 128), 0) % NS
    lane = iota((TB * NS, 128), 1)
    own = (iota((T, NS * TB), 1) // NS) == (iota((T, NS * TB), 0) % TB)
    gb_own = jnp.where(own, gb[...], 0.0).astype(bf16)
    bc = nn(gb_own, (lane == RK + k).astype(bf16)) + nn(gc[...], (lane == RK + NS + k).astype(bf16))
    gp[...] = jnp.where(iota((T, 128), 1) < RK, pltpu.roll(acc, RK, 1), bc).astype(bf16)


def b_conv(first, reset, rows, small, x_ref, dact, gs, gd, rate, gp, gm, sm):
    keep = keeps(reset)
    for c in range(DI // C):
        s = pl.ds(c * C, C)
        ga = gs[:, s] * rows[22:23, s] + gd[:, s] * rate[:, s] + nt(gp[...], small[s, 0:128])
        gc = ga * dact[:, s]
        x = x_ref[:, s]
        part = jnp.sum(gc, axis=0, keepdims=True)
        sm[20:21, s] = total(sm[20:21, s], first, part)
        gx = jnp.zeros((T, C), f32)
        for k in range(KC):
            ahead = pltpu.roll(gc * keep[k], T - k, 0) if k else gc
            part = jnp.sum(ahead * x, axis=0, keepdims=True)
            sm[16 + k : 17 + k, s] = total(sm[16 + k : 17 + k, s], first, part)
            gx = gx + ahead * rows[16 + k : 17 + k, s]
        gm[:, s] = gx.astype(bf16)


def b_in(first, u_ref, go_ref, gain, win, gm, sg, gg):
    gn = jnp.zeros((T, D), f32)
    for c in range(2 * DI // C):
        s = pl.ds(c * C, C)
        gn = gn + nn(gm[:, s], win[s, :])
    u = u_ref[...].astype(f32)
    inv = lax.rsqrt(jnp.mean(u * u, axis=-1, keepdims=True) + EPS)
    g = gn * gain[...]
    gg[...] = total(gg[...], first, jnp.sum(gn * u * inv, axis=0, keepdims=True))
    mean = jnp.mean(g * u, axis=-1, keepdims=True)
    sg[...] = go_ref[...].astype(f32) + inv * g - u * (inv * inv * inv) * mean


class Links:
    def __init__(self, n):
        self.zs = n // 4
        i = lax.axis_index(DP)
        self.i = i
        self.c = i % 2
        self.x = (i // 2) % 2
        self.z = i // 4

    def owner(self, z, x, c):
        return 4 * z + 2 * x + c

    def dev(self, route):
        step = (4, -4, 2 - 4 * self.x, 1 - 2 * self.c)[route]
        return dict(dp=self.i + step)

    def greet(self):
        sem = pltpu.get_barrier_semaphore()

        def tell(device):
            pl.semaphore_signal(sem, inc=1, device_id=device, device_id_type=pl.DeviceIdType.MESH)

        tell(self.dev(ACROSS))
        tell(self.dev(CORE))
        tell(dict(section=1 - lax.axis_index(SECTION)))

        @pl.when(self.z < self.zs - 1)
        def _():
            tell(self.dev(UP))

        @pl.when(self.z > 0)
        def _():
            tell(self.dev(DOWN))

    def meet(self):
        ends = jnp.where(self.z < self.zs - 1, 1, 0) + jnp.where(self.z > 0, 1, 0)
        pl.semaphore_wait(pltpu.get_barrier_semaphore(), 3 + ends)


def part(ref, index, count, first=0, rows=None):
    return ref.at[pl.ds(pl.multiple_of(index * count + first, 16), rows or count), :]


def remote(src, dst, send, recv, device):
    return pltpu.make_async_remote_copy(
        src_ref=src,
        dst_ref=dst,
        send_sem=send,
        recv_sem=recv,
        device_id=device,
        device_id_type=pl.DeviceIdType.MESH,
    )


class Gather:
    def __init__(self, links, pieces, balanced, line_send, core_send, recv):
        self.k, self.pieces, self.balanced = links, pieces, balanced
        self.line_send, self.core_send, self.recv = line_send, core_send, recv

    def copy(self, p, z, x, c, route, slot=None):
        whole, count = self.pieces[p][:2]
        ref = part(whole, self.k.owner(z, x, c), count)
        if route == CORE:
            send = self.core_send.at[p, 2 * z + x]
        else:
            send = self.line_send.at[p, route if slot is None else slot, z]
        return remote(ref, ref, send, self.recv.at[p, self.k.owner(z, x, c)], self.k.dev(route))

    def each(self, p, side, r, act):
        k = self.k
        lo, hi = self.pieces[p][2:]
        z = k.z - r if side == BELOW else k.z + r

        @pl.when((z >= lo) & (z < hi))
        def _():
            act(z)

    def line(self, p, r):
        def pass_on(z, side):
            k = self.k
            self.copy(p, z, k.x, k.c, ACROSS).wait_recv()
            self.go(p, z, side, START)

        for side in (BELOW, ABOVE):
            self.each(p, side, r, functools.partial(pass_on, side=side))

    def go(self, p, z, side, do):
        k = self.k

        def one(route):
            copy = self.copy(p, z, k.x, k.c, route)
            copy.wait_send() if do == FINISH else copy.start()

        @pl.when(jnp.logical_not(self.by_line(p, z)))
        def _():
            one(ACROSS)

        if side != ABOVE:

            @pl.when(k.z < k.zs - 1)
            def _():
                one(UP)

        if side != BELOW:

            @pl.when(k.z > 0)
            def _():
                one(DOWN)

        one(CORE)

    def by_line(self, p, z):
        k = self.k
        last = k.zs - 1
        near = ((k.z == 1) & (z == 0)) | ((k.z == last - 1) & (z == last))
        if p not in self.balanced:
            return near
        return near | ((k.z == 0) & (z == last)) | ((k.z == last) & (z == 0))

    def relay(self, p, z, do):
        k = self.k
        last = k.zs - 1
        far = int(p in self.balanced)

        def one(route):
            copy = self.copy(p, z, 1 - k.x, k.c, route, 3)
            copy.wait_send() if do == FINISH else copy.start()

        @pl.when(((k.z == 0) & (z == 0)) | ((k.z == last - 1) & (z == 0) & (far == 1)))
        def _():
            one(UP)

        @pl.when(((k.z == last) & (z == last)) | ((k.z == 1) & (z == last) & (far == 1)))
        def _():
            one(DOWN)

    def start(self, p):
        self.each(p, BELOW, 0, lambda z: self.go(p, z, None, START))

    def across(self, p, r):
        def pass_on(z):
            copy = self.copy(p, z, 1 - self.k.x, self.k.c, CORE)
            copy.wait_recv()
            self.relay(p, z, START)
            copy.start()

        self.each(p, BELOW, r, pass_on)
        if r:
            self.each(p, ABOVE, r, pass_on)

    def arrived(self, p):
        for z in range(*self.pieces[p][2:]):
            for x in range(2):
                self.copy(p, z, x, 1 - self.k.c, CORE).wait_recv()

    def finish(self, p):
        k = self.k

        def crossed(z):
            self.copy(p, z, 1 - k.x, k.c, CORE).wait_send()
            self.relay(p, z, FINISH)

        for r in range(k.zs):
            for side in (BELOW, ABOVE) if r else (BELOW,):
                self.each(p, side, r, lambda z, side=side: self.go(p, z, side if r else None, FINISH))
                self.each(p, side, r, crossed)


def add_rows(dst, src):
    count = dst.shape[0]
    step = 48 if count % 48 == 0 else 16

    def add(i, carry):
        s = pl.ds(pl.multiple_of(i * step, 16), step)
        dst[s, :] = (dst[s, :].astype(f32) + src[s, :].astype(f32)).astype(dst.dtype)
        return carry

    lax.fori_loop(0, count // step, add, 0)


class Scatter:
    def __init__(self, links, pieces, subs, core_sems, line_sems):
        self.k, self.pieces, self.subs = links, pieces, subs
        self.core_sems, self.line_sems = core_sems, line_sems

    def rows(self, p, c, z, count=1):
        g, first, _, _, _, _, size, _, _ = self.pieces[p]
        return part(g, 1, first + (c * self.k.zs + z) * size, 0, count * size)

    def mine(self, p, z, sub=None):
        whole = self.rows(p, self.k.c, z)
        return whole if sub is None else self.half(p, whole, sub)

    def half(self, p, ref, sub):
        count = ref.shape[0] // self.subs[p]
        return ref.at[pl.ds(sub * count, count), :]

    def copy(self, p, route, z=None, sub=0):
        k = self.k
        _, _, core, below, above, _, size, lo, hi = self.pieces[p]
        if route == CORE:
            send, recv = self.core_sems.at[p, 0], self.core_sems.at[p, 1]
            src, dst = self.rows(p, 1 - k.c, lo, hi - lo), part(core, 1, lo * size, 0, (hi - lo) * size)
        else:
            at = 4 * sub + 2 * route
            send, recv = self.line_sems.at[p, at, z], self.line_sems.at[p, at + 1, z]
            src, dst = self.mine(p, z, sub), self.half(p, part((below, above)[route], z, size), sub)
        return remote(src, dst, send, recv, k.dev(route))

    def far_first(self, p):
        k = self.k
        lo, hi = self.pieces[p][7:]
        for i in range(hi - lo):
            table = [sorted(range(lo, hi), key=lambda o: (-abs(o - z), o))[i] for z in range(k.zs)]
            z = table[0]
            for at in range(1, k.zs):
                z = jnp.where(k.z == at, table[at], z)
            yield z

    def start(self, p):
        self.copy(p, CORE).start()

    def core(self, p):
        _, _, core, _, _, _, size, lo, hi = self.pieces[p]
        self.copy(p, CORE).wait_recv()
        add_rows(self.rows(p, self.k.c, lo, hi - lo), part(core, 1, lo * size, 0, (hi - lo) * size))

    def line(self, p):
        k = self.k
        _, _, _, below, above, _, size, _, _ = self.pieces[p]
        for z in self.far_first(p):

            def hop(route, inner, source):
                for sub in range(self.subs[p]):

                    @pl.when(inner)
                    def _():
                        self.copy(p, route, z, sub).wait_recv()
                        add_rows(self.mine(p, z, sub), self.half(p, part(source, z, size), sub))

                    self.copy(p, route, z, sub).start()

            @pl.when(z > k.z)
            def _():
                hop(UP, k.z > 0, below)

            @pl.when(z < k.z)
            def _():
                hop(DOWN, k.z < k.zs - 1, above)

    def own(self, p):
        k = self.k
        _, _, _, below, above, result, size, lo, hi = self.pieces[p]

        @pl.when((k.z >= lo) & (k.z < hi))
        def _():
            result[...] = self.mine(p, k.z)[...].astype(f32)
            for sub in range(self.subs[p]):

                def take(route, source):
                    self.copy(p, route, k.z, sub).wait_recv()
                    add_rows(self.half(p, result, sub), self.half(p, part(source, k.z, size), sub))

                @pl.when(k.z > 0)
                def _():
                    take(UP, below)

                @pl.when(k.z < k.zs - 1)
                def _():
                    take(DOWN, above)

    def finish(self, p):
        k = self.k
        self.copy(p, CORE).wait_send()
        for z in range(*self.pieces[p][7:]):
            for sub in range(self.subs[p]):

                @pl.when(z > k.z)
                def _():
                    self.copy(p, UP, z, sub).wait_send()

                @pl.when(z < k.z)
                def _():
                    self.copy(p, DOWN, z, sub).wait_send()


def weight_rows(tails, rows, gain, n):
    r2, gw = DI // n, D // n
    parts = [tails[i * 32 : i * 32 + 32, :].astype(f32) for i in range(n)]
    rows[...] = jnp.concatenate([p[:, 0:r2] for p in parts], axis=1)
    gain[...] = jnp.concatenate([p[23:24, 0:gw] for p in parts], axis=1)


def block(names, inside, n, *refs):
    r = types.SimpleNamespace(**dict(zip(names, refs)))
    sec = lax.axis_index(SECTION)
    links = Links(n)
    r1, r2, gw = 2 * DI // n, DI // n, D // n
    r3 = r2 + 32
    if inside:
        far_in = (r.markers, r.norm_gain, r.in_proj, r.conv_weight, r.conv_bias, r.x_proj)
        far_in += (r.dt_proj, r.dt_bias, r.a_log, r.d_skip, r.out_proj)
        near_in = (r.v_markers, r.v_norm_gain, r.v_in_proj, r.v_conv_weight, r.v_conv_bias, r.v_x_proj)
        near_in += (r.v_dt_proj, r.v_dt_bias, r.v_a_log, r.v_d_skip, r.v_out_proj)
    else:
        far_in = (r.markers, r.all_win, r.all_wout, r.all_small, r.raw_rows, r.all_gain)
        near_in = (r.v_markers, r.win, r.wout, r.small, r.v_raw_rows, r.gain)
    rows, small, gain, win, wout = r.rows, r.small, r.gain, r.win, r.wout

    def of(ref, m):
        return ref.at[pl.ds(pl.multiple_of(m * T, T), T), :]

    def load(m, at):
        src, dst = ((r.inputs, r.u), (r.cotangent, r.go))[at]
        return pltpu.make_async_copy(src.at[m], of(dst, m), r.loads.at[m])

    if inside:
        links.greet()
    fetches = [
        pltpu.make_async_copy(src, dst, r.fetch.at[at])
        for at, (src, dst) in enumerate(zip(far_in, near_in, strict=True))
    ]
    for fetch in fetches:
        fetch.start()
    for at in range(2):

        @pl.when(sec == at)
        def _():
            for m in range(MICRO):
                load(m, at).start()

    r.sm[...] = jnp.zeros_like(r.sm)
    for fetch in fetches:
        fetch.wait()
    starts = jnp.where((r.v_markers[...] > 0) | (iota((MICRO, T), 1) == 0), 1.0, 0.0)
    starts = jnp.concatenate([starts, jnp.zeros((8 - MICRO, T), f32)], axis=0).T
    for m in range(MICRO):
        r.reset[m] = jnp.broadcast_to(starts[:, m : m + 1], (T, 128))
    def keep(m, at):
        src, dst = ((r.v_out, r.section_out), (r.v_grad, r.section_grad))[at]
        return pltpu.make_async_copy(of(src, m), dst.at[m], r.keeps.at[at, m])

    def boundary(route, m):
        if route == RIGHT:
            src, dst, at = of(r.v_out, m), of(r.u, m), 0
        else:
            src, dst, at = of(r.back, m), of(r.go, m), 1
        return remote(src, dst, r.edge.at[at, 0, m], r.edge.at[at, 1, m], dict(section=1 - sec))

    if inside:
        tails = r.tails
        part(win, links.i, r1)[...] = r.v_in_proj[...].astype(bf16)
        part(wout, links.i, r2)[...] = r.v_out_proj[0].astype(bf16)
        head = jnp.concatenate([r.v_x_proj[...], r.v_dt_proj[0]], axis=0).T
        part(small, links.i, r2)[...] = head.astype(bf16)
        top = [r.v_a_log[...], r.v_conv_weight[0], r.v_conv_bias[...], r.v_dt_bias[...], r.v_d_skip[...]]
        top.append(jnp.concatenate([r.v_norm_gain[...], jnp.zeros((1, r2 - gw), f32)], axis=1))
        top = jnp.concatenate(top + [jnp.zeros((8, r2), f32)], axis=0)
        top = jnp.concatenate([top, jnp.zeros((32, 128 - r2), f32)], axis=1)
        part(tails, links.i, 32)[...] = top.astype(bf16)
        links.meet()
        half = links.zs // 2
        pieces = [
            (tails, 32, 0, links.zs),
            (small, r2, 0, links.zs),
            (win, r1, 0, half),
            (win, r1, half, links.zs),
            (wout, r2, 0, links.zs),
        ]
        gather = Gather(links, pieces, (4,), r.ag_line, r.ag_core, r.ag_recv)
        early, late = (0, 1, 2), (3, 4)

        def pass_on(ps, hops):
            for hop in hops:
                for p in ps:
                    if hop < links.zs:
                        gather.line(p, hop)
                for p in ps:
                    gather.across(p, hop - 1)

        for p in early:
            gather.start(p)
        for p in late:
            gather.start(p)
        for p in early:
            gather.line(p, 1)
        for p in late:
            gather.line(p, 1)
        for p in early:
            gather.across(p, 0)
        for p in early:
            gather.line(p, 2)
        for p in late:
            gather.across(p, 0)
        for p in early:
            gather.across(p, 1)
        for p in early:
            gather.line(p, 3)
        for p in late:
            gather.line(p, 2)
        for p in early:
            gather.across(p, 2)
        for p in late:
            gather.across(p, 1)
        for p in early:
            gather.across(p, 3)
        for p in late:
            gather.line(p, 3)
        for p in early:
            gather.arrived(p)

        def rest(hops):
            for hop in hops:
                for p in late:
                    gather.across(p, hop - 1)
            if links.zs in hops:
                for p in late:
                    gather.arrived(p)

        @pl.when(sec == 1)
        def _():
            rest((links.zs - 1, links.zs))

        weight_rows(tails, rows, gain, n)
        half_rows = 2 * links.zs
        pieces = [
            (r.gwo, 0, r.co, r.uo, r.do, r.v_gout, r2, 0, links.zs),
            (r.gwi, 0, r.ci, r.ui, r.di, r.v_gin, r1, half, links.zs),
            (r.gwi, 0, r.ci, r.ui, r.di, r.v_gin, r1, 0, half),
            (r.gws, links.x * half_rows * r3, r.cs, None, None, None, r3, 0, links.zs),
        ]
        scatter = Scatter(links, pieces, (1, 2, 2, 1), r.rs_core, r.rs_line)
        strip = 2 * r1

        def operand(kind, m, zz=0):
            src = of((r.gated, r.normed, r.go, r.gm)[kind], m)
            dst = of((r.xg, r.xn, r.xo, r.xm)[kind], m)
            if kind == 3:
                at = pl.multiple_of((2 * zz + 1 - links.x) * strip, 128)
                src, dst = src.at[:, pl.ds(at, strip)], dst.at[:, pl.ds(zz * strip, strip)]
            sems = r.xs_sems.at[kind + zz, m]
            return remote(src, dst, sems.at[0], sems.at[1], links.dev(ACROSS))

        def small_across():
            sems = r.xs_sems.at[7, 0]
            src = part(r.gws, 1 - links.x, half_rows * r3)
            return remote(src, r.xs, sems.at[0], sems.at[1], links.dev(ACROSS))

        def small_direct(act):
            for step in range(1, links.zs):
                to = (links.z + step) % links.zs
                sems = r.xs_sems.at[7, step]
                dst = part(r.ss, step, r3)
                act(remote(scatter.mine(3, to), dst, sems.at[0], sems.at[1], dict(dp=links.owner(to, links.x, links.c))))

    else:
        sem = pltpu.get_barrier_semaphore()
        pl.semaphore_signal(
            sem, inc=1, device_id=dict(section=1 - sec), device_id_type=pl.DeviceIdType.MESH
        )
        pl.semaphore_wait(sem, 1)
        rows[...] = r.v_raw_rows[...]
    for c in range(DI // C):
        s = pl.ds(c * C, C)
        rows[0:NS, s] = -jnp.exp(rows[0:NS, s]) * LOG2E

    def forward(k, carry):
        m = k - sec

        @pl.when((m >= 0) & (m < MICRO))
        def _():
            @pl.when(sec == 1)
            def _():
                boundary(RIGHT, m).wait_recv()

            @pl.when(sec == 0)
            def _():
                load(m, 0).wait()

            def gathering(hops):
                if inside:

                    @pl.when((sec == 0) & (m == 0))
                    def _():
                        rest(hops)

            u = of(r.u, m)
            reset = r.reset[m][:, 0:1]
            v = u[...].astype(f32)
            inv = lax.rsqrt(jnp.mean(v * v, axis=-1, keepdims=True) + EPS)
            normed, act, ssm = of(r.normed, m), of(r.act, m), r.gr
            normed[...] = (v * inv * gain[...]).astype(bf16)
            f_x(reset, normed, win, rows, of(r.x, m), act, of(r.dact, m))
            gathering((links.zs - 1,))
            f_rate(
                reset,
                act,
                small,
                rows,
                of(r.proj, m),
                of(r.rin, m),
                of(r.rate, m),
                of(r.drate, m),
                of(r.dec, m),
                r.gs,
                of(r.drive, m),
                r.cols,
                r.diag,
            )
            f_scan(act, rows, of(r.dec, m), r.gs, r.cols, r.diag, r.h.at[m], ssm)
            gathering((links.zs,))
            f_out(u, normed, win, wout, ssm, of(r.sz, m), of(r.dz, m), of(r.gated, m), of(r.v_out, m))

            @pl.when(sec == 0)
            def _():
                boundary(RIGHT, m).start()

            keep(m, 0).start()
            if inside:
                operand(0, m).start()
                operand(1, m).start()

        return carry

    lax.fori_loop(0, MICRO + 1, forward, 0)

    @pl.when(sec == 1)
    def _():
        for m in range(MICRO):
            load(m, 1).wait()

    def owners_rows(g, first, size, zz, value):
        for c in range(2):
            at = pl.ds(pl.multiple_of(first + (c * links.zs + zz) * size, 16), size)
            g[at, :] = value[c * size : (c + 1) * size].astype(g.dtype)

    def products_out():
        if inside:
            for kind in (0, 2):
                for m in range(MICRO):
                    operand(kind, m).wait_recv()
            def mine(ref, zz):
                at = zz * 4 * r2
                return jnp.where(links.x == 0, ref[:, at : at + 2 * r2], ref[:, at + 2 * r2 : at + 4 * r2])

            for zz in range(links.zs):
                value = tn(mine(r.gated, zz), r.go[...]) + tn(mine(r.xg, zz), r.xo[...])
                owners_rows(r.gwo, 0, r2, zz, value)
        else:
            for c in range(DI // C):
                s = pl.ds(c * C, C)
                r.gwo[s, :] = tn(r.gated[:, s], r.go[...])

    def products_in(zzs):
        if inside:
            for m in range(MICRO):
                if half in zzs:
                    operand(1, m).wait_recv()
                for zz in zzs:
                    operand(3, m, zz).wait_recv()
            for zz in zzs:
                mine = pl.ds(pl.multiple_of((2 * zz + links.x) * strip, 128), strip)
                full = tn(r.gm[:, mine], r.normed[...]) + tn(r.xm[:, pl.ds(zz * strip, strip)], r.xn[...])
                owners_rows(r.gwi, 0, r1, zz, full)
        else:
            for c in range(2 * DI // C):
                s = pl.ds(c * C, C)
                r.gwi[s, :] = tn(r.gm[:, s], r.normed[...])

    def products_head():
        for c in range(DI // C):
            s = pl.ds(c * C, C)
            value = tn(r.act[:, s], r.gp[...]) + tn(r.gpre[:, s], r.rin[...])
            if inside:
                r.head[s, :] = value
            else:
                r.gws[s, :] = value

    def products_small():
        sm, gg = r.sm[0:32, :], r.gg[...]
        for i in range(n):
            z, x, c = i // 4, (i // 2) % 2, i % 2
            to = ((x * 2 + c) * links.zs + z) * r3
            r.gws[pl.ds(to, r2), :] = r.head[pl.ds(i * r2, r2), :].astype(bf16)
            top = pltpu.roll(sm, -i * r2 % DI, 1)[:, 0:128]
            g = pltpu.roll(gg, -i * gw % D, 1)[:, 0:128]
            top = jnp.where(iota((32, 128), 0) == 23, jnp.broadcast_to(g, (32, 128)), top)
            r.gws[pl.ds(to + r2, 32), :] = top.astype(bf16)

    if inside:
        low, high = range(half), range(half, links.zs)
        end = (links.z == 0) | (links.z == links.zs - 1)

        def first_products():
            products_out()
            scatter.start(0)

        def second_products():
            scatter.core(0)
            products_in(high)
            scatter.start(1)

            @pl.when(end)
            def _():
                scatter.line(0)

        def fourth_step():
            products_small()
            small_across().start()
            scatter.core(1)

            @pl.when(end)
            def _():
                scatter.line(1)

    def backward(k, carry):
        m = k - (1 - sec)

        @pl.when((m >= 0) & (m < MICRO))
        def _():
            @pl.when(sec == 0)
            def _():
                boundary(LEFT, m).wait_recv()

            first = m == 0
            reset = r.reset[m][:, 0:1]
            go, gm, sm = of(r.go, m), of(r.gm, m), r.sm
            act, dec = of(r.act, m), of(r.dec, m)
            gs, gd, gr, gb, gc = r.gs, dec, r.gr, r.gb, r.gc

            def early(step):
                @pl.when((m == MICRO - 1) & (sec == 0))
                def _():
                    step()

            if inside:
                operand(2, m).start()
            b_gate(first, go, wout, of(r.sz, m), of(r.dz, m), act, gs, gm, sm)
            if inside:
                for zz in high:
                    operand(3, m, zz).start()
            b_prep(of(r.proj, m), r.cols, r.diag)
            b_scan(
                (lambda: early(first_products)) if inside else None,
                first, gs, rows, dec, r.cols, r.diag, of(r.drive, m), r.h.at[m], r.adj, gd, gr, gb, gc, sm
            )
            if inside:
                early(second_products)
            b_pre(first, act, of(r.drate, m), small, gd, gr, gb, gc, of(r.gpre, m), of(r.gp, m), sm)
            b_conv(first, reset, rows, small, of(r.x, m), of(r.dact, m), gs, gd, of(r.rate, m), of(r.gp, m), gm, sm)
            if inside:
                for zz in low:
                    operand(3, m, zz).start()
                early(products_head)
            sg = of(r.v_grad, m)
            b_in(first, of(r.u, m), go, gain, win, gm, sg, r.gg)

            @pl.when(sec == 1)
            def _():
                of(r.back, m)[...] = sg[...].astype(bf16)
                boundary(LEFT, m).start()

            keep(m, 1).start()
            if inside:
                early(fourth_step)

        return carry

    lax.fori_loop(0, MICRO + 1, backward, 0)
    if inside:

        @pl.when(sec == 1)
        def _():
            first_products()
            second_products()
            products_head()
            fourth_step()

        @pl.when(jnp.logical_not(end))
        def _():
            scatter.line(0)

        products_in(low)
        scatter.start(2)
        small_across().wait_recv()
        add_rows(part(r.gws, links.x, half_rows * r3), r.xs)
        scatter.start(3)

        @pl.when(jnp.logical_not(end))
        def _():
            scatter.line(1)

        scatter.core(2)

        @pl.when(end)
        def _():
            scatter.line(2)

        scatter.core(3)
        small_direct(lambda copy: copy.start())

        @pl.when(jnp.logical_not(end))
        def _():
            scatter.line(2)

        for p in range(len(gather.pieces)):
            gather.finish(p)
        for m in range(MICRO):
            for kind in range(3):
                operand(kind, m).wait_send()
            for zz in range(links.zs):
                operand(3, m, zz).wait_send()
        small_across().wait_send()
        results = [
            pltpu.make_async_copy(src, dst, r.fetch.at[at])
            for at, (src, dst) in enumerate(
                ((r.v_gsmall, r.gsmall_shard), (r.v_gout, r.gout_shard), (r.v_gin, r.gin_shard))
            )
        ]
        small_direct(lambda copy: copy.wait_recv())
        total_small = scatter.mine(3, links.z)[...].astype(f32)
        for step in range(1, links.zs):
            total_small = total_small + part(r.ss, step, r3)[...].astype(f32)
        r.v_gsmall[...] = total_small
        results[0].start()
        scatter.own(0)
        results[1].start()
        scatter.finish(0)
        small_direct(lambda copy: copy.wait_send())
        scatter.copy(3, CORE).wait_send()
        scatter.own(1)
        scatter.finish(1)
        scatter.own(2)
        results[2].start()
        scatter.finish(2)
        for result in results:
            result.wait()
    else:
        products_out()
        products_in(None)
        products_head()

    for m in range(MICRO):
        for at in range(2):
            keep(m, at).wait()

    for m in range(MICRO):

        @pl.when(sec == 0)
        def _():
            boundary(RIGHT, m).wait_send()

        @pl.when(sec == 1)
        def _():
            boundary(LEFT, m).wait_send()


def call(n, inside, arrays):
    r1, r2, zs = 2 * DI // n, DI // n, n // 4
    rows2 = MICRO * T
    outs = dict(
        section_out=((MICRO, T, D), bf16),
        section_grad=((MICRO, T, D), f32),
    )
    scratch = dict(
        reset=((MICRO, T, 128), f32),
        u=((rows2, D), bf16),
        go=((rows2, D), bf16),
        back=((rows2, D), bf16),
        normed=((rows2, D), bf16),
        x=((rows2, DI), f32),
        dact=((rows2, DI), f32),
        sz=((rows2, DI), f32),
        dz=((rows2, DI), f32),
        rate=((rows2, DI), f32),
        drate=((rows2, DI), f32),
        act=((rows2, DI), bf16),
        gated=((rows2, DI), bf16),
        gpre=((rows2, DI), bf16),
        gm=((rows2, 2 * DI), bf16),
        proj=((rows2, 128), f32),
        rin=((rows2, 128), bf16),
        gp=((rows2, 128), bf16),
        h=((MICRO, (T + 1) * NS, DI), bf16),
        adj=((T * NS, CS), bf16),
        dec=((rows2, DI), f32),
        gs=((T, DI), f32),
        gr=((T, DI), f32),
        gb=((T, NS * TB), f32),
        gc=((T, NS * TB), bf16),
        drive=((rows2, DI), bf16),
        cols=((T * NS, 128), f32),
        diag=((T, NS * TB), bf16),
        rows=((32, DI), f32),
        gain=((1, D), f32),
    )
    scratch |= dict(v_out=((rows2, D), bf16), v_grad=((rows2, D), f32), v_markers=((MICRO, T), jnp.int32))
    sems = dict(edge=(2, 2, MICRO), loads=(MICRO,), keeps=(2, MICRO), fetch=(12,))
    if inside:
        outs |= dict(
            gin_shard=((r1, D), f32),
            gout_shard=((r2, D), f32),
            gsmall_shard=((r2 + 32, 128), f32),
        )
        scratch |= dict(
            v_norm_gain=((1, D // n), f32),
            v_in_proj=((r1, D), f32),
            v_conv_weight=((1, KC, r2), f32),
            v_conv_bias=((1, r2), f32),
            v_x_proj=((RK + 2 * NS, r2), f32),
            v_dt_proj=((1, RK, r2), f32),
            v_dt_bias=((1, r2), f32),
            v_a_log=((NS, r2), f32),
            v_d_skip=((1, r2), f32),
            v_out_proj=((1, r2, D), f32),
            v_gin=((r1, D), f32),
            v_gout=((r2, D), f32),
            v_gsmall=((r2 + 32, 128), f32),
            sm=((32, DI), f32),
            gg=((1, D), f32),
            win=((2 * DI, D), bf16),
            wout=((DI, D), bf16),
            small=((DI, 128), bf16),
            tails=((32 * n, 128), bf16),
            gwi=((DI, D), bf16),
            gwo=((DI // 2, D), bf16),
            gws=((n * (r2 + 32), 128), bf16),
            head=((DI, 128), f32),
            xg=((rows2, DI), bf16),
            xn=((rows2, D), bf16),
            xo=((rows2, D), bf16),
            xm=((rows2, DI), bf16),
            ci=((zs * r1, D), bf16),
            co=((zs * r2, D), bf16),
            cs=((zs * (r2 + 32), 128), bf16),
            xs=((2 * zs * (r2 + 32), 128), bf16),
            ss=((zs * (r2 + 32), 128), bf16),
            ui=((zs * r1, D), bf16),
            uo=((zs * r2, D), bf16),
            di=((zs * r1, D), bf16),
            do=((zs * r2, D), bf16),
        )
        sems |= dict(
            ag_line=(5, 4, zs),
            ag_core=(5, 2 * zs),
            ag_recv=(5, n),
            rs_core=(4, 2),
            rs_line=(3, 8, zs),
            xs_sems=(8, max(MICRO, zs), 2),
        )
    else:
        outs |= dict(
            gwi=((2 * DI, D), f32),
            gwo=((DI, D), f32),
            gws=((DI, 128), f32),
            gg=((1, D), f32),
            sm=((32, DI), f32),
        )
        scratch |= dict(
            win=((2 * DI, D), bf16),
            wout=((DI, D), bf16),
            small=((DI, 128), bf16),
            v_raw_rows=((32, DI), f32),
        )
    names = list(arrays) + list(outs) + list(scratch) + list(sems)
    whole = pl.BlockSpec(memory_space=pltpu.VMEM)
    far = pl.BlockSpec(memory_space=pl.ANY)
    results = pl.pallas_call(
        functools.partial(block, names, inside, n),
        out_shape=[jax.ShapeDtypeStruct(*spec) for spec in outs.values()],
        in_specs=[far] * len(arrays),
        out_specs=[far] * len(outs) if inside else [far] * 2 + [whole] * (len(outs) - 2),
        scratch_shapes=[pltpu.VMEM(*spec) for spec in scratch.values()]
        + [pltpu.SemaphoreType.DMA(shape) for shape in sems.values()],
        compiler_params=pltpu.CompilerParams(
            collective_id=0, has_side_effects=True, vmem_limit_bytes=63 * 2**20
        ),
        name="two_layer_block",
    )(*arrays.values())
    return types.SimpleNamespace(**dict(zip(outs, results)))


def unpack(
    out, grad, gin, gout, gsmall, out_o, grad_o, gain_o, in_o, cw_o, cb_o, x_o, dt_o, db_o, a_o, ds_o, po_o
):
    r2, gw = cb_o.shape[1], gain_o.shape[1]
    out_o[0] = out[...]
    grad_o[0] = grad[...]
    po_o[0] = gout[...]
    in_o[...] = gin[...]
    tail = gsmall[pl.ds(r2, 32), :]
    gain_o[...] = tail[23:24, 0:gw]
    cw_o[0] = tail[NS : NS + KC, 0:r2]
    cb_o[...] = tail[20:21, 0:r2]
    db_o[...] = tail[21:22, 0:r2]
    ds_o[...] = tail[22:23, 0:r2]
    a_o[...] = tail[0:NS, 0:r2]
    small = gsmall[pl.ds(0, r2), :].T
    x_o[...] = small[0 : RK + 2 * NS, :]
    dt_o[0] = small[RK + 2 * NS : 128, :]


def on_device(inputs, cotangent, markers, *weights):
    (
        norm_gain,
        in_proj,
        conv_weight,
        conv_bias,
        x_proj,
        dt_proj,
        dt_bias,
        a_log,
        d_skip,
        out_proj,
    ) = weights
    n = lax.axis_size(DP)
    inside = n == 16
    arrays = dict(inputs=inputs, cotangent=cotangent, markers=markers)
    if inside:
        arrays |= dict(
            norm_gain=norm_gain,
            in_proj=in_proj[0].T,
            conv_weight=conv_weight,
            conv_bias=conv_bias,
            x_proj=x_proj[0].T,
            dt_proj=dt_proj,
            dt_bias=dt_bias,
            a_log=a_log[0].T,
            d_skip=d_skip,
            out_proj=out_proj,
        )
        res = call(n, inside, arrays)
        whole = pl.BlockSpec(memory_space=pltpu.VMEM)
        turned = (in_proj, x_proj, a_log)
        shapes = [((1,) + res.section_out.shape, bf16), ((1,) + res.section_grad.shape, f32)]
        shapes += [(w.shape[:0:-1] if any(w is t for t in turned) else w.shape, f32) for w in weights]
        done = pl.pallas_call(
            unpack,
            out_shape=[jax.ShapeDtypeStruct(*spec) for spec in shapes],
            in_specs=[whole] * 5,
            out_specs=[whole] * 12,
            name="unpack",
        )(
            res.section_out,
            res.section_grad,
            res.gin_shard,
            res.gout_shard,
            res.gsmall_shard,
        )
        grads = (g.T[None] if any(w is t for t in turned) else g for w, g in zip(weights, done[2:]))
        return (*done[:2], *grads)

    def gathered(value, axis):
        return lax.all_gather(value.astype(bf16), DP, axis=axis, tiled=True)

    r2 = DI // n
    raw = jnp.concatenate(
        [a_log[0].T, conv_weight[0], conv_bias, dt_bias, d_skip, jnp.zeros((9, r2), f32)], axis=0
    )
    arrays |= dict(
        all_win=gathered(in_proj[0].T, 0),
        all_wout=gathered(out_proj[0], 0),
        all_small=gathered(jnp.concatenate([x_proj[0], dt_proj[0].T], axis=1), 0),
        raw_rows=gathered(raw, 1).astype(f32),
        all_gain=gathered(norm_gain, 1).astype(f32),
    )
    res = call(n, inside, arrays)

    def scattered(value, axis):
        return lax.psum_scatter(value, DP, scatter_dimension=axis, tiled=True)

    gin, gout, gsmall = scattered(res.gwi, 0), scattered(res.gwo, 0), scattered(res.gws, 0)
    rows = scattered(res.sm, 1)
    return (
        res.section_out[None],
        res.section_grad[None],
        scattered(res.gg, 1),
        gin.T[None],
        rows[NS : NS + KC][None],
        rows[20:21],
        gsmall[:, 0 : RK + 2 * NS][None],
        gsmall[:, RK + 2 * NS : 128].T[None],
        rows[21:22],
        rows[0:NS].T[None],
        rows[22:23],
        gout[None],
    )


def solution(mesh):
    tokens = P(None, DP, None)
    columns = P(SECTION, None, DP)
    channels = P(SECTION, DP)
    rows = P(SECTION, DP, None)
    kept = P(SECTION, None, DP, None)
    weights = (
        channels,
        columns,
        columns,
        channels,
        rows,
        columns,
        channels,
        rows,
        channels,
        rows,
    )
    return jax.shard_map(
        on_device,
        mesh=mesh,
        in_specs=(tokens, tokens, P(None, DP)) + weights,
        out_specs=(kept, kept) + weights,
        check_vma=False,
    )
```

```python
import functools
import types

import jax
import jax.numpy as jnp
from jax import lax
from jax.experimental import pallas as pl
from jax.experimental.pallas import tpu as pltpu
from jax.sharding import PartitionSpec as P

T = 128
D = 768
DI = 1536
NS = 16
KC = 4
RK = 48
MICRO = 2
C = 512
CS = 768
TB = 16
NB = T // TB
EPS = 1e-5
LOG2E = 1.4426950408889634
LN2 = 0.6931471805599453
BIG = 1e30
DP, SECTION = "dp", "section"
UP, DOWN, ACROSS, CORE = range(4)
BELOW, ABOVE = range(2)
START, FINISH = range(2)
RIGHT, LEFT = range(2)
f32 = jnp.float32
bf16 = jnp.bfloat16


def nn(a, b):
    return lax.dot_general(a, b, (((1,), (0,)), ((), ())), preferred_element_type=f32)


def nt(a, b):
    return lax.dot_general(a, b, (((1,), (1,)), ((), ())), preferred_element_type=f32)


def tn(a, b):
    return lax.dot_general(a, b, (((0,), (0,)), ((), ())), preferred_element_type=f32)


def iota(shape, axis):
    return lax.broadcasted_iota(jnp.int32, shape, axis)


def sigmoid(v):
    return 0.5 * jnp.tanh(0.5 * v) + 0.5


def wide(v):
    return jnp.concatenate([v] * (CS // 128), axis=1)


def keeps(reset):
    keep = [None]
    cur = jnp.ones_like(reset)
    for k in range(1, KC):
        cur = cur * (1.0 - (reset if k == 1 else pltpu.roll(reset, k - 1, 0)))
        keep.append(cur)
    return keep


def block_diagonal(cols):
    tile = (iota((NS, NS * TB), 1) % NS == iota((NS, NS * TB), 0)).astype(bf16)
    rep = nn(cols.astype(bf16), tile)
    own = (iota((T, NS * TB), 1) // NS) == (iota((T, NS * TB), 0) % TB)
    return jnp.where(own, rep, 0.0).astype(bf16)


def lane_columns(dst, val):
    for t in range(T):
        dst[pl.ds(t * NS, NS), :] = jnp.broadcast_to(val[:, t : t + 1], (NS, 128))


def f_x(reset, normed, win, rows, x_ref, act, dact):
    keep = keeps(reset)
    for c in range(DI // C):
        s = pl.ds(c * C, C)
        x = nt(normed[...], win[s, :])
        x_ref[:, s] = x
        v = rows[20:21, s] + rows[16:17, s] * x
        for k in range(1, KC):
            v = v + rows[16 + k : 17 + k, s] * (pltpu.roll(x, k, 0) * keep[k])
        sg = sigmoid(v)
        act[:, s] = (v * sg).astype(bf16)
        dact[:, s] = sg * (1.0 + v * (1.0 - sg))


def f_rate(reset, act, small, rows, proj, rin, rate_ref, drate, dec, drive, drive_low, cols, diag):
    p = nn(act[...], small[:, 0:128])
    proj[...] = p
    lane_columns(cols, p.T[RK : RK + NS, :])
    diag[...] = block_diagonal(p[:, RK + NS : RK + 2 * NS])
    rin[...] = pltpu.roll(jnp.where(iota((T, 128), 1) < RK, p, 0.0), RK + 2 * NS, 1).astype(bf16)
    for c in range(DI // C):
        s = pl.ds(c * C, C)
        pre = nt(rin[...], small[s, 0:128]) + rows[21:22, s]
        e = jnp.exp(-jnp.abs(pre))
        rate = jnp.maximum(pre, 0.0) + jnp.log1p(e)
        rate_ref[:, s] = rate
        drate[:, s] = jnp.where(pre >= 0.0, 1.0, e) / (1.0 + e)
        dec[:, s] = jnp.where(reset > 0.0, BIG, rate)
        both = rate * act[:, s].astype(f32)
        drive[:, s] = both
        drive_low[:, s] = both.astype(bf16)


def f_scan(act, rows, dec, drive, cols, diag, h_ref, ssm):
    h_ref[0:NS, :] = jnp.zeros((NS, DI), bf16)
    for c in range(DI // CS):
        s = pl.ds(c * CS, CS)

        def block(i, h):
            t0 = pl.multiple_of(i * TB, TB)
            a2 = rows[0:NS, s]
            d = dec[pl.ds(t0, TB), s]
            v = drive[pl.ds(t0, TB), s]
            for j in range(TB):
                b = wide(cols[pl.ds(t0 * NS + j * NS, NS), :])
                h = jnp.exp2(d[j : j + 1, :] * a2) * h + v[j : j + 1, :] * b
                h_ref[pl.ds(t0 * NS + (j + 1) * NS, NS), s] = h.astype(bf16)
            return h

        lax.fori_loop(0, NB, block, jnp.zeros((NS, CS), f32))

    def sums(i, carry):
        for q in range(8):
            t0 = pl.multiple_of(i * (8 * TB) + q * TB, TB)
            tt = pl.ds(t0, TB)
            y = nn(diag[tt, :], h_ref[pl.ds(t0 * NS + NS, TB * NS), :])
            ssm[tt, :] = y + rows[22:23, :] * act[tt, :].astype(f32)
        return carry

    lax.fori_loop(0, NB // 8, sums, 0)


def f_out(u, normed, win, wout, ssm, sz_ref, dz_ref, gated, out):
    acc = u[...].astype(f32)
    for c in range(DI // C):
        s = pl.ds(c * C, C)
        z = nt(normed[...], win[pl.ds(DI + c * C, C), :])
        sg = sigmoid(z)
        sz = z * sg
        sz_ref[:, s] = sz
        dz_ref[:, s] = ssm[:, s] * (sg * (1.0 + z * (1.0 - sg)))
        g = (ssm[:, s] * sz).astype(bf16)
        gated[:, s] = g
        acc = acc + nn(g, wout[s, :])
    out[...] = acc.astype(bf16)


def total(old, first, value):
    return jnp.where(first, value, old + value)


def b_gate(first, go_ref, wout, sz, dz, act, gs_ref, gm, sm):
    go = go_ref[...]
    for c in range(DI // C):
        s = pl.ds(c * C, C)
        gg = nt(go, wout[s, :])
        gs = gg * sz[:, s]
        gs_ref[:, s] = gs
        gm[:, pl.ds(DI + c * C, C)] = (gg * dz[:, s]).astype(bf16)
        part = jnp.sum(gs * act[:, s].astype(f32), axis=0, keepdims=True)
        sm[22:23, s] = total(sm[22:23, s], first, part)


def b_prep(proj, cols, diag):
    p = proj[...]
    lane_columns(cols, p.T[RK + NS : RK + 2 * NS, :])
    diag[...] = block_diagonal(p[:, RK : RK + NS])


def b_scan(between, first, gs, rows, dec, cols, diag, drive, h_ref, adj_ref, ea_ref, gd, gr, gb, gc, sm):
    ones = (iota((TB, TB * NS), 1) // NS) == iota((TB, TB * NS), 0)
    od = (iota((TB, TB * NS // 2), 1) // (NS // 2) == iota((TB, TB * NS // 2), 0)).astype(bf16)

    def state_sums(i, carry):
        for q in range(8):
            t0 = pl.multiple_of(i * (8 * TB) + q * TB, TB)
            tt = pl.ds(t0, TB)
            full = nt(gs[tt, :].astype(bf16), h_ref[pl.ds(t0 * NS + NS, TB * NS), :])
            gc[tt, :] = jnp.where(ones, full, 0.0).astype(bf16)
        return carry

    lax.fori_loop(0, NB // 8, state_sums, 0)
    for c in range(DI // CS):
        s = pl.ds(c * CS, CS)

        def block(i, state):
            carry, acc = state
            t0 = pl.multiple_of((NB - 1 - i) * TB, TB)
            a2 = rows[0:NS, s]
            d = dec[pl.ds(t0, TB), s]
            g = gs[pl.ds(t0, TB), s]
            later = None
            for j in reversed(range(TB)):
                row = pl.ds(t0 * NS + j * NS, NS)
                adj = g[j : j + 1, :] * wide(cols[row, :]) + carry
                adj_ref[row, :] = adj.astype(bf16)
                dj = d[j : j + 1, :]
                carry = jnp.exp2(dj * a2) * adj
                expo = carry * h_ref[row, s].astype(f32)
                weighted = expo * a2
                weighted = weighted[0 : NS // 2] + weighted[NS // 2 :]
                if j % 2:
                    later = weighted
                else:
                    pair = pl.ds(pl.multiple_of(t0 * (NS // 2), NS) + j * (NS // 2), NS)
                    ea_ref[pair, :] = jnp.concatenate([weighted, later], axis=0).astype(bf16)
                acc = acc + expo * dj
            return carry, acc

        zero = jnp.zeros((NS, CS), f32)
        _, acc = lax.fori_loop(0, NB, block, (zero, zero))
        sm[0:NS, s] = total(sm[0:NS, s], first, acc * rows[0:NS, s] * LN2)

        def adjoint_sums(i, carry):
            for q in range(8):
                t0 = pl.multiple_of(i * (8 * TB) + q * TB, TB)
                tt = pl.ds(t0, TB)
                row = pl.ds(t0 * NS, TB * NS)
                gd[tt, s] = nn(diag[tt, :], adj_ref[row, :])
            for q in range(8):
                t0 = pl.multiple_of(i * (8 * TB) + q * TB, TB)
                tt = pl.ds(t0, TB)
                ea = ea_ref[pl.ds(pl.multiple_of(t0 * (NS // 2), NS), TB * NS // 2), :]
                gr[tt, s] = nn(od, ea) * LN2
            for q in range(8):
                t0 = pl.multiple_of(i * (8 * TB) + q * TB, TB)
                tt = pl.ds(t0, TB)
                row = pl.ds(t0 * NS, TB * NS)
                full = nt(drive[tt, s], adj_ref[row, :])
                gb[tt, :] = full if c == 0 else gb[tt, :] + full
            return carry

        lax.fori_loop(0, NB // 8, adjoint_sums, 0)
        if c == 0 and between is not None:
            between()


def b_pre(first, act, drate, small, gd, gr, gb, gc, gpre, gp, sm):
    acc = jnp.zeros((T, 128), f32)
    for c in range(DI // C):
        s = pl.ds(c * C, C)
        g = ((gr[:, s] + gd[:, s] * act[:, s].astype(f32)) * drate[:, s]).astype(bf16)
        gpre[:, s] = g
        part = jnp.sum(g.astype(f32), axis=0, keepdims=True)
        sm[21:22, s] = total(sm[21:22, s], first, part)
        acc = acc + nn(g, small[s, 0:128])
    k = iota((TB * NS, 128), 0) % NS
    lane = iota((TB * NS, 128), 1)
    own = (iota((T, NS * TB), 1) // NS) == (iota((T, NS * TB), 0) % TB)
    gb_own = jnp.where(own, gb[...], 0.0).astype(bf16)
    bc = nn(gb_own, (lane == RK + k).astype(bf16)) + nn(gc[...], (lane == RK + NS + k).astype(bf16))
    gp[...] = jnp.where(iota((T, 128), 1) < RK, pltpu.roll(acc, RK, 1), bc).astype(bf16)


def b_conv(first, reset, rows, small, x_ref, dact, gs, gd, rate, gp, gm, sm):
    keep = keeps(reset)
    for c in range(DI // C):
        s = pl.ds(c * C, C)
        ga = gs[:, s] * rows[22:23, s] + gd[:, s] * rate[:, s] + nt(gp[...], small[s, 0:128])
        gc = ga * dact[:, s]
        x = x_ref[:, s]
        part = jnp.sum(gc, axis=0, keepdims=True)
        sm[20:21, s] = total(sm[20:21, s], first, part)
        gx = jnp.zeros((T, C), f32)
        for k in range(KC):
            ahead = pltpu.roll(gc * keep[k], T - k, 0) if k else gc
            part = jnp.sum(ahead * x, axis=0, keepdims=True)
            sm[16 + k : 17 + k, s] = total(sm[16 + k : 17 + k, s], first, part)
            gx = gx + ahead * rows[16 + k : 17 + k, s]
        gm[:, s] = gx.astype(bf16)


def b_in(first, u_ref, go_ref, gain, win, gm, sg, gg):
    gn = jnp.zeros((T, D), f32)
    for c in range(2 * DI // C):
        s = pl.ds(c * C, C)
        gn = gn + nn(gm[:, s], win[s, :])
    u = u_ref[...].astype(f32)
    inv = lax.rsqrt(jnp.mean(u * u, axis=-1, keepdims=True) + EPS)
    g = gn * gain[...]
    gg[...] = total(gg[...], first, jnp.sum(gn * u * inv, axis=0, keepdims=True))
    mean = jnp.mean(g * u, axis=-1, keepdims=True)
    sg[...] = go_ref[...].astype(f32) + inv * g - u * (inv * inv * inv) * mean


class Links:
    def __init__(self, n):
        self.zs = n // 4
        i = lax.axis_index(DP)
        self.i = i
        self.c = i % 2
        self.x = (i // 2) % 2
        self.z = i // 4

    def owner(self, z, x, c):
        return 4 * z + 2 * x + c

    def dev(self, route):
        step = (4, -4, 2 - 4 * self.x, 1 - 2 * self.c)[route]
        return dict(dp=self.i + step)

    def greet(self):
        sem = pltpu.get_barrier_semaphore()

        def tell(device):
            pl.semaphore_signal(sem, inc=1, device_id=device, device_id_type=pl.DeviceIdType.MESH)

        tell(self.dev(ACROSS))
        tell(self.dev(CORE))
        tell(dict(section=1 - lax.axis_index(SECTION)))

        @pl.when(self.z < self.zs - 1)
        def _():
            tell(self.dev(UP))

        @pl.when(self.z > 0)
        def _():
            tell(self.dev(DOWN))

    def meet(self):
        ends = jnp.where(self.z < self.zs - 1, 1, 0) + jnp.where(self.z > 0, 1, 0)
        pl.semaphore_wait(pltpu.get_barrier_semaphore(), 3 + ends)


def part(ref, index, count, first=0, rows=None):
    return ref.at[pl.ds(pl.multiple_of(index * count + first, 16), rows or count), :]


def remote(src, dst, send, recv, device):
    return pltpu.make_async_remote_copy(
        src_ref=src,
        dst_ref=dst,
        send_sem=send,
        recv_sem=recv,
        device_id=device,
        device_id_type=pl.DeviceIdType.MESH,
    )


class Gather:
    def __init__(self, links, pieces, balanced, line_send, core_send, recv):
        self.k, self.pieces, self.balanced = links, pieces, balanced
        self.line_send, self.core_send, self.recv = line_send, core_send, recv

    def copy(self, p, z, x, c, route, slot=None):
        whole, count = self.pieces[p][:2]
        ref = part(whole, self.k.owner(z, x, c), count)
        if route == CORE:
            send = self.core_send.at[p, 2 * z + x]
        else:
            send = self.line_send.at[p, route if slot is None else slot, z]
        return remote(ref, ref, send, self.recv.at[p, self.k.owner(z, x, c)], self.k.dev(route))

    def each(self, p, side, r, act):
        k = self.k
        lo, hi = self.pieces[p][2:]
        z = k.z - r if side == BELOW else k.z + r

        @pl.when((z >= lo) & (z < hi))
        def _():
            act(z)

    def line(self, p, r):
        def pass_on(z, side):
            k = self.k
            self.copy(p, z, k.x, k.c, ACROSS).wait_recv()
            self.go(p, z, side, START)

        for side in (BELOW, ABOVE):
            self.each(p, side, r, functools.partial(pass_on, side=side))

    def go(self, p, z, side, do):
        k = self.k

        def one(route):
            copy = self.copy(p, z, k.x, k.c, route)
            copy.wait_send() if do == FINISH else copy.start()

        @pl.when(jnp.logical_not(self.by_line(p, z)))
        def _():
            one(ACROSS)

        if side != ABOVE:

            @pl.when(k.z < k.zs - 1)
            def _():
                one(UP)

        if side != BELOW:

            @pl.when(k.z > 0)
            def _():
                one(DOWN)

        one(CORE)

    def by_line(self, p, z):
        k = self.k
        last = k.zs - 1
        near = ((k.z == 1) & (z == 0)) | ((k.z == last - 1) & (z == last))
        if p not in self.balanced:
            return near
        return near | ((k.z == 0) & (z == last)) | ((k.z == last) & (z == 0))

    def relay(self, p, z, do):
        k = self.k
        last = k.zs - 1
        far = int(p in self.balanced)

        def one(route):
            copy = self.copy(p, z, 1 - k.x, k.c, route, 3)
            copy.wait_send() if do == FINISH else copy.start()

        @pl.when(((k.z == 0) & (z == 0)) | ((k.z == last - 1) & (z == 0) & (far == 1)))
        def _():
            one(UP)

        @pl.when(((k.z == last) & (z == last)) | ((k.z == 1) & (z == last) & (far == 1)))
        def _():
            one(DOWN)

    def start(self, p):
        self.each(p, BELOW, 0, lambda z: self.go(p, z, None, START))

    def across(self, p, r):
        def pass_on(z):
            copy = self.copy(p, z, 1 - self.k.x, self.k.c, CORE)
            copy.wait_recv()
            self.relay(p, z, START)
            copy.start()

        self.each(p, BELOW, r, pass_on)
        if r:
            self.each(p, ABOVE, r, pass_on)

    def arrived(self, p):
        for z in range(*self.pieces[p][2:]):
            for x in range(2):
                self.copy(p, z, x, 1 - self.k.c, CORE).wait_recv()

    def finish(self, p):
        k = self.k

        def crossed(z):
            self.copy(p, z, 1 - k.x, k.c, CORE).wait_send()
            self.relay(p, z, FINISH)

        for r in range(k.zs):
            for side in (BELOW, ABOVE) if r else (BELOW,):
                self.each(p, side, r, lambda z, side=side: self.go(p, z, side if r else None, FINISH))
                self.each(p, side, r, crossed)


def add_rows(dst, src):
    count = dst.shape[0]
    step = 48 if count % 48 == 0 else 16

    def add(i, carry):
        s = pl.ds(pl.multiple_of(i * step, 16), step)
        dst[s, :] = (dst[s, :].astype(f32) + src[s, :].astype(f32)).astype(dst.dtype)
        return carry

    lax.fori_loop(0, count // step, add, 0)


class Scatter:
    def __init__(self, links, pieces, subs, core_sems, line_sems):
        self.k, self.pieces, self.subs = links, pieces, subs
        self.core_sems, self.line_sems = core_sems, line_sems

    def rows(self, p, c, z, count=1):
        g, first, _, _, _, _, size, _, _ = self.pieces[p]
        return part(g, 1, first + (c * self.k.zs + z) * size, 0, count * size)

    def mine(self, p, z, sub=None):
        whole = self.rows(p, self.k.c, z)
        return whole if sub is None else self.half(p, whole, sub)

    def half(self, p, ref, sub):
        count = ref.shape[0] // self.subs[p]
        return ref.at[pl.ds(sub * count, count), :]

    def copy(self, p, route, z=None, sub=0):
        k = self.k
        _, _, core, below, above, _, size, lo, hi = self.pieces[p]
        if route == CORE:
            send, recv = self.core_sems.at[p, 0], self.core_sems.at[p, 1]
            src, dst = self.rows(p, 1 - k.c, lo, hi - lo), part(core, 1, lo * size, 0, (hi - lo) * size)
        else:
            at = 4 * sub + 2 * route
            send, recv = self.line_sems.at[p, at, z], self.line_sems.at[p, at + 1, z]
            src, dst = self.mine(p, z, sub), self.half(p, part((below, above)[route], z, size), sub)
        return remote(src, dst, send, recv, k.dev(route))

    def far_first(self, p):
        k = self.k
        lo, hi = self.pieces[p][7:]
        for i in range(hi - lo):
            table = [sorted(range(lo, hi), key=lambda o: (-abs(o - z), o))[i] for z in range(k.zs)]
            z = table[0]
            for at in range(1, k.zs):
                z = jnp.where(k.z == at, table[at], z)
            yield z

    def start(self, p):
        self.copy(p, CORE).start()

    def core(self, p):
        _, _, core, _, _, _, size, lo, hi = self.pieces[p]
        self.copy(p, CORE).wait_recv()
        add_rows(self.rows(p, self.k.c, lo, hi - lo), part(core, 1, lo * size, 0, (hi - lo) * size))

    def line(self, p):
        k = self.k
        _, _, _, below, above, _, size, _, _ = self.pieces[p]
        for z in self.far_first(p):

            def hop(route, inner, source):
                for sub in range(self.subs[p]):

                    @pl.when(inner)
                    def _():
                        self.copy(p, route, z, sub).wait_recv()
                        add_rows(self.mine(p, z, sub), self.half(p, part(source, z, size), sub))

                    self.copy(p, route, z, sub).start()

            @pl.when(z > k.z)
            def _():
                hop(UP, k.z > 0, below)

            @pl.when(z < k.z)
            def _():
                hop(DOWN, k.z < k.zs - 1, above)

    def own(self, p):
        k = self.k
        _, _, _, below, above, result, size, lo, hi = self.pieces[p]

        @pl.when((k.z >= lo) & (k.z < hi))
        def _():
            result[...] = self.mine(p, k.z)[...].astype(f32)
            for sub in range(self.subs[p]):

                def take(route, source):
                    self.copy(p, route, k.z, sub).wait_recv()
                    add_rows(self.half(p, result, sub), self.half(p, part(source, k.z, size), sub))

                @pl.when(k.z > 0)
                def _():
                    take(UP, below)

                @pl.when(k.z < k.zs - 1)
                def _():
                    take(DOWN, above)

    def finish(self, p):
        k = self.k
        self.copy(p, CORE).wait_send()
        for z in range(*self.pieces[p][7:]):
            for sub in range(self.subs[p]):

                @pl.when(z > k.z)
                def _():
                    self.copy(p, UP, z, sub).wait_send()

                @pl.when(z < k.z)
                def _():
                    self.copy(p, DOWN, z, sub).wait_send()


def weight_rows(tails, rows, gain, n):
    r2, gw = DI // n, D // n
    parts = [tails[i * 32 : i * 32 + 32, :].astype(f32) for i in range(n)]
    rows[...] = jnp.concatenate([p[:, 0:r2] for p in parts], axis=1)
    gain[...] = jnp.concatenate([p[23:24, 0:gw] for p in parts], axis=1)


def block(names, inside, n, *refs):
    r = types.SimpleNamespace(**dict(zip(names, refs)))
    sec = lax.axis_index(SECTION)
    links = Links(n)
    r1, r2, gw = 2 * DI // n, DI // n, D // n
    r3 = r2 + 32
    if inside:
        far_in = (r.markers, r.norm_gain, r.in_proj, r.conv_weight, r.conv_bias, r.x_proj)
        far_in += (r.dt_proj, r.dt_bias, r.a_log, r.d_skip, r.out_proj)
        near_in = (r.v_markers, r.v_norm_gain, r.v_in_proj, r.v_conv_weight, r.v_conv_bias, r.v_x_proj)
        near_in += (r.v_dt_proj, r.v_dt_bias, r.v_a_log, r.v_d_skip, r.v_out_proj)
    else:
        far_in = (r.markers, r.all_win, r.all_wout, r.all_small, r.raw_rows, r.all_gain)
        near_in = (r.v_markers, r.win, r.wout, r.small, r.v_raw_rows, r.gain)
    rows, small, gain, win, wout = r.rows, r.small, r.gain, r.win, r.wout

    def of(ref, m):
        return ref.at[pl.ds(pl.multiple_of(m * T, T), T), :]

    def load(m, at):
        src, dst = ((r.inputs, r.u), (r.cotangent, r.go))[at]
        return pltpu.make_async_copy(src.at[m], of(dst, m), r.loads.at[m])

    if inside:
        links.greet()
    fetches = [
        pltpu.make_async_copy(src, dst, r.fetch.at[at])
        for at, (src, dst) in enumerate(zip(far_in, near_in, strict=True))
    ]
    for fetch in fetches:
        fetch.start()
    for at in range(2):

        @pl.when(sec == at)
        def _():
            for m in range(MICRO):
                load(m, at).start()

    r.sm[...] = jnp.zeros_like(r.sm)
    for fetch in fetches:
        fetch.wait()
    starts = jnp.where((r.v_markers[...] > 0) | (iota((MICRO, T), 1) == 0), 1.0, 0.0)
    starts = jnp.concatenate([starts, jnp.zeros((8 - MICRO, T), f32)], axis=0).T
    for m in range(MICRO):
        r.reset[m] = jnp.broadcast_to(starts[:, m : m + 1], (T, 128))
    def keep(m, at):
        src, dst = ((r.v_out, r.section_out), (r.v_grad, r.section_grad))[at]
        return pltpu.make_async_copy(of(src, m), dst.at[m], r.keeps.at[at, m])

    def boundary(route, m):
        if route == RIGHT:
            src, dst, at = of(r.v_out, m), of(r.u, m), 0
        else:
            src, dst, at = of(r.back, m), of(r.go, m), 1
        return remote(src, dst, r.edge.at[at, 0, m], r.edge.at[at, 1, m], dict(section=1 - sec))

    if inside:
        tails = r.tails
        part(win, links.i, r1)[...] = r.v_in_proj[...].astype(bf16)
        part(wout, links.i, r2)[...] = r.v_out_proj[0].astype(bf16)
        head = jnp.concatenate([r.v_x_proj[...], r.v_dt_proj[0]], axis=0).T
        part(small, links.i, r2)[...] = head.astype(bf16)
        top = [r.v_a_log[...], r.v_conv_weight[0], r.v_conv_bias[...], r.v_dt_bias[...], r.v_d_skip[...]]
        top.append(jnp.concatenate([r.v_norm_gain[...], jnp.zeros((1, r2 - gw), f32)], axis=1))
        top = jnp.concatenate(top + [jnp.zeros((8, r2), f32)], axis=0)
        top = jnp.concatenate([top, jnp.zeros((32, 128 - r2), f32)], axis=1)
        part(tails, links.i, 32)[...] = top.astype(bf16)
        links.meet()
        half = links.zs // 2
        pieces = [
            (tails, 32, 0, links.zs),
            (small, r2, 0, links.zs),
            (win, r1, 0, half),
            (win, r1, half, links.zs),
            (wout, r2, 0, links.zs),
        ]
        gather = Gather(links, pieces, (4,), r.ag_line, r.ag_core, r.ag_recv)
        early, late = (0, 1, 2), (3, 4)

        def pass_on(ps, hops):
            for hop in hops:
                for p in ps:
                    if hop < links.zs:
                        gather.line(p, hop)
                for p in ps:
                    gather.across(p, hop - 1)

        for p in early:
            gather.start(p)
        for p in late:
            gather.start(p)
        for p in early:
            gather.line(p, 1)
        for p in late:
            gather.line(p, 1)
        for p in early:
            gather.across(p, 0)
        for p in early:
            gather.line(p, 2)
        for p in late:
            gather.across(p, 0)
        for p in early:
            gather.across(p, 1)
        for p in early:
            gather.line(p, 3)
        for p in late:
            gather.line(p, 2)
        for p in early:
            gather.across(p, 2)
        for p in late:
            gather.across(p, 1)
        for p in early:
            gather.across(p, 3)
        for p in late:
            gather.line(p, 3)
        for p in early:
            gather.arrived(p)

        def rest(hops):
            for hop in hops:
                for p in late:
                    gather.across(p, hop - 1)
            if links.zs in hops:
                for p in late:
                    gather.arrived(p)

        @pl.when(sec == 1)
        def _():
            rest((links.zs - 1, links.zs))

        weight_rows(tails, rows, gain, n)
        half_rows = 2 * links.zs
        pieces = [
            (r.gwo, 0, r.co, r.uo, r.do, r.v_gout, r2, 0, links.zs),
            (r.gwi, 0, r.ci, r.ui, r.di, r.v_gin, r1, half, links.zs),
            (r.gwi, 0, r.ci, r.ui, r.di, r.v_gin, r1, 0, half),
            (r.gws, links.x * half_rows * r3, r.cs, None, None, None, r3, 0, links.zs),
        ]
        scatter = Scatter(links, pieces, (1, 2, 2, 1), r.rs_core, r.rs_line)
        strip = 2 * r1

        def operand(kind, m, zz=0):
            src = of((r.gated, r.normed, r.go, r.gm)[kind], m)
            dst = of((r.xg, r.xn, r.xo, r.xm)[kind], m)
            if kind == 3:
                at = pl.multiple_of((2 * zz + 1 - links.x) * strip, 128)
                src, dst = src.at[:, pl.ds(at, strip)], dst.at[:, pl.ds(zz * strip, strip)]
            sems = r.xs_sems.at[kind + zz, m]
            return remote(src, dst, sems.at[0], sems.at[1], links.dev(ACROSS))

        def small_across():
            sems = r.xs_sems.at[7, 0]
            src = part(r.gws, 1 - links.x, half_rows * r3)
            return remote(src, r.xs, sems.at[0], sems.at[1], links.dev(ACROSS))

        def small_direct(act):
            for step in range(1, links.zs):
                to = (links.z + step) % links.zs
                sems = r.xs_sems.at[7, step]
                dst = part(r.ss, step, r3)
                act(remote(scatter.mine(3, to), dst, sems.at[0], sems.at[1], dict(dp=links.owner(to, links.x, links.c))))

    else:
        sem = pltpu.get_barrier_semaphore()
        pl.semaphore_signal(
            sem, inc=1, device_id=dict(section=1 - sec), device_id_type=pl.DeviceIdType.MESH
        )
        pl.semaphore_wait(sem, 1)
        rows[...] = r.v_raw_rows[...]
    for c in range(DI // C):
        s = pl.ds(c * C, C)
        rows[0:NS, s] = -jnp.exp(rows[0:NS, s]) * LOG2E

    def forward(k, carry):
        m = k - sec

        @pl.when((m >= 0) & (m < MICRO))
        def _():
            @pl.when(sec == 1)
            def _():
                boundary(RIGHT, m).wait_recv()

            @pl.when(sec == 0)
            def _():
                load(m, 0).wait()

            def gathering(hops):
                if inside:

                    @pl.when((sec == 0) & (m == 0))
                    def _():
                        rest(hops)

            u = of(r.u, m)
            reset = r.reset[m][:, 0:1]
            v = u[...].astype(f32)
            inv = lax.rsqrt(jnp.mean(v * v, axis=-1, keepdims=True) + EPS)
            normed, act, ssm = of(r.normed, m), of(r.act, m), r.gr
            normed[...] = (v * inv * gain[...]).astype(bf16)
            f_x(reset, normed, win, rows, of(r.x, m), act, of(r.dact, m))
            gathering((links.zs - 1,))
            f_rate(
                reset,
                act,
                small,
                rows,
                of(r.proj, m),
                of(r.rin, m),
                of(r.rate, m),
                of(r.drate, m),
                of(r.dec, m),
                r.gs,
                of(r.drive, m),
                r.cols,
                r.diag,
            )
            f_scan(act, rows, of(r.dec, m), r.gs, r.cols, r.diag, r.h.at[m], ssm)
            gathering((links.zs,))
            f_out(u, normed, win, wout, ssm, of(r.sz, m), of(r.dz, m), of(r.gated, m), of(r.v_out, m))

            @pl.when(sec == 0)
            def _():
                boundary(RIGHT, m).start()

            keep(m, 0).start()
            if inside:
                operand(0, m).start()
                operand(1, m).start()

        return carry

    lax.fori_loop(0, MICRO + 1, forward, 0)

    @pl.when(sec == 1)
    def _():
        for m in range(MICRO):
            load(m, 1).wait()

    def owners_rows(g, first, size, zz, value):
        for c in range(2):
            at = pl.ds(pl.multiple_of(first + (c * links.zs + zz) * size, 16), size)
            g[at, :] = value[c * size : (c + 1) * size].astype(g.dtype)

    def products_out():
        if inside:
            for kind in (0, 2):
                for m in range(MICRO):
                    operand(kind, m).wait_recv()
            def mine(ref, zz):
                at = zz * 4 * r2
                return jnp.where(links.x == 0, ref[:, at : at + 2 * r2], ref[:, at + 2 * r2 : at + 4 * r2])

            for zz in range(links.zs):
                value = tn(mine(r.gated, zz), r.go[...]) + tn(mine(r.xg, zz), r.xo[...])
                owners_rows(r.gwo, 0, r2, zz, value)
        else:
            for c in range(DI // C):
                s = pl.ds(c * C, C)
                r.gwo[s, :] = tn(r.gated[:, s], r.go[...])

    def products_in(zzs):
        if inside:
            for m in range(MICRO):
                if half in zzs:
                    operand(1, m).wait_recv()
                for zz in zzs:
                    operand(3, m, zz).wait_recv()
            for zz in zzs:
                mine = pl.ds(pl.multiple_of((2 * zz + links.x) * strip, 128), strip)
                full = tn(r.gm[:, mine], r.normed[...]) + tn(r.xm[:, pl.ds(zz * strip, strip)], r.xn[...])
                owners_rows(r.gwi, 0, r1, zz, full)
        else:
            for c in range(2 * DI // C):
                s = pl.ds(c * C, C)
                r.gwi[s, :] = tn(r.gm[:, s], r.normed[...])

    def products_head():
        for c in range(DI // C):
            s = pl.ds(c * C, C)
            value = tn(r.act[:, s], r.gp[...]) + tn(r.gpre[:, s], r.rin[...])
            if inside:
                r.head[s, :] = value
            else:
                r.gws[s, :] = value

    def products_small():
        sm, gg = r.sm[0:32, :], r.gg[...]
        for i in range(n):
            z, x, c = i // 4, (i // 2) % 2, i % 2
            to = ((x * 2 + c) * links.zs + z) * r3
            r.gws[pl.ds(to, r2), :] = r.head[pl.ds(i * r2, r2), :].astype(bf16)
            top = pltpu.roll(sm, -i * r2 % DI, 1)[:, 0:128]
            g = pltpu.roll(gg, -i * gw % D, 1)[:, 0:128]
            top = jnp.where(iota((32, 128), 0) == 23, jnp.broadcast_to(g, (32, 128)), top)
            r.gws[pl.ds(to + r2, 32), :] = top.astype(bf16)

    if inside:
        low, high = range(half), range(half, links.zs)
        end = (links.z == 0) | (links.z == links.zs - 1)

        def first_products():
            products_out()
            scatter.start(0)

        def second_products():
            scatter.core(0)
            products_in(high)
            scatter.start(1)

            @pl.when(end)
            def _():
                scatter.line(0)

        def fourth_step():
            products_small()
            small_across().start()
            scatter.core(1)

            @pl.when(end)
            def _():
                scatter.line(1)

    def backward(k, carry):
        m = k - (1 - sec)

        @pl.when((m >= 0) & (m < MICRO))
        def _():
            @pl.when(sec == 0)
            def _():
                boundary(LEFT, m).wait_recv()

            first = m == 0
            reset = r.reset[m][:, 0:1]
            go, gm, sm = of(r.go, m), of(r.gm, m), r.sm
            act, dec = of(r.act, m), of(r.dec, m)
            gs, gd, gr, gb, gc = r.gs, dec, r.gr, r.gb, r.gc

            def early(step):
                @pl.when((m == MICRO - 1) & (sec == 0))
                def _():
                    step()

            if inside:
                operand(2, m).start()
            b_gate(first, go, wout, of(r.sz, m), of(r.dz, m), act, gs, gm, sm)
            if inside:
                for zz in high:
                    operand(3, m, zz).start()
            b_prep(of(r.proj, m), r.cols, r.diag)
            b_scan(
                (lambda: early(first_products)) if inside else None,
                first, gs, rows, dec, r.cols, r.diag, of(r.drive, m), r.h.at[m], r.adj, r.ea, gd, gr, gb, gc, sm
            )
            if inside:
                early(second_products)
            b_pre(first, act, of(r.drate, m), small, gd, gr, gb, gc, of(r.gpre, m), of(r.gp, m), sm)
            b_conv(first, reset, rows, small, of(r.x, m), of(r.dact, m), gs, gd, of(r.rate, m), of(r.gp, m), gm, sm)
            if inside:
                for zz in low:
                    operand(3, m, zz).start()
                early(products_head)
            sg = of(r.v_grad, m)
            b_in(first, of(r.u, m), go, gain, win, gm, sg, r.gg)

            @pl.when(sec == 1)
            def _():
                of(r.back, m)[...] = sg[...].astype(bf16)
                boundary(LEFT, m).start()

            keep(m, 1).start()
            if inside:
                early(fourth_step)

        return carry

    lax.fori_loop(0, MICRO + 1, backward, 0)
    if inside:

        @pl.when(sec == 1)
        def _():
            first_products()
            second_products()
            products_head()
            fourth_step()

        @pl.when(jnp.logical_not(end))
        def _():
            scatter.line(0)

        products_in(low)
        scatter.start(2)
        small_across().wait_recv()
        add_rows(part(r.gws, links.x, half_rows * r3), r.xs)
        scatter.start(3)

        @pl.when(jnp.logical_not(end))
        def _():
            scatter.line(1)

        scatter.core(2)

        @pl.when(end)
        def _():
            scatter.line(2)

        scatter.core(3)
        small_direct(lambda copy: copy.start())

        @pl.when(jnp.logical_not(end))
        def _():
            scatter.line(2)

        for p in range(len(gather.pieces)):
            gather.finish(p)
        for m in range(MICRO):
            for kind in range(3):
                operand(kind, m).wait_send()
            for zz in range(links.zs):
                operand(3, m, zz).wait_send()
        small_across().wait_send()
        results = [
            pltpu.make_async_copy(src, dst, r.fetch.at[at])
            for at, (src, dst) in enumerate(
                ((r.v_gsmall, r.gsmall_shard), (r.v_gout, r.gout_shard), (r.v_gin, r.gin_shard))
            )
        ]
        small_direct(lambda copy: copy.wait_recv())
        total_small = scatter.mine(3, links.z)[...].astype(f32)
        for step in range(1, links.zs):
            total_small = total_small + part(r.ss, step, r3)[...].astype(f32)
        r.v_gsmall[...] = total_small
        results[0].start()
        scatter.own(0)
        results[1].start()
        scatter.finish(0)
        small_direct(lambda copy: copy.wait_send())
        scatter.copy(3, CORE).wait_send()
        scatter.own(1)
        scatter.finish(1)
        scatter.own(2)
        results[2].start()
        scatter.finish(2)
        for result in results:
            result.wait()
    else:
        products_out()
        products_in(None)
        products_head()

    for m in range(MICRO):
        for at in range(2):
            keep(m, at).wait()

    for m in range(MICRO):

        @pl.when(sec == 0)
        def _():
            boundary(RIGHT, m).wait_send()

        @pl.when(sec == 1)
        def _():
            boundary(LEFT, m).wait_send()


def call(n, inside, arrays):
    r1, r2, zs = 2 * DI // n, DI // n, n // 4
    rows2 = MICRO * T
    outs = dict(
        section_out=((MICRO, T, D), bf16),
        section_grad=((MICRO, T, D), f32),
    )
    scratch = dict(
        reset=((MICRO, T, 128), f32),
        u=((rows2, D), bf16),
        go=((rows2, D), bf16),
        back=((rows2, D), bf16),
        normed=((rows2, D), bf16),
        x=((rows2, DI), f32),
        dact=((rows2, DI), f32),
        sz=((rows2, DI), f32),
        dz=((rows2, DI), f32),
        rate=((rows2, DI), f32),
        drate=((rows2, DI), f32),
        act=((rows2, DI), bf16),
        gated=((rows2, DI), bf16),
        gpre=((rows2, DI), bf16),
        gm=((rows2, 2 * DI), bf16),
        proj=((rows2, 128), f32),
        rin=((rows2, 128), bf16),
        gp=((rows2, 128), bf16),
        h=((MICRO, (T + 1) * NS, DI), bf16),
        adj=((T * NS, CS), bf16),
        ea=((T * NS // 2, CS), bf16),
        dec=((rows2, DI), f32),
        gs=((T, DI), f32),
        gr=((T, DI), f32),
        gb=((T, NS * TB), f32),
        gc=((T, NS * TB), bf16),
        drive=((rows2, DI), bf16),
        cols=((T * NS, 128), f32),
        diag=((T, NS * TB), bf16),
        rows=((32, DI), f32),
        gain=((1, D), f32),
    )
    scratch |= dict(v_out=((rows2, D), bf16), v_grad=((rows2, D), f32), v_markers=((MICRO, T), jnp.int32))
    sems = dict(edge=(2, 2, MICRO), loads=(MICRO,), keeps=(2, MICRO), fetch=(12,))
    if inside:
        outs |= dict(
            gin_shard=((r1, D), f32),
            gout_shard=((r2, D), f32),
            gsmall_shard=((r2 + 32, 128), f32),
        )
        scratch |= dict(
            v_norm_gain=((1, D // n), f32),
            v_in_proj=((r1, D), f32),
            v_conv_weight=((1, KC, r2), f32),
            v_conv_bias=((1, r2), f32),
            v_x_proj=((RK + 2 * NS, r2), f32),
            v_dt_proj=((1, RK, r2), f32),
            v_dt_bias=((1, r2), f32),
            v_a_log=((NS, r2), f32),
            v_d_skip=((1, r2), f32),
            v_out_proj=((1, r2, D), f32),
            v_gin=((r1, D), f32),
            v_gout=((r2, D), f32),
            v_gsmall=((r2 + 32, 128), f32),
            sm=((32, DI), f32),
            gg=((1, D), f32),
            win=((2 * DI, D), bf16),
            wout=((DI, D), bf16),
            small=((DI, 128), bf16),
            tails=((32 * n, 128), bf16),
            gwi=((DI, D), bf16),
            gwo=((DI // 2, D), bf16),
            gws=((n * (r2 + 32), 128), bf16),
            head=((DI, 128), f32),
            xg=((rows2, DI), bf16),
            xn=((rows2, D), bf16),
            xo=((rows2, D), bf16),
            xm=((rows2, DI), bf16),
            ci=((zs * r1, D), bf16),
            co=((zs * r2, D), bf16),
            cs=((zs * (r2 + 32), 128), bf16),
            xs=((2 * zs * (r2 + 32), 128), bf16),
            ss=((zs * (r2 + 32), 128), bf16),
            ui=((zs * r1, D), bf16),
            uo=((zs * r2, D), bf16),
            di=((zs * r1, D), bf16),
            do=((zs * r2, D), bf16),
        )
        sems |= dict(
            ag_line=(5, 4, zs),
            ag_core=(5, 2 * zs),
            ag_recv=(5, n),
            rs_core=(4, 2),
            rs_line=(3, 8, zs),
            xs_sems=(8, max(MICRO, zs), 2),
        )
    else:
        outs |= dict(
            gwi=((2 * DI, D), f32),
            gwo=((DI, D), f32),
            gws=((DI, 128), f32),
            gg=((1, D), f32),
            sm=((32, DI), f32),
        )
        scratch |= dict(
            win=((2 * DI, D), bf16),
            wout=((DI, D), bf16),
            small=((DI, 128), bf16),
            v_raw_rows=((32, DI), f32),
        )
    names = list(arrays) + list(outs) + list(scratch) + list(sems)
    whole = pl.BlockSpec(memory_space=pltpu.VMEM)
    far = pl.BlockSpec(memory_space=pl.ANY)
    results = pl.pallas_call(
        functools.partial(block, names, inside, n),
        out_shape=[jax.ShapeDtypeStruct(*spec) for spec in outs.values()],
        in_specs=[far] * len(arrays),
        out_specs=[far] * len(outs) if inside else [far] * 2 + [whole] * (len(outs) - 2),
        scratch_shapes=[pltpu.VMEM(*spec) for spec in scratch.values()]
        + [pltpu.SemaphoreType.DMA(shape) for shape in sems.values()],
        compiler_params=pltpu.CompilerParams(
            collective_id=0, has_side_effects=True, vmem_limit_bytes=63 * 2**20
        ),
        name="two_layer_block",
    )(*arrays.values())
    return types.SimpleNamespace(**dict(zip(outs, results)))


def unpack(*refs):
    far_in, far_out, near_in, near_out, sems = refs[:5], refs[5:17], refs[17:22], refs[22:31], refs[31]
    gsmall = near_in[4]
    gain_o, in_o, cw_o, cb_o, x_o, dt_o, db_o, a_o, ds_o = near_out
    loads = [pltpu.make_async_copy(far, near, sems.at[0, at]) for at, (far, near) in enumerate(zip(far_in, near_in))]
    for at in (4, 1, 0, 2, 3):
        loads[at].start()
    stores = []

    def store(src, at):
        stores.append(pltpu.make_async_copy(src, far_out[at], sems.at[1, at]))
        stores[-1].start()

    loads[4].wait()
    r2, gw = cb_o.shape[1], gain_o.shape[1]
    tail = gsmall[pl.ds(r2, 32), :]
    small = gsmall[pl.ds(0, r2), :].T
    gain_o[...] = tail[23:24, 0:gw]
    cw_o[0] = tail[NS : NS + KC, 0:r2]
    cb_o[...] = tail[20:21, 0:r2]
    db_o[...] = tail[21:22, 0:r2]
    ds_o[...] = tail[22:23, 0:r2]
    a_o[...] = tail[0:NS, 0:r2]
    x_o[...] = small[0 : RK + 2 * NS, :]
    dt_o[0] = small[RK + 2 * NS : 128, :]
    for src, at in ((gain_o, 2), (cw_o, 4), (cb_o, 5), (x_o, 6), (dt_o, 7), (db_o, 8), (a_o, 9), (ds_o, 10)):
        store(src, at)
    for src, at in ((1, 1), (0, 0), (2, 3), (3, 11)):
        loads[src].wait()
        far = far_out[at] if at == 3 else far_out[at].at[0]
        stores.append(pltpu.make_async_copy(near_in[src], far, sems.at[1, at]))
        stores[-1].start()
    for copy in stores:
        copy.wait()


def on_device(inputs, cotangent, markers, *weights):
    (
        norm_gain,
        in_proj,
        conv_weight,
        conv_bias,
        x_proj,
        dt_proj,
        dt_bias,
        a_log,
        d_skip,
        out_proj,
    ) = weights
    n = lax.axis_size(DP)
    inside = n == 16
    arrays = dict(inputs=inputs, cotangent=cotangent, markers=markers)
    if inside:
        arrays |= dict(
            norm_gain=norm_gain,
            in_proj=in_proj[0].T,
            conv_weight=conv_weight,
            conv_bias=conv_bias,
            x_proj=x_proj[0].T,
            dt_proj=dt_proj,
            dt_bias=dt_bias,
            a_log=a_log[0].T,
            d_skip=d_skip,
            out_proj=out_proj,
        )
        res = call(n, inside, arrays)
        far = pl.BlockSpec(memory_space=pl.ANY)
        turned = (in_proj, x_proj, a_log)
        shapes = [((1,) + res.section_out.shape, bf16), ((1,) + res.section_grad.shape, f32)]
        shapes += [(w.shape[:0:-1] if any(w is t for t in turned) else w.shape, f32) for w in weights]
        parts = (res.section_out, res.section_grad, res.gin_shard, res.gout_shard, res.gsmall_shard)
        done = pl.pallas_call(
            unpack,
            out_shape=[jax.ShapeDtypeStruct(*spec) for spec in shapes],
            in_specs=[far] * 5,
            out_specs=[far] * 12,
            scratch_shapes=[pltpu.VMEM(part.shape, part.dtype) for part in parts]
            + [pltpu.VMEM(*spec) for spec in shapes[2:11]]
            + [pltpu.SemaphoreType.DMA((2, 12))],
            name="unpack",
        )(*parts)
        grads = (g.T[None] if any(w is t for t in turned) else g for w, g in zip(weights, done[2:]))
        return (*done[:2], *grads)

    def gathered(value, axis):
        return lax.all_gather(value.astype(bf16), DP, axis=axis, tiled=True)

    r2 = DI // n
    raw = jnp.concatenate(
        [a_log[0].T, conv_weight[0], conv_bias, dt_bias, d_skip, jnp.zeros((9, r2), f32)], axis=0
    )
    arrays |= dict(
        all_win=gathered(in_proj[0].T, 0),
        all_wout=gathered(out_proj[0], 0),
        all_small=gathered(jnp.concatenate([x_proj[0], dt_proj[0].T], axis=1), 0),
        raw_rows=gathered(raw, 1).astype(f32),
        all_gain=gathered(norm_gain, 1).astype(f32),
    )
    res = call(n, inside, arrays)

    def scattered(value, axis):
        return lax.psum_scatter(value, DP, scatter_dimension=axis, tiled=True)

    gin, gout, gsmall = scattered(res.gwi, 0), scattered(res.gwo, 0), scattered(res.gws, 0)
    rows = scattered(res.sm, 1)
    return (
        res.section_out[None],
        res.section_grad[None],
        scattered(res.gg, 1),
        gin.T[None],
        rows[NS : NS + KC][None],
        rows[20:21],
        gsmall[:, 0 : RK + 2 * NS][None],
        gsmall[:, RK + 2 * NS : 128].T[None],
        rows[21:22],
        rows[0:NS].T[None],
        rows[22:23],
        gout[None],
    )


def solution(mesh):
    tokens = P(None, DP, None)
    columns = P(SECTION, None, DP)
    channels = P(SECTION, DP)
    rows = P(SECTION, DP, None)
    kept = P(SECTION, None, DP, None)
    weights = (
        channels,
        columns,
        columns,
        channels,
        rows,
        columns,
        channels,
        rows,
        channels,
        rows,
    )
    return jax.shard_map(
        on_device,
        mesh=mesh,
        in_specs=(tokens, tokens, P(None, DP)) + weights,
        out_specs=(kept, kept) + weights,
        check_vma=False,
    )
```

```python
import functools
import types

import jax
import jax.numpy as jnp
from jax import lax
from jax.experimental import pallas as pl
from jax.experimental.pallas import tpu as pltpu
from jax.sharding import PartitionSpec as P

T = 128
D = 768
DI = 1536
NS = 16
KC = 4
RK = 48
MICRO = 2
C = 512
CS = 768
TB = 16
NB = T // TB
EPS = 1e-5
LOG2E = 1.4426950408889634
LN2 = 0.6931471805599453
BIG = 1e30
DP, SECTION = "dp", "section"
UP, DOWN, ACROSS, CORE = range(4)
BELOW, ABOVE = range(2)
START, FINISH = range(2)
RIGHT, LEFT = range(2)
f32 = jnp.float32
bf16 = jnp.bfloat16


def nn(a, b):
    return lax.dot_general(a, b, (((1,), (0,)), ((), ())), preferred_element_type=f32)


def nt(a, b):
    return lax.dot_general(a, b, (((1,), (1,)), ((), ())), preferred_element_type=f32)


def tn(a, b):
    return lax.dot_general(a, b, (((0,), (0,)), ((), ())), preferred_element_type=f32)


def iota(shape, axis):
    return lax.broadcasted_iota(jnp.int32, shape, axis)


def sigmoid(v):
    return 0.5 * jnp.tanh(0.5 * v) + 0.5


def wide(v):
    return jnp.concatenate([v] * (CS // 128), axis=1)


def keeps(reset):
    keep = [None]
    cur = jnp.ones_like(reset)
    for k in range(1, KC):
        cur = cur * (1.0 - (reset if k == 1 else pltpu.roll(reset, k - 1, 0)))
        keep.append(cur)
    return keep


def block_diagonal(cols):
    tile = (iota((NS, NS * TB), 1) % NS == iota((NS, NS * TB), 0)).astype(bf16)
    rep = nn(cols.astype(bf16), tile)
    own = (iota((T, NS * TB), 1) // NS) == (iota((T, NS * TB), 0) % TB)
    return jnp.where(own, rep, 0.0).astype(bf16)


def lane_columns(dst, val):
    for t in range(T):
        dst[pl.ds(t * NS, NS), :] = jnp.broadcast_to(val[:, t : t + 1], (NS, 128))


def f_x(reset, normed, win, rows, x_ref, act, dact):
    keep = keeps(reset)
    for c in range(DI // C):
        s = pl.ds(c * C, C)
        x = nt(normed[...], win[s, :])
        x_ref[:, s] = x
        v = rows[20:21, s] + rows[16:17, s] * x
        for k in range(1, KC):
            v = v + rows[16 + k : 17 + k, s] * (pltpu.roll(x, k, 0) * keep[k])
        sg = sigmoid(v)
        act[:, s] = (v * sg).astype(bf16)
        dact[:, s] = sg * (1.0 + v * (1.0 - sg))


def f_rate(reset, act, small, rows, proj, rin, rate_ref, drate, dec, drive, drive_low, cols, diag):
    p = nn(act[...], small[:, 0:128])
    proj[...] = p
    lane_columns(cols, p.T[RK : RK + NS, :])
    diag[...] = block_diagonal(p[:, RK + NS : RK + 2 * NS])
    rin[...] = pltpu.roll(jnp.where(iota((T, 128), 1) < RK, p, 0.0), RK + 2 * NS, 1).astype(bf16)
    for c in range(DI // C):
        s = pl.ds(c * C, C)
        pre = nt(rin[...], small[s, 0:128]) + rows[21:22, s]
        e = jnp.exp(-jnp.abs(pre))
        rate = jnp.maximum(pre, 0.0) + jnp.log1p(e)
        rate_ref[:, s] = rate
        drate[:, s] = jnp.where(pre >= 0.0, 1.0, e) / (1.0 + e)
        dec[:, s] = jnp.where(reset > 0.0, BIG, rate)
        both = rate * act[:, s].astype(f32)
        drive[:, s] = both
        drive_low[:, s] = both.astype(bf16)


def f_scan(act, rows, dec, drive, cols, diag, h_ref, ssm):
    h_ref[0:NS, :] = jnp.zeros((NS, DI), bf16)
    for c in range(DI // CS):
        s = pl.ds(c * CS, CS)

        def block(i, h):
            t0 = pl.multiple_of(i * TB, TB)
            a2 = rows[0:NS, s]
            d = dec[pl.ds(t0, TB), s]
            v = drive[pl.ds(t0, TB), s]
            for j in range(TB):
                b = wide(cols[pl.ds(t0 * NS + j * NS, NS), :])
                h = jnp.exp2(d[j : j + 1, :] * a2) * h + v[j : j + 1, :] * b
                h_ref[pl.ds(t0 * NS + (j + 1) * NS, NS), s] = h.astype(bf16)
            return h

        lax.fori_loop(0, NB, block, jnp.zeros((NS, CS), f32))

    def sums(i, carry):
        for q in range(8):
            t0 = pl.multiple_of(i * (8 * TB) + q * TB, TB)
            tt = pl.ds(t0, TB)
            y = nn(diag[tt, :], h_ref[pl.ds(t0 * NS + NS, TB * NS), :])
            ssm[tt, :] = y + rows[22:23, :] * act[tt, :].astype(f32)
        return carry

    lax.fori_loop(0, NB // 8, sums, 0)


def f_out(u, normed, win, wout, ssm, sz_ref, dz_ref, gated, out):
    acc = u[...].astype(f32)
    for c in range(DI // C):
        s = pl.ds(c * C, C)
        z = nt(normed[...], win[pl.ds(DI + c * C, C), :])
        sg = sigmoid(z)
        sz = z * sg
        sz_ref[:, s] = sz
        dz_ref[:, s] = ssm[:, s] * (sg * (1.0 + z * (1.0 - sg)))
        g = (ssm[:, s] * sz).astype(bf16)
        gated[:, s] = g
        acc = acc + nn(g, wout[s, :])
    out[...] = acc.astype(bf16)


def total(old, first, value):
    return jnp.where(first, value, old + value)


def b_gate(first, go_ref, wout, sz, dz, act, gs_ref, gm, sm):
    go = go_ref[...]
    for c in range(DI // C):
        s = pl.ds(c * C, C)
        gg = nt(go, wout[s, :])
        gs = gg * sz[:, s]
        gs_ref[:, s] = gs
        gm[:, pl.ds(DI + c * C, C)] = (gg * dz[:, s]).astype(bf16)
        part = jnp.sum(gs * act[:, s].astype(f32), axis=0, keepdims=True)
        sm[22:23, s] = total(sm[22:23, s], first, part)


def b_prep(proj, cols, diag):
    p = proj[...]
    lane_columns(cols, p.T[RK + NS : RK + 2 * NS, :])
    diag[...] = block_diagonal(p[:, RK : RK + NS])


def b_scan(between, first, gs, rows, dec, cols, diag, drive, h_ref, adj_ref, ea_ref, gd, gr, gb, gc, sm):
    ones = (iota((TB, TB * NS), 1) // NS) == iota((TB, TB * NS), 0)
    od = (iota((TB, TB * NS // 2), 1) // (NS // 2) == iota((TB, TB * NS // 2), 0)).astype(bf16)

    def state_sums(i, carry):
        for q in range(8):
            t0 = pl.multiple_of(i * (8 * TB) + q * TB, TB)
            tt = pl.ds(t0, TB)
            full = nt(gs[tt, :].astype(bf16), h_ref[pl.ds(t0 * NS + NS, TB * NS), :])
            gc[tt, :] = jnp.where(ones, full, 0.0).astype(bf16)
        return carry

    lax.fori_loop(0, NB // 8, state_sums, 0)
    for c in range(DI // CS):
        s = pl.ds(c * CS, CS)

        def block(i, state):
            carry, acc = state
            t0 = pl.multiple_of((NB - 1 - i) * TB, TB)
            a2 = rows[0:NS, s]
            d = dec[pl.ds(t0, TB), s]
            g = gs[pl.ds(t0, TB), s]
            later = None
            for j in reversed(range(TB)):
                row = pl.ds(t0 * NS + j * NS, NS)
                adj = g[j : j + 1, :] * wide(cols[row, :]) + carry
                adj_ref[row, :] = adj.astype(bf16)
                dj = d[j : j + 1, :]
                carry = jnp.exp2(dj * a2) * adj
                expo = carry * h_ref[row, s].astype(f32)
                weighted = expo * a2
                weighted = weighted[0 : NS // 2] + weighted[NS // 2 :]
                if j % 2:
                    later = weighted
                else:
                    pair = pl.ds(pl.multiple_of(t0 * (NS // 2), NS) + j * (NS // 2), NS)
                    ea_ref[pair, :] = jnp.concatenate([weighted, later], axis=0).astype(bf16)
                acc = acc + expo * dj
            return carry, acc

        zero = jnp.zeros((NS, CS), f32)
        _, acc = lax.fori_loop(0, NB, block, (zero, zero))
        sm[0:NS, s] = total(sm[0:NS, s], first, acc * rows[0:NS, s] * LN2)

        def adjoint_sums(i, carry):
            for q in range(8):
                t0 = pl.multiple_of(i * (8 * TB) + q * TB, TB)
                tt = pl.ds(t0, TB)
                row = pl.ds(t0 * NS, TB * NS)
                gd[tt, s] = nn(diag[tt, :], adj_ref[row, :])
            for q in range(8):
                t0 = pl.multiple_of(i * (8 * TB) + q * TB, TB)
                tt = pl.ds(t0, TB)
                ea = ea_ref[pl.ds(pl.multiple_of(t0 * (NS // 2), NS), TB * NS // 2), :]
                gr[tt, s] = nn(od, ea) * LN2
            for q in range(8):
                t0 = pl.multiple_of(i * (8 * TB) + q * TB, TB)
                tt = pl.ds(t0, TB)
                row = pl.ds(t0 * NS, TB * NS)
                full = nt(drive[tt, s], adj_ref[row, :])
                gb[tt, :] = full if c == 0 else gb[tt, :] + full
            return carry

        lax.fori_loop(0, NB // 8, adjoint_sums, 0)
        if c == 0 and between is not None:
            between()


def b_pre(first, act, drate, small, gd, gr, gb, gc, gpre, gp, sm):
    acc = jnp.zeros((T, 128), f32)
    for c in range(DI // C):
        s = pl.ds(c * C, C)
        g = ((gr[:, s] + gd[:, s] * act[:, s].astype(f32)) * drate[:, s]).astype(bf16)
        gpre[:, s] = g
        part = jnp.sum(g.astype(f32), axis=0, keepdims=True)
        sm[21:22, s] = total(sm[21:22, s], first, part)
        acc = acc + nn(g, small[s, 0:128])
    k = iota((TB * NS, 128), 0) % NS
    lane = iota((TB * NS, 128), 1)
    own = (iota((T, NS * TB), 1) // NS) == (iota((T, NS * TB), 0) % TB)
    gb_own = jnp.where(own, gb[...], 0.0).astype(bf16)
    bc = nn(gb_own, (lane == RK + k).astype(bf16)) + nn(gc[...], (lane == RK + NS + k).astype(bf16))
    gp[...] = jnp.where(iota((T, 128), 1) < RK, pltpu.roll(acc, RK, 1), bc).astype(bf16)


def b_conv(first, reset, rows, small, x_ref, dact, gs, gd, rate, gp, gm, sm):
    keep = keeps(reset)
    for c in range(DI // C):
        s = pl.ds(c * C, C)
        ga = gs[:, s] * rows[22:23, s] + gd[:, s] * rate[:, s] + nt(gp[...], small[s, 0:128])
        gc = ga * dact[:, s]
        x = x_ref[:, s]
        part = jnp.sum(gc, axis=0, keepdims=True)
        sm[20:21, s] = total(sm[20:21, s], first, part)
        gx = jnp.zeros((T, C), f32)
        for k in range(KC):
            ahead = pltpu.roll(gc * keep[k], T - k, 0) if k else gc
            part = jnp.sum(ahead * x, axis=0, keepdims=True)
            sm[16 + k : 17 + k, s] = total(sm[16 + k : 17 + k, s], first, part)
            gx = gx + ahead * rows[16 + k : 17 + k, s]
        gm[:, s] = gx.astype(bf16)


def b_in(first, u_ref, go_ref, gain, win, gm, sg, gg):
    gn = jnp.zeros((T, D), f32)
    for c in range(2 * DI // C):
        s = pl.ds(c * C, C)
        gn = gn + nn(gm[:, s], win[s, :])
    u = u_ref[...].astype(f32)
    inv = lax.rsqrt(jnp.mean(u * u, axis=-1, keepdims=True) + EPS)
    g = gn * gain[...]
    gg[...] = total(gg[...], first, jnp.sum(gn * u * inv, axis=0, keepdims=True))
    mean = jnp.mean(g * u, axis=-1, keepdims=True)
    sg[...] = go_ref[...].astype(f32) + inv * g - u * (inv * inv * inv) * mean


class Links:
    def __init__(self, n):
        self.zs = n // 4
        i = lax.axis_index(DP)
        self.i = i
        self.c = i % 2
        self.x = (i // 2) % 2
        self.z = i // 4

    def owner(self, z, x, c):
        return 4 * z + 2 * x + c

    def dev(self, route):
        step = (4, -4, 2 - 4 * self.x, 1 - 2 * self.c)[route]
        return dict(dp=self.i + step)

    def greet(self):
        sem = pltpu.get_barrier_semaphore()

        def tell(device):
            pl.semaphore_signal(sem, inc=1, device_id=device, device_id_type=pl.DeviceIdType.MESH)

        tell(self.dev(ACROSS))
        tell(self.dev(CORE))
        tell(dict(section=1 - lax.axis_index(SECTION)))

        @pl.when(self.z < self.zs - 1)
        def _():
            tell(self.dev(UP))

        @pl.when(self.z > 0)
        def _():
            tell(self.dev(DOWN))

    def meet(self):
        ends = jnp.where(self.z < self.zs - 1, 1, 0) + jnp.where(self.z > 0, 1, 0)
        pl.semaphore_wait(pltpu.get_barrier_semaphore(), 3 + ends)


def part(ref, index, count, first=0, rows=None):
    return ref.at[pl.ds(pl.multiple_of(index * count + first, 16), rows or count), :]


def remote(src, dst, send, recv, device):
    return pltpu.make_async_remote_copy(
        src_ref=src,
        dst_ref=dst,
        send_sem=send,
        recv_sem=recv,
        device_id=device,
        device_id_type=pl.DeviceIdType.MESH,
    )


class Gather:
    def __init__(self, links, pieces, balanced, line_send, core_send, recv):
        self.k, self.pieces, self.balanced = links, pieces, balanced
        self.line_send, self.core_send, self.recv = line_send, core_send, recv

    def copy(self, p, z, x, c, route, slot=None):
        whole, count = self.pieces[p][:2]
        ref = part(whole, self.k.owner(z, x, c), count)
        if route == CORE:
            send = self.core_send.at[p, 2 * z + x]
        else:
            send = self.line_send.at[p, route if slot is None else slot, z]
        return remote(ref, ref, send, self.recv.at[p, self.k.owner(z, x, c)], self.k.dev(route))

    def each(self, p, side, r, act):
        k = self.k
        lo, hi = self.pieces[p][2:]
        z = k.z - r if side == BELOW else k.z + r

        @pl.when((z >= lo) & (z < hi))
        def _():
            act(z)

    def line(self, p, r):
        def pass_on(z, side):
            k = self.k
            self.copy(p, z, k.x, k.c, ACROSS).wait_recv()
            self.go(p, z, side, START)

        for side in (BELOW, ABOVE):
            self.each(p, side, r, functools.partial(pass_on, side=side))

    def go(self, p, z, side, do):
        k = self.k

        def one(route):
            copy = self.copy(p, z, k.x, k.c, route)
            copy.wait_send() if do == FINISH else copy.start()

        @pl.when(jnp.logical_not(self.by_line(p, z)))
        def _():
            one(ACROSS)

        if side != ABOVE:

            @pl.when(k.z < k.zs - 1)
            def _():
                one(UP)

        if side != BELOW:

            @pl.when(k.z > 0)
            def _():
                one(DOWN)

        one(CORE)

    def by_line(self, p, z):
        k = self.k
        last = k.zs - 1
        near = ((k.z == 1) & (z == 0)) | ((k.z == last - 1) & (z == last))
        if p not in self.balanced:
            return near
        return near | ((k.z == 0) & (z == last)) | ((k.z == last) & (z == 0))

    def relay(self, p, z, do):
        k = self.k
        last = k.zs - 1
        far = int(p in self.balanced)

        def one(route):
            copy = self.copy(p, z, 1 - k.x, k.c, route, 3)
            copy.wait_send() if do == FINISH else copy.start()

        @pl.when(((k.z == 0) & (z == 0)) | ((k.z == last - 1) & (z == 0) & (far == 1)))
        def _():
            one(UP)

        @pl.when(((k.z == last) & (z == last)) | ((k.z == 1) & (z == last) & (far == 1)))
        def _():
            one(DOWN)

    def start(self, p):
        self.each(p, BELOW, 0, lambda z: self.go(p, z, None, START))

    def across(self, p, r):
        def pass_on(z):
            copy = self.copy(p, z, 1 - self.k.x, self.k.c, CORE)
            copy.wait_recv()
            self.relay(p, z, START)
            copy.start()

        self.each(p, BELOW, r, pass_on)
        if r:
            self.each(p, ABOVE, r, pass_on)

    def arrived(self, p):
        for z in range(*self.pieces[p][2:]):
            for x in range(2):
                self.copy(p, z, x, 1 - self.k.c, CORE).wait_recv()

    def finish(self, p):
        k = self.k

        def crossed(z):
            self.copy(p, z, 1 - k.x, k.c, CORE).wait_send()
            self.relay(p, z, FINISH)

        for r in range(k.zs):
            for side in (BELOW, ABOVE) if r else (BELOW,):
                self.each(p, side, r, lambda z, side=side: self.go(p, z, side if r else None, FINISH))
                self.each(p, side, r, crossed)


def add_rows(dst, src):
    count = dst.shape[0]
    step = 48 if count % 48 == 0 else 16

    def add(i, carry):
        s = pl.ds(pl.multiple_of(i * step, 16), step)
        dst[s, :] = (dst[s, :].astype(f32) + src[s, :].astype(f32)).astype(dst.dtype)
        return carry

    lax.fori_loop(0, count // step, add, 0)


class Scatter:
    def __init__(self, links, pieces, subs, core_sems, line_sems):
        self.k, self.pieces, self.subs = links, pieces, subs
        self.core_sems, self.line_sems = core_sems, line_sems

    def rows(self, p, c, z, count=1):
        g, first, _, _, _, _, size, _, _ = self.pieces[p]
        return part(g, 1, first + (c * self.k.zs + z) * size, 0, count * size)

    def mine(self, p, z, sub=None):
        whole = self.rows(p, self.k.c, z)
        return whole if sub is None else self.half(p, whole, sub)

    def half(self, p, ref, sub):
        count = ref.shape[0] // self.subs[p]
        return ref.at[pl.ds(sub * count, count), :]

    def copy(self, p, route, z=None, sub=0):
        k = self.k
        _, _, core, below, above, _, size, lo, hi = self.pieces[p]
        if route == CORE:
            send, recv = self.core_sems.at[p, 0], self.core_sems.at[p, 1]
            src, dst = self.rows(p, 1 - k.c, lo, hi - lo), part(core, 1, lo * size, 0, (hi - lo) * size)
        else:
            at = 4 * sub + 2 * route
            send, recv = self.line_sems.at[p, at, z], self.line_sems.at[p, at + 1, z]
            src, dst = self.mine(p, z, sub), self.half(p, part((below, above)[route], z, size), sub)
        return remote(src, dst, send, recv, k.dev(route))

    def far_first(self, p):
        k = self.k
        lo, hi = self.pieces[p][7:]
        for i in range(hi - lo):
            table = [sorted(range(lo, hi), key=lambda o: (-abs(o - z), o))[i] for z in range(k.zs)]
            z = table[0]
            for at in range(1, k.zs):
                z = jnp.where(k.z == at, table[at], z)
            yield z

    def start(self, p):
        self.copy(p, CORE).start()

    def core(self, p):
        _, _, core, _, _, _, size, lo, hi = self.pieces[p]
        self.copy(p, CORE).wait_recv()
        add_rows(self.rows(p, self.k.c, lo, hi - lo), part(core, 1, lo * size, 0, (hi - lo) * size))

    def line(self, p):
        k = self.k
        _, _, _, below, above, _, size, _, _ = self.pieces[p]
        for z in self.far_first(p):

            def hop(route, inner, source):
                for sub in range(self.subs[p]):

                    @pl.when(inner)
                    def _():
                        self.copy(p, route, z, sub).wait_recv()
                        add_rows(self.mine(p, z, sub), self.half(p, part(source, z, size), sub))

                    self.copy(p, route, z, sub).start()

            @pl.when(z > k.z)
            def _():
                hop(UP, k.z > 0, below)

            @pl.when(z < k.z)
            def _():
                hop(DOWN, k.z < k.zs - 1, above)

    def own(self, p):
        k = self.k
        _, _, _, below, above, result, size, lo, hi = self.pieces[p]

        @pl.when((k.z >= lo) & (k.z < hi))
        def _():
            result[...] = self.mine(p, k.z)[...].astype(f32)
            for sub in range(self.subs[p]):

                def take(route, source):
                    self.copy(p, route, k.z, sub).wait_recv()
                    add_rows(self.half(p, result, sub), self.half(p, part(source, k.z, size), sub))

                @pl.when(k.z > 0)
                def _():
                    take(UP, below)

                @pl.when(k.z < k.zs - 1)
                def _():
                    take(DOWN, above)

    def finish(self, p):
        k = self.k
        self.copy(p, CORE).wait_send()
        for z in range(*self.pieces[p][7:]):
            for sub in range(self.subs[p]):

                @pl.when(z > k.z)
                def _():
                    self.copy(p, UP, z, sub).wait_send()

                @pl.when(z < k.z)
                def _():
                    self.copy(p, DOWN, z, sub).wait_send()


def weight_rows(tails, rows, gain, n):
    r2, gw = DI // n, D // n
    parts = [tails[i * 32 : i * 32 + 32, :].astype(f32) for i in range(n)]
    rows[...] = jnp.concatenate([p[:, 0:r2] for p in parts], axis=1)
    gain[...] = jnp.concatenate([p[23:24, 0:gw] for p in parts], axis=1)


def block(names, inside, n, *refs):
    r = types.SimpleNamespace(**dict(zip(names, refs)))
    sec = lax.axis_index(SECTION)
    links = Links(n)
    r1, r2, gw = 2 * DI // n, DI // n, D // n
    r3 = r2 + 32
    if inside:
        far_in = (r.markers, r.norm_gain, r.in_proj, r.conv_weight, r.conv_bias, r.x_proj)
        far_in += (r.dt_proj, r.dt_bias, r.a_log, r.d_skip, r.out_proj)
        near_in = (r.v_markers, r.v_norm_gain, r.v_in_proj, r.v_conv_weight, r.v_conv_bias, r.v_x_proj)
        near_in += (r.v_dt_proj, r.v_dt_bias, r.v_a_log, r.v_d_skip, r.v_out_proj)
    else:
        far_in = (r.markers, r.all_win, r.all_wout, r.all_small, r.raw_rows, r.all_gain)
        near_in = (r.v_markers, r.win, r.wout, r.small, r.v_raw_rows, r.gain)
    rows, small, gain, win, wout = r.rows, r.small, r.gain, r.win, r.wout

    def of(ref, m):
        return ref.at[pl.ds(pl.multiple_of(m * T, T), T), :]

    def load(m, at):
        src, dst = ((r.inputs, r.u), (r.cotangent, r.go))[at]
        return pltpu.make_async_copy(src.at[m], of(dst, m), r.loads.at[m])

    if inside:
        links.greet()
    fetches = [
        pltpu.make_async_copy(src, dst, r.fetch.at[at])
        for at, (src, dst) in enumerate(zip(far_in, near_in, strict=True))
    ]
    for fetch in fetches:
        fetch.start()
    for at in range(2):

        @pl.when(sec == at)
        def _():
            for m in range(MICRO):
                load(m, at).start()

    r.sm[...] = jnp.zeros_like(r.sm)
    for fetch in fetches:
        fetch.wait()
    starts = jnp.where((r.v_markers[...] > 0) | (iota((MICRO, T), 1) == 0), 1.0, 0.0)
    starts = jnp.concatenate([starts, jnp.zeros((8 - MICRO, T), f32)], axis=0).T
    for m in range(MICRO):
        r.reset[m] = jnp.broadcast_to(starts[:, m : m + 1], (T, 128))
    def keep(m, at):
        src, dst = ((r.v_out, r.section_out), (r.v_grad, r.section_grad))[at]
        return pltpu.make_async_copy(of(src, m), dst.at[m], r.keeps.at[at, m])

    def boundary(route, m):
        if route == RIGHT:
            src, dst, at = of(r.v_out, m), of(r.u, m), 0
        else:
            src, dst, at = of(r.back, m), of(r.go, m), 1
        return remote(src, dst, r.edge.at[at, 0, m], r.edge.at[at, 1, m], dict(section=1 - sec))

    if inside:
        tails = r.tails
        part(win, links.i, r1)[...] = r.v_in_proj[...].astype(bf16)
        part(wout, links.i, r2)[...] = r.v_out_proj[0].astype(bf16)
        head = jnp.concatenate([r.v_x_proj[...], r.v_dt_proj[0]], axis=0).T
        part(small, links.i, r2)[...] = head.astype(bf16)
        top = [r.v_a_log[...], r.v_conv_weight[0], r.v_conv_bias[...], r.v_dt_bias[...], r.v_d_skip[...]]
        top.append(jnp.concatenate([r.v_norm_gain[...], jnp.zeros((1, r2 - gw), f32)], axis=1))
        top = jnp.concatenate(top + [jnp.zeros((8, r2), f32)], axis=0)
        top = jnp.concatenate([top, jnp.zeros((32, 128 - r2), f32)], axis=1)
        part(tails, links.i, 32)[...] = top.astype(bf16)
        links.meet()
        half = links.zs // 2
        pieces = [
            (tails, 32, 0, links.zs),
            (small, r2, 0, links.zs),
            (win, r1, 0, half),
            (win, r1, half, links.zs),
            (wout, r2, 0, links.zs),
        ]
        gather = Gather(links, pieces, (4,), r.ag_line, r.ag_core, r.ag_recv)
        early, late = (0, 1, 2), (3, 4)

        def pass_on(ps, hops):
            for hop in hops:
                for p in ps:
                    if hop < links.zs:
                        gather.line(p, hop)
                for p in ps:
                    gather.across(p, hop - 1)

        for p in early:
            gather.start(p)
        for p in late:
            gather.start(p)
        for p in early:
            gather.line(p, 1)
        for p in late:
            gather.line(p, 1)
        for p in early:
            gather.across(p, 0)
        for p in early:
            gather.line(p, 2)
        for p in late:
            gather.across(p, 0)
        for p in early:
            gather.across(p, 1)
        for p in early:
            gather.line(p, 3)
        for p in late:
            gather.line(p, 2)
        for p in early:
            gather.across(p, 2)
        for p in late:
            gather.across(p, 1)
        for p in early:
            gather.across(p, 3)
        for p in late:
            gather.line(p, 3)
        for p in early:
            gather.arrived(p)

        def rest(hops):
            for hop in hops:
                for p in late:
                    gather.across(p, hop - 1)
            if links.zs in hops:
                for p in late:
                    gather.arrived(p)

        @pl.when(sec == 1)
        def _():
            rest((links.zs - 1, links.zs))

        weight_rows(tails, rows, gain, n)
        half_rows = 2 * links.zs
        pieces = [
            (r.gwo, 0, r.co, r.uo, r.do, r.v_gout, r2, 0, links.zs),
            (r.gwi, 0, r.ci, r.ui, r.di, r.v_gin, r1, half, links.zs),
            (r.gwi, 0, r.ci, r.ui, r.di, r.v_gin, r1, 0, half),
            (r.gws, links.x * half_rows * r3, r.cs, None, None, None, r3, 0, links.zs),
        ]
        scatter = Scatter(links, pieces, (1, 2, 2, 1), r.rs_core, r.rs_line)
        strip = 2 * r1

        def operand(kind, m, zz=0):
            src = of((r.gated, r.normed, r.go, r.gm)[kind], m)
            dst = of((r.xg, r.xn, r.xo, r.xm)[kind], m)
            if kind == 3:
                at = pl.multiple_of((2 * zz + 1 - links.x) * strip, 128)
                src, dst = src.at[:, pl.ds(at, strip)], dst.at[:, pl.ds(zz * strip, strip)]
            sems = r.xs_sems.at[kind + zz, m]
            return remote(src, dst, sems.at[0], sems.at[1], links.dev(ACROSS))

        def small_across():
            sems = r.xs_sems.at[7, 0]
            src = part(r.gws, 1 - links.x, half_rows * r3)
            return remote(src, r.xs, sems.at[0], sems.at[1], links.dev(ACROSS))

        def small_direct(act):
            for step in range(1, links.zs):
                to = (links.z + step) % links.zs
                sems = r.xs_sems.at[7, step]
                dst = part(r.ss, step, r3)
                act(remote(scatter.mine(3, to), dst, sems.at[0], sems.at[1], dict(dp=links.owner(to, links.x, links.c))))

    else:
        sem = pltpu.get_barrier_semaphore()
        pl.semaphore_signal(
            sem, inc=1, device_id=dict(section=1 - sec), device_id_type=pl.DeviceIdType.MESH
        )
        pl.semaphore_wait(sem, 1)
        rows[...] = r.v_raw_rows[...]
    for c in range(DI // C):
        s = pl.ds(c * C, C)
        rows[0:NS, s] = -jnp.exp(rows[0:NS, s]) * LOG2E

    def forward(k, carry):
        m = k - sec

        @pl.when((m >= 0) & (m < MICRO))
        def _():
            @pl.when(sec == 1)
            def _():
                boundary(RIGHT, m).wait_recv()

            @pl.when(sec == 0)
            def _():
                load(m, 0).wait()

            def gathering(hops):
                if inside:

                    @pl.when((sec == 0) & (m == 0))
                    def _():
                        rest(hops)

            u = of(r.u, m)
            reset = r.reset[m][:, 0:1]
            v = u[...].astype(f32)
            inv = lax.rsqrt(jnp.mean(v * v, axis=-1, keepdims=True) + EPS)
            normed, act, ssm = of(r.normed, m), of(r.act, m), r.gr
            normed[...] = (v * inv * gain[...]).astype(bf16)
            f_x(reset, normed, win, rows, of(r.x, m), act, of(r.dact, m))
            gathering((links.zs - 1,))
            f_rate(
                reset,
                act,
                small,
                rows,
                of(r.proj, m),
                of(r.rin, m),
                of(r.rate, m),
                of(r.drate, m),
                of(r.dec, m),
                r.gs,
                of(r.drive, m),
                r.cols,
                r.diag,
            )
            f_scan(act, rows, of(r.dec, m), r.gs, r.cols, r.diag, r.h.at[m], ssm)
            gathering((links.zs,))
            f_out(u, normed, win, wout, ssm, of(r.sz, m), of(r.dz, m), of(r.gated, m), of(r.v_out, m))

            @pl.when(sec == 0)
            def _():
                boundary(RIGHT, m).start()

            keep(m, 0).start()
            if inside:
                operand(0, m).start()
                operand(1, m).start()

        return carry

    lax.fori_loop(0, MICRO + 1, forward, 0)

    @pl.when(sec == 1)
    def _():
        for m in range(MICRO):
            load(m, 1).wait()

    def owners_rows(g, first, size, zz, value):
        for c in range(2):
            at = pl.ds(pl.multiple_of(first + (c * links.zs + zz) * size, 16), size)
            g[at, :] = value[c * size : (c + 1) * size].astype(g.dtype)

    def products_out():
        if inside:
            for kind in (0, 2):
                for m in range(MICRO):
                    operand(kind, m).wait_recv()
            def mine(ref, zz):
                at = zz * 4 * r2
                return jnp.where(links.x == 0, ref[:, at : at + 2 * r2], ref[:, at + 2 * r2 : at + 4 * r2])

            for zz in range(links.zs):
                value = tn(mine(r.gated, zz), r.go[...]) + tn(mine(r.xg, zz), r.xo[...])
                owners_rows(r.gwo, 0, r2, zz, value)
        else:
            for c in range(DI // C):
                s = pl.ds(c * C, C)
                r.gwo[s, :] = tn(r.gated[:, s], r.go[...])

    def products_in(zzs):
        if inside:
            for m in range(MICRO):
                if half in zzs:
                    operand(1, m).wait_recv()
                for zz in zzs:
                    operand(3, m, zz).wait_recv()
            for zz in zzs:
                mine = pl.ds(pl.multiple_of((2 * zz + links.x) * strip, 128), strip)
                full = tn(r.gm[:, mine], r.normed[...]) + tn(r.xm[:, pl.ds(zz * strip, strip)], r.xn[...])
                owners_rows(r.gwi, 0, r1, zz, full)
        else:
            for c in range(2 * DI // C):
                s = pl.ds(c * C, C)
                r.gwi[s, :] = tn(r.gm[:, s], r.normed[...])

    def products_head():
        for c in range(DI // C):
            s = pl.ds(c * C, C)
            value = tn(r.act[:, s], r.gp[...]) + tn(r.gpre[:, s], r.rin[...])
            if inside:
                r.head[s, :] = value
            else:
                r.gws[s, :] = value

    def products_small():
        sm, gg = r.sm[0:32, :], r.gg[...]
        for i in range(n):
            z, x, c = i // 4, (i // 2) % 2, i % 2
            to = ((x * 2 + c) * links.zs + z) * r3
            r.gws[pl.ds(to, r2), :] = r.head[pl.ds(i * r2, r2), :].astype(bf16)
            top = pltpu.roll(sm, -i * r2 % DI, 1)[:, 0:128]
            g = pltpu.roll(gg, -i * gw % D, 1)[:, 0:128]
            top = jnp.where(iota((32, 128), 0) == 23, jnp.broadcast_to(g, (32, 128)), top)
            r.gws[pl.ds(to + r2, 32), :] = top.astype(bf16)

    if inside:
        low, high = range(half), range(half, links.zs)
        end = (links.z == 0) | (links.z == links.zs - 1)

        def first_products():
            products_out()
            scatter.start(0)

        def second_products():
            scatter.core(0)
            products_in(high)
            scatter.start(1)

            @pl.when(end)
            def _():
                scatter.line(0)

        def fourth_step():
            products_small()
            small_across().start()
            scatter.core(1)

            @pl.when(end)
            def _():
                scatter.line(1)

    def backward(k, carry):
        m = k - (1 - sec)

        @pl.when((m >= 0) & (m < MICRO))
        def _():
            b_prep(of(r.proj, m), r.cols, r.diag)

            @pl.when(sec == 0)
            def _():
                boundary(LEFT, m).wait_recv()

            first = m == 0
            reset = r.reset[m][:, 0:1]
            go, gm, sm = of(r.go, m), of(r.gm, m), r.sm
            act, dec = of(r.act, m), of(r.dec, m)
            gs, gd, gr, gb, gc = r.gs, dec, r.gr, r.gb, r.gc

            def early(step):
                @pl.when((m == MICRO - 1) & (sec == 0))
                def _():
                    step()

            if inside:
                operand(2, m).start()
            b_gate(first, go, wout, of(r.sz, m), of(r.dz, m), act, gs, gm, sm)
            if inside:
                for zz in high:
                    operand(3, m, zz).start()
            b_scan(
                (lambda: early(first_products)) if inside else None,
                first, gs, rows, dec, r.cols, r.diag, of(r.drive, m), r.h.at[m], r.adj, r.ea, gd, gr, gb, gc, sm
            )
            if inside:
                early(second_products)
            b_pre(first, act, of(r.drate, m), small, gd, gr, gb, gc, of(r.gpre, m), of(r.gp, m), sm)
            b_conv(first, reset, rows, small, of(r.x, m), of(r.dact, m), gs, gd, of(r.rate, m), of(r.gp, m), gm, sm)
            if inside:
                for zz in low:
                    operand(3, m, zz).start()
                early(products_head)
            sg = of(r.v_grad, m)
            b_in(first, of(r.u, m), go, gain, win, gm, sg, r.gg)

            @pl.when(sec == 1)
            def _():
                of(r.back, m)[...] = sg[...].astype(bf16)
                boundary(LEFT, m).start()

            keep(m, 1).start()
            if inside:
                early(fourth_step)

        return carry

    lax.fori_loop(0, MICRO + 1, backward, 0)
    if inside:

        @pl.when(sec == 1)
        def _():
            first_products()
            second_products()
            products_head()
            fourth_step()

        @pl.when(jnp.logical_not(end))
        def _():
            scatter.line(0)

        products_in(low)
        scatter.start(2)
        small_across().wait_recv()
        add_rows(part(r.gws, links.x, half_rows * r3), r.xs)
        scatter.start(3)

        @pl.when(jnp.logical_not(end))
        def _():
            scatter.line(1)

        scatter.core(2)

        @pl.when(end)
        def _():
            scatter.line(2)

        scatter.core(3)
        small_direct(lambda copy: copy.start())

        @pl.when(jnp.logical_not(end))
        def _():
            scatter.line(2)

        for p in range(len(gather.pieces)):
            gather.finish(p)
        for m in range(MICRO):
            for kind in range(3):
                operand(kind, m).wait_send()
            for zz in range(links.zs):
                operand(3, m, zz).wait_send()
        small_across().wait_send()
        results = [
            pltpu.make_async_copy(src, dst, r.fetch.at[at])
            for at, (src, dst) in enumerate(
                ((r.v_gsmall, r.gsmall_shard), (r.v_gout, r.gout_shard), (r.v_gin, r.gin_shard))
            )
        ]
        small_direct(lambda copy: copy.wait_recv())
        total_small = scatter.mine(3, links.z)[...].astype(f32)
        for step in range(1, links.zs):
            total_small = total_small + part(r.ss, step, r3)[...].astype(f32)
        r.v_gsmall[...] = total_small
        results[0].start()
        scatter.own(0)
        results[1].start()
        scatter.finish(0)
        small_direct(lambda copy: copy.wait_send())
        scatter.copy(3, CORE).wait_send()
        scatter.own(1)
        scatter.finish(1)
        scatter.own(2)
        results[2].start()
        scatter.finish(2)
        for result in results:
            result.wait()
    else:
        products_out()
        products_in(None)
        products_head()

    for m in range(MICRO):
        for at in range(2):
            keep(m, at).wait()

    for m in range(MICRO):

        @pl.when(sec == 0)
        def _():
            boundary(RIGHT, m).wait_send()

        @pl.when(sec == 1)
        def _():
            boundary(LEFT, m).wait_send()


def call(n, inside, arrays):
    r1, r2, zs = 2 * DI // n, DI // n, n // 4
    rows2 = MICRO * T
    outs = dict(
        section_out=((MICRO, T, D), bf16),
        section_grad=((MICRO, T, D), f32),
    )
    scratch = dict(
        reset=((MICRO, T, 128), f32),
        u=((rows2, D), bf16),
        go=((rows2, D), bf16),
        back=((rows2, D), bf16),
        normed=((rows2, D), bf16),
        x=((rows2, DI), f32),
        dact=((rows2, DI), f32),
        sz=((rows2, DI), f32),
        dz=((rows2, DI), f32),
        rate=((rows2, DI), f32),
        drate=((rows2, DI), f32),
        act=((rows2, DI), bf16),
        gated=((rows2, DI), bf16),
        gpre=((rows2, DI), bf16),
        gm=((rows2, 2 * DI), bf16),
        proj=((rows2, 128), f32),
        rin=((rows2, 128), bf16),
        gp=((rows2, 128), bf16),
        h=((MICRO, (T + 1) * NS, DI), bf16),
        adj=((T * NS, CS), bf16),
        ea=((T * NS // 2, CS), bf16),
        dec=((rows2, DI), f32),
        gs=((T, DI), f32),
        gr=((T, DI), f32),
        gb=((T, NS * TB), f32),
        gc=((T, NS * TB), bf16),
        drive=((rows2, DI), bf16),
        cols=((T * NS, 128), f32),
        diag=((T, NS * TB), bf16),
        rows=((32, DI), f32),
        gain=((1, D), f32),
    )
    scratch |= dict(v_out=((rows2, D), bf16), v_grad=((rows2, D), f32), v_markers=((MICRO, T), jnp.int32))
    sems = dict(edge=(2, 2, MICRO), loads=(MICRO,), keeps=(2, MICRO), fetch=(12,))
    if inside:
        outs |= dict(
            gin_shard=((r1, D), f32),
            gout_shard=((r2, D), f32),
            gsmall_shard=((r2 + 32, 128), f32),
        )
        scratch |= dict(
            v_norm_gain=((1, D // n), f32),
            v_in_proj=((r1, D), f32),
            v_conv_weight=((1, KC, r2), f32),
            v_conv_bias=((1, r2), f32),
            v_x_proj=((RK + 2 * NS, r2), f32),
            v_dt_proj=((1, RK, r2), f32),
            v_dt_bias=((1, r2), f32),
            v_a_log=((NS, r2), f32),
            v_d_skip=((1, r2), f32),
            v_out_proj=((1, r2, D), f32),
            v_gin=((r1, D), f32),
            v_gout=((r2, D), f32),
            v_gsmall=((r2 + 32, 128), f32),
            sm=((32, DI), f32),
            gg=((1, D), f32),
            win=((2 * DI, D), bf16),
            wout=((DI, D), bf16),
            small=((DI, 128), bf16),
            tails=((32 * n, 128), bf16),
            gwi=((DI, D), bf16),
            gwo=((DI // 2, D), bf16),
            gws=((n * (r2 + 32), 128), bf16),
            head=((DI, 128), f32),
            xg=((rows2, DI), bf16),
            xn=((rows2, D), bf16),
            xo=((rows2, D), bf16),
            xm=((rows2, DI), bf16),
            ci=((zs * r1, D), bf16),
            co=((zs * r2, D), bf16),
            cs=((zs * (r2 + 32), 128), bf16),
            xs=((2 * zs * (r2 + 32), 128), bf16),
            ss=((zs * (r2 + 32), 128), bf16),
            ui=((zs * r1, D), bf16),
            uo=((zs * r2, D), bf16),
            di=((zs * r1, D), bf16),
            do=((zs * r2, D), bf16),
        )
        sems |= dict(
            ag_line=(5, 4, zs),
            ag_core=(5, 2 * zs),
            ag_recv=(5, n),
            rs_core=(4, 2),
            rs_line=(3, 8, zs),
            xs_sems=(8, max(MICRO, zs), 2),
        )
    else:
        outs |= dict(
            gwi=((2 * DI, D), f32),
            gwo=((DI, D), f32),
            gws=((DI, 128), f32),
            gg=((1, D), f32),
            sm=((32, DI), f32),
        )
        scratch |= dict(
            win=((2 * DI, D), bf16),
            wout=((DI, D), bf16),
            small=((DI, 128), bf16),
            v_raw_rows=((32, DI), f32),
        )
    names = list(arrays) + list(outs) + list(scratch) + list(sems)
    whole = pl.BlockSpec(memory_space=pltpu.VMEM)
    far = pl.BlockSpec(memory_space=pl.ANY)
    results = pl.pallas_call(
        functools.partial(block, names, inside, n),
        out_shape=[jax.ShapeDtypeStruct(*spec) for spec in outs.values()],
        in_specs=[far] * len(arrays),
        out_specs=[far] * len(outs) if inside else [far] * 2 + [whole] * (len(outs) - 2),
        scratch_shapes=[pltpu.VMEM(*spec) for spec in scratch.values()]
        + [pltpu.SemaphoreType.DMA(shape) for shape in sems.values()],
        compiler_params=pltpu.CompilerParams(
            collective_id=0, has_side_effects=True, vmem_limit_bytes=63 * 2**20
        ),
        name="two_layer_block",
    )(*arrays.values())
    return types.SimpleNamespace(**dict(zip(outs, results)))


def unpack(*refs):
    far_in, far_out, near_in, near_out, sems = refs[:5], refs[5:17], refs[17:22], refs[22:31], refs[31]
    gsmall = near_in[4]
    gain_o, in_o, cw_o, cb_o, x_o, dt_o, db_o, a_o, ds_o = near_out
    loads = [pltpu.make_async_copy(far, near, sems.at[0, at]) for at, (far, near) in enumerate(zip(far_in, near_in))]
    for at in (4, 1, 0, 2, 3):
        loads[at].start()
    stores = []

    def store(src, at):
        stores.append(pltpu.make_async_copy(src, far_out[at], sems.at[1, at]))
        stores[-1].start()

    loads[4].wait()
    r2, gw = cb_o.shape[1], gain_o.shape[1]
    tail = gsmall[pl.ds(r2, 32), :]
    small = gsmall[pl.ds(0, r2), :].T
    gain_o[...] = tail[23:24, 0:gw]
    cw_o[0] = tail[NS : NS + KC, 0:r2]
    cb_o[...] = tail[20:21, 0:r2]
    db_o[...] = tail[21:22, 0:r2]
    ds_o[...] = tail[22:23, 0:r2]
    a_o[...] = tail[0:NS, 0:r2]
    x_o[...] = small[0 : RK + 2 * NS, :]
    dt_o[0] = small[RK + 2 * NS : 128, :]
    for src, at in ((gain_o, 2), (cw_o, 4), (cb_o, 5), (x_o, 6), (dt_o, 7), (db_o, 8), (a_o, 9), (ds_o, 10)):
        store(src, at)
    for src, at in ((1, 1), (0, 0), (2, 3), (3, 11)):
        loads[src].wait()
        far = far_out[at] if at == 3 else far_out[at].at[0]
        stores.append(pltpu.make_async_copy(near_in[src], far, sems.at[1, at]))
        stores[-1].start()
    for copy in stores:
        copy.wait()


def on_device(inputs, cotangent, markers, *weights):
    (
        norm_gain,
        in_proj,
        conv_weight,
        conv_bias,
        x_proj,
        dt_proj,
        dt_bias,
        a_log,
        d_skip,
        out_proj,
    ) = weights
    n = lax.axis_size(DP)
    inside = n == 16
    arrays = dict(inputs=inputs, cotangent=cotangent, markers=markers)
    if inside:
        arrays |= dict(
            norm_gain=norm_gain,
            in_proj=in_proj[0].T,
            conv_weight=conv_weight,
            conv_bias=conv_bias,
            x_proj=x_proj[0].T,
            dt_proj=dt_proj,
            dt_bias=dt_bias,
            a_log=a_log[0].T,
            d_skip=d_skip,
            out_proj=out_proj,
        )
        res = call(n, inside, arrays)
        far = pl.BlockSpec(memory_space=pl.ANY)
        turned = (in_proj, x_proj, a_log)
        shapes = [((1,) + res.section_out.shape, bf16), ((1,) + res.section_grad.shape, f32)]
        shapes += [(w.shape[:0:-1] if any(w is t for t in turned) else w.shape, f32) for w in weights]
        parts = (res.section_out, res.section_grad, res.gin_shard, res.gout_shard, res.gsmall_shard)
        done = pl.pallas_call(
            unpack,
            out_shape=[jax.ShapeDtypeStruct(*spec) for spec in shapes],
            in_specs=[far] * 5,
            out_specs=[far] * 12,
            scratch_shapes=[pltpu.VMEM(part.shape, part.dtype) for part in parts]
            + [pltpu.VMEM(*spec) for spec in shapes[2:11]]
            + [pltpu.SemaphoreType.DMA((2, 12))],
            name="unpack",
        )(*parts)
        grads = (g.T[None] if any(w is t for t in turned) else g for w, g in zip(weights, done[2:]))
        return (*done[:2], *grads)

    def gathered(value, axis):
        return lax.all_gather(value.astype(bf16), DP, axis=axis, tiled=True)

    r2 = DI // n
    raw = jnp.concatenate(
        [a_log[0].T, conv_weight[0], conv_bias, dt_bias, d_skip, jnp.zeros((9, r2), f32)], axis=0
    )
    arrays |= dict(
        all_win=gathered(in_proj[0].T, 0),
        all_wout=gathered(out_proj[0], 0),
        all_small=gathered(jnp.concatenate([x_proj[0], dt_proj[0].T], axis=1), 0),
        raw_rows=gathered(raw, 1).astype(f32),
        all_gain=gathered(norm_gain, 1).astype(f32),
    )
    res = call(n, inside, arrays)

    def scattered(value, axis):
        return lax.psum_scatter(value, DP, scatter_dimension=axis, tiled=True)

    gin, gout, gsmall = scattered(res.gwi, 0), scattered(res.gwo, 0), scattered(res.gws, 0)
    rows = scattered(res.sm, 1)
    return (
        res.section_out[None],
        res.section_grad[None],
        scattered(res.gg, 1),
        gin.T[None],
        rows[NS : NS + KC][None],
        rows[20:21],
        gsmall[:, 0 : RK + 2 * NS][None],
        gsmall[:, RK + 2 * NS : 128].T[None],
        rows[21:22],
        rows[0:NS].T[None],
        rows[22:23],
        gout[None],
    )


def solution(mesh):
    tokens = P(None, DP, None)
    columns = P(SECTION, None, DP)
    channels = P(SECTION, DP)
    rows = P(SECTION, DP, None)
    kept = P(SECTION, None, DP, None)
    weights = (
        channels,
        columns,
        columns,
        channels,
        rows,
        columns,
        channels,
        rows,
        channels,
        rows,
    )
    return jax.shard_map(
        on_device,
        mesh=mesh,
        in_specs=(tokens, tokens, P(None, DP)) + weights,
        out_specs=(kept, kept) + weights,
        check_vma=False,
    )
```
